32 devices in a mesh: ctx: 8 (over y, x, core), fsdp: 4 (over z).
Axes of the slice: x: 2, y: 2, z: 4, core: 2. Of those that a mesh axis runs over, the one named last changes fastest.
Arguments:
- layer_in: bfloat16 [4, 8, 192, 768], P('fsdp', 'ctx'), may hold values from -6 to 6
- qkv_weight: bfloat16 [768, 2304], P('fsdp'), may hold values from -0.21875 to 0.21875
- query_bias: float32 [768], replicated, may hold values from -3 to 3
- value_bias: float32 [768], replicated, may hold values from -3 to 3
- out_weight: bfloat16 [768, 768], P('fsdp'), may hold values from -1.5 to 1.5
- out_bias: float32 [768], replicated, may hold values from -3 to 3
- fc_weight: bfloat16 [768, 3072], P('fsdp'), may hold values from -0.21875 to 0.21875
- fc_bias: float32 [3072], replicated, may hold values from -3 to 3
- proj_weight: bfloat16 [3072, 768], P('fsdp'), may hold values from -0.109375 to 0.109375
- proj_bias: float32 [768], replicated, may hold values from -3 to 3
- attn_norm_gain: float32 [768], replicated, may hold values from 0.5 to 1.5
- attn_norm_shift: float32 [768], replicated, may hold values from -2 to 2
- mlp_norm_gain: float32 [768], replicated, may hold values from 0.5 to 1.5
- mlp_norm_shift: float32 [768], replicated, may hold values from -2 to 2
- cotangent: bfloat16 [4, 8, 192, 768], P('fsdp', 'ctx'), may hold values from -6 to 6
- pair_table: int32 [8], replicated, may hold values from 0 to 7, each once
Outputs:
- layer_out: bfloat16 [4, 8, 192, 768], P('fsdp', 'ctx')
- grad_in: float32 [4, 8, 192, 768], P('fsdp', 'ctx')
- grad_qkv_weight: float32 [768, 2304], P(('ctx', 'fsdp'))
- grad_query_bias: float32 [768], P(('ctx', 'fsdp'))
- grad_value_bias: float32 [768], P(('ctx', 'fsdp'))
- grad_out_weight: float32 [768, 768], P(('ctx', 'fsdp'))
- grad_out_bias: float32 [768], P(('ctx', 'fsdp'))
- grad_fc_weight: float32 [768, 3072], P(('ctx', 'fsdp'))
- grad_fc_bias: float32 [3072], P(('ctx', 'fsdp'))
- grad_proj_weight: float32 [3072, 768], P(('ctx', 'fsdp'))
- grad_proj_bias: float32 [768], P(('ctx', 'fsdp'))
- grad_attn_norm_gain: float32 [768], P(('ctx', 'fsdp'))
- grad_attn_norm_shift: float32 [768], P(('ctx', 'fsdp'))
- grad_mlp_norm_gain: float32 [768], P(('ctx', 'fsdp'))
- grad_mlp_norm_shift: float32 [768], P(('ctx', 'fsdp'))
The draws below stay inside these ranges and needn't reach their ends.
Inputs may be any that keep to these rules, and one draw needn't show every extreme that they name: pair_table is a permutation: index c of ctx holds blocks pair_table[c] and 15 - pair_table[c] of every sequence.
All inputs are finite; a program needn't handle non-finite values.
Results may differ from the reference program's by a relative error of at most 0.035.
Values may be sent and summed in bfloat16 or wider, within the bound.
A program may use at most 256 MiB of HBM per device.

```python
import jax
import jax.numpy as jnp
from jax import lax

D = 768
H = 12
HEAD_DIM = 64
FF = 3072
BLK = 96
SEQ_ALL = 4
N_CTX = 8


def levels(key, dims, cuts, low, high):
    factor_of, own = 1.0, jax.random.fold_in(key, 6)
    for dim, parts in cuts:
        draws = jnp.exp(jax.random.uniform(jax.random.fold_in(own, dim), (parts,), jnp.float32, low / len(cuts), high / len(cuts)))
        factor_of = factor_of * jnp.repeat(draws, dims[dim] // parts).reshape([-1 if axis == dim else 1 for axis in range(len(dims))])
    return factor_of


def normal_values(own_key, dims, scale, most, shards=(), kind=jnp.bfloat16):
    drawn = scale * jax.random.normal(own_key, dims, jnp.float32)
    if shards:
        drawn = drawn * levels(own_key, dims, shards, -0.22, 0.18)
    return jnp.clip(drawn, -most, most).astype(kind)


def setup_inputs(seed: int = 0) -> dict:
    seeds = jax.random.split(jax.random.key(seed), 17)
    layer_in = normal_values(seeds[0], (SEQ_ALL, N_CTX, 2 * BLK, D), 1.0, 6.0, ((0, 4), (1, 8)))
    qkv_weight = normal_values(seeds[1], (D, 3 * D), D ** -0.5, 0.21875, ((0, 4),))
    query_bias = normal_values(seeds[2], (D,), 0.5, 3.0, (), jnp.float32)
    value_bias = normal_values(seeds[3], (D,), 0.5, 3.0, (), jnp.float32)
    out_weight = normal_values(seeds[4], (D, D), 16 ** -0.5, 1.5, ((0, 4),))
    out_bias = normal_values(seeds[5], (D,), 0.5, 3.0, (), jnp.float32)
    fc_weight = normal_values(seeds[6], (D, FF), D ** -0.5, 0.21875, ((0, 4),))
    fc_bias = normal_values(seeds[7], (FF,), 0.5, 3.0, (), jnp.float32)
    proj_weight = normal_values(seeds[8], (FF, D), FF ** -0.5, 0.109375, ((0, 4),))
    proj_bias = normal_values(seeds[9], (D,), 0.5, 3.0, (), jnp.float32)
    attn_norm_gain = jnp.clip(1.0 + 0.1 * jax.random.normal(seeds[10], (D,), jnp.float32), 0.5, 1.5)
    attn_norm_shift = normal_values(seeds[11], (D,), 0.3, 2.0, (), jnp.float32)
    mlp_norm_gain = jnp.clip(1.0 + 0.1 * jax.random.normal(seeds[12], (D,), jnp.float32), 0.5, 1.5)
    mlp_norm_shift = normal_values(seeds[13], (D,), 0.3, 2.0, (), jnp.float32)
    cotangent = normal_values(seeds[14], (SEQ_ALL, N_CTX, 2 * BLK, D), 1.0, 6.0, ((0, 4), (1, 8)))
    pair_table = jax.random.permutation(seeds[15], N_CTX).astype(jnp.int32)
    return dict(layer_in=layer_in, qkv_weight=qkv_weight, query_bias=query_bias, value_bias=value_bias, out_weight=out_weight, out_bias=out_bias, fc_weight=fc_weight, fc_bias=fc_bias, proj_weight=proj_weight, proj_bias=proj_bias, attn_norm_gain=attn_norm_gain, attn_norm_shift=attn_norm_shift, mlp_norm_gain=mlp_norm_gain, mlp_norm_shift=mlp_norm_shift, cotangent=cotangent, pair_table=pair_table)


@jax.custom_vjp
def low(v):
    return lax.optimization_barrier(v.astype(jnp.bfloat16)).astype(jnp.float32)

@jax.custom_vjp
def low_back(v):
    return v

def low_keep(v):
    return (low(v), None)

def low_pass(kept, grad):
    return (grad,)

def back_keep(v):
    return (v, None)

def back_low(kept, grad):
    return (low(grad),)
low.defvjp(low_keep, low_pass)
low_back.defvjp(back_keep, back_low)
epsilon = 1e-05
masked_score = -1e+30
highest = lax.Precision.HIGHEST

def layer_norm(values, gain, shift):
    centered = values - lax.optimization_barrier(jnp.mean(values, axis=-1, keepdims=True))
    variance = lax.optimization_barrier(jnp.mean(centered * centered, axis=-1, keepdims=True))
    return centered * lax.rsqrt(variance + epsilon) * gain + shift

def matmul(left, right):
    return jnp.dot(left, right, precision=highest)

def positions(pair_table):
    column = jnp.arange(2 * BLK, dtype=jnp.int32)[None, :]
    pair_index = pair_table.astype(jnp.int32)[:, None]
    lower = pair_index * BLK + column
    upper = (2 * N_CTX - 1 - pair_index) * BLK + column - BLK
    return jnp.where(column < BLK, lower, upper)

def attend(query, keys, values, key_pos):
    length = query.shape[0]
    block = 512 if length % 512 == 0 else length
    query_heads = query.reshape(length // block, block, H, HEAD_DIM)
    pos_blocks = key_pos.reshape(length // block, block)
    key_heads = keys.reshape(length, H, HEAD_DIM)
    value_heads = values.reshape(length, H, HEAD_DIM)

    def one_block(pieces):
        query_blk, query_pos = pieces
        scores = jnp.einsum('qhe,khe->hqk', query_blk, key_heads, precision=highest) * HEAD_DIM ** (-0.5)
        scores = low_back(scores)
        allowed = key_pos[None, None, :] <= query_pos[None, :, None]
        weights = low(jax.nn.softmax(jnp.where(allowed, scores, masked_score), axis=-1))
        return jnp.einsum('hqk,khe->qhe', weights, value_heads, precision=highest)
    mixed = lax.map(jax.checkpoint(one_block), (query_heads, pos_blocks))
    return mixed.reshape(length, H * HEAD_DIM)

def forward(seq_in, qkv_weight, query_bias, value_bias, out_weight, out_bias, fc_weight, fc_bias, proj_weight, proj_bias, attn_norm_gain, attn_norm_shift, mlp_norm_gain, mlp_norm_shift, key_pos):
    first_in = low(layer_norm(seq_in, attn_norm_gain, attn_norm_shift))
    projected = matmul(first_in, qkv_weight)
    query = low(low_back(projected[:, :D] + query_bias))
    keys = low(low_back(projected[:, D:2 * D]))
    values = low(low_back(projected[:, 2 * D:] + value_bias))
    attended = low(low_back(attend(query, keys, values, key_pos)))
    middle = seq_in + low_back(matmul(attended, out_weight)) + out_bias
    second_in = low(layer_norm(middle, mlp_norm_gain, mlp_norm_shift))
    pre_act = low_back(matmul(second_in, fc_weight) + fc_bias)
    activated = low(jax.nn.gelu(pre_act, approximate=True))
    return middle + matmul(activated, proj_weight) + proj_bias

def reference(layer_in, qkv_weight, query_bias, value_bias, out_weight, out_bias, fc_weight, fc_bias, proj_weight, proj_bias, attn_norm_gain, attn_norm_shift, mlp_norm_gain, mlp_norm_shift, cotangent, pair_table):
    key_pos = positions(pair_table).reshape(-1)
    params = tuple((item.astype(jnp.float32) for item in (qkv_weight, query_bias, value_bias, out_weight, out_bias, fc_weight, fc_bias, proj_weight, proj_bias, attn_norm_gain, attn_norm_shift, mlp_norm_gain, mlp_norm_shift)))
    seq_count = layer_in.shape[0]
    flat_in = layer_in.reshape(seq_count, -1, D).astype(jnp.float32)
    flat_cot = cotangent.reshape(seq_count, -1, D).astype(jnp.float32)

    def whole(inputs, weights):
        return forward(inputs, *weights, key_pos)

    def one_sequence(totals, pieces):
        seq_in, seq_cot = pieces
        output, pullback = jax.vjp(whole, seq_in, params)
        grad_seq, grad_params = pullback(seq_cot)
        totals = jax.tree.map(jnp.add, totals, grad_params)
        return (totals, (output, grad_seq))
    zeros = jax.tree.map(jnp.zeros_like, params)
    totals, (outputs, grads_seq) = lax.scan(one_sequence, zeros, (flat_in, flat_cot))
    layer_out = outputs.astype(jnp.bfloat16).reshape(layer_in.shape)
    grad_in = grads_seq.reshape(layer_in.shape)
    return (layer_out, grad_in, totals[0], totals[1], totals[2], totals[3], totals[4], totals[5], totals[6], totals[7], totals[8], totals[9], totals[10], totals[11], totals[12])
```

```python
from functools import partial

import jax
import jax.numpy as jnp
from jax import lax
from jax.experimental import pallas as pl
from jax.experimental.pallas import tpu as pltpu
from jax.sharding import PartitionSpec as P

H = 12
HEAD_DIM = 64
BLK = 96


epsilon = 1e-05
masked_score = -1e30


def normalize(values):
    centered = values - jnp.mean(values, axis=-1, keepdims=True)
    inverse = lax.rsqrt(jnp.mean(centered * centered, axis=-1, keepdims=True) + epsilon)
    return (centered * inverse, inverse)


def norm_back(grad_out, normed, inverse, gain):
    scaled = grad_out * gain
    grad_input = inverse * (
        scaled
        - jnp.mean(scaled, axis=-1, keepdims=True)
        - normed * jnp.mean(scaled * normed, axis=-1, keepdims=True)
    )
    return (grad_input, jnp.sum(grad_out * normed, axis=0), jnp.sum(grad_out, axis=0))


def block_positions(pair_table, device, ctx_count):
    pair_index = lax.dynamic_index_in_dim(pair_table, device, 0, keepdims=False)
    column = jnp.arange(2 * BLK, dtype=jnp.int32)
    lower = pair_index * BLK + column
    upper = (2 * ctx_count - 1 - pair_index) * BLK + column - BLK
    return jnp.where(column < BLK, lower, upper)


PAIR = 2 * HEAD_DIM
CHUNK = 8 * 2 * BLK
NT = (((1,), (1,)), ((), ()))


def chunk_of(total):
    return CHUNK if total % CHUNK == 0 else total


def head_only(block, head):
    lane = lax.broadcasted_iota(jnp.int32, block.shape, 1)
    return jnp.where((lane // HEAD_DIM) == head, block, jnp.zeros_like(block))


def head_pick(first, second):
    lane = lax.broadcasted_iota(jnp.int32, first.shape, 1)
    return jnp.where(lane < HEAD_DIM, first, second)


def dot_nt(left, right):
    return lax.dot_general(left, right, NT, preferred_element_type=jnp.float32)


def dot_nn(left, right):
    return jnp.dot(left, right, preferred_element_type=jnp.float32)


def forward_kernel(qpos_ref, kpos_ref, q_ref, k_ref, v_ref, out_ref, lse_ref, max_ref, sum_ref):
    step = pl.program_id(1)
    last = pl.num_programs(1) - 1

    @pl.when(step == 0)
    def _():
        max_ref[...] = jnp.full_like(max_ref, masked_score)
        sum_ref[...] = jnp.zeros_like(sum_ref)
        out_ref[...] = jnp.zeros_like(out_ref)

    allowed = kpos_ref[...] <= qpos_ref[...]
    query, keys, values = q_ref[...], k_ref[...], v_ref[...]
    mixed, factors = [], []
    for head in range(2):
        scores = jnp.where(allowed, dot_nt(head_only(query, head), keys), masked_score)
        old_max = max_ref[head]
        new_max = jnp.maximum(old_max, jnp.max(scores, axis=-1, keepdims=True))
        expd = jnp.exp(scores - new_max)
        factor = jnp.exp(old_max - new_max)
        sum_ref[head] = sum_ref[head] * factor + jnp.sum(expd, axis=-1, keepdims=True)
        max_ref[head] = new_max
        mixed.append(dot_nn(expd.astype(jnp.bfloat16), values))
        factors.append(factor)
    rows = query.shape[0]
    scale = head_pick(*(jnp.broadcast_to(f, (rows, PAIR)) for f in factors))
    out_ref[...] = out_ref[...] * scale + head_pick(mixed[0], mixed[1])

    @pl.when(step == last)
    def _():
        total = head_pick(*(jnp.broadcast_to(sum_ref[h], (rows, PAIR)) for h in range(2)))
        out_ref[...] = out_ref[...] / total
        lse_ref[0] = jnp.concatenate(
            [max_ref[h] + jnp.log(sum_ref[h]) for h in range(2)], axis=-1
        )


def forward_attention(query_pos, key_pos, query, keys_values):
    rows, width = query.shape
    total = keys_values.shape[0]
    chunk = chunk_of(total)
    pairs = width // PAIR
    return pl.pallas_call(
        forward_kernel,
        grid=(pairs, total // chunk),
        in_specs=[
            pl.BlockSpec((rows, 1), lambda h, c: (0, 0)),
            pl.BlockSpec((1, chunk), lambda h, c: (0, c)),
            pl.BlockSpec((rows, PAIR), lambda h, c: (0, h)),
            pl.BlockSpec((chunk, PAIR), lambda h, c: (c, h)),
            pl.BlockSpec((chunk, PAIR), lambda h, c: (c, h + pairs)),
        ],
        out_specs=[
            pl.BlockSpec((rows, PAIR), lambda h, c: (0, h)),
            pl.BlockSpec((1, rows, 2), lambda h, c: (h, 0, 0)),
        ],
        out_shape=[
            jax.ShapeDtypeStruct((rows, width), jnp.float32),
            jax.ShapeDtypeStruct((pairs, rows, 2), jnp.float32),
        ],
        scratch_shapes=[
            pltpu.VMEM((2, rows, 1), jnp.float32),
            pltpu.VMEM((2, rows, 1), jnp.float32),
        ],
        compiler_params=pltpu.CompilerParams(vmem_limit_bytes=40 * 2**20),
        cost_estimate=pl.CostEstimate(
            flops=8 * rows * total * width,
            bytes_accessed=4 * total * width,
            transcendentals=rows * total * H,
        ),
        name="attention_forward",
    )(query_pos[:, None], key_pos[None, :], query, keys_values, keys_values)


def query_kernel(qpos_ref, kpos_ref, q_ref, do_ref, stat_ref, k_ref, v_ref, dq_ref):
    @pl.when(pl.program_id(1) == 0)
    def _():
        dq_ref[...] = jnp.zeros_like(dq_ref)

    allowed = kpos_ref[...] <= qpos_ref[...]
    query, d_out, keys, values = q_ref[...], do_ref[...], k_ref[...], v_ref[...]
    parts = []
    for head in range(2):
        lse = stat_ref[0, :, head : head + 1]
        delta = stat_ref[0, :, head + 2 : head + 3]
        scores = jnp.where(allowed, dot_nt(head_only(query, head), keys), masked_score)
        prob = jnp.exp(scores - lse)
        d_prob = dot_nt(head_only(d_out, head), values)
        d_score = (prob * (d_prob - delta)).astype(jnp.bfloat16)
        parts.append(dot_nn(d_score, keys))
    dq_ref[...] += head_pick(parts[0], parts[1]) * HEAD_DIM ** (-0.5)


def query_gradient(query_pos, key_pos, query, d_out, stats, keys_values):
    rows, width = query.shape
    total = keys_values.shape[0]
    chunk = chunk_of(total)
    pairs = width // PAIR
    return pl.pallas_call(
        query_kernel,
        grid=(pairs, total // chunk),
        in_specs=[
            pl.BlockSpec((rows, 1), lambda h, c: (0, 0)),
            pl.BlockSpec((1, chunk), lambda h, c: (0, c)),
            pl.BlockSpec((rows, PAIR), lambda h, c: (0, h)),
            pl.BlockSpec((rows, PAIR), lambda h, c: (0, h)),
            pl.BlockSpec((1, rows, 4), lambda h, c: (h, 0, 0)),
            pl.BlockSpec((chunk, PAIR), lambda h, c: (c, h)),
            pl.BlockSpec((chunk, PAIR), lambda h, c: (c, h + pairs)),
        ],
        out_specs=pl.BlockSpec((rows, PAIR), lambda h, c: (0, h)),
        out_shape=jax.ShapeDtypeStruct((rows, width), jnp.float32),
        compiler_params=pltpu.CompilerParams(vmem_limit_bytes=40 * 2**20),
        cost_estimate=pl.CostEstimate(
            flops=12 * rows * total * width,
            bytes_accessed=4 * total * width,
            transcendentals=rows * total * H,
        ),
        name="attention_query_gradient",
    )(query_pos[:, None], key_pos[None, :], query, d_out, stats, keys_values, keys_values)


def key_kernel(kpos_ref, qpos_ref, k_ref, v_ref, q_ref, do_ref, stat_ref, dk_ref, dv_ref):
    @pl.when(pl.program_id(1) == 0)
    def _():
        dk_ref[...] = jnp.zeros_like(dk_ref)
        dv_ref[...] = jnp.zeros_like(dv_ref)

    allowed = kpos_ref[...] <= qpos_ref[...]
    keys, values, query, d_out = k_ref[...], v_ref[...], q_ref[...], do_ref[...]
    key_parts, value_parts = [], []
    for head in range(2):
        lse = stat_ref[0, head : head + 1, :]
        delta = stat_ref[0, head + 2 : head + 3, :]
        scores = jnp.where(allowed, dot_nt(head_only(keys, head), query), masked_score)
        prob = jnp.exp(scores - lse)
        value_parts.append(dot_nn(prob.astype(jnp.bfloat16), d_out))
        d_prob = dot_nt(head_only(values, head), d_out)
        d_score = (prob * (d_prob - delta)).astype(jnp.bfloat16)
        key_parts.append(dot_nn(d_score, query))
    dk_ref[...] += head_pick(key_parts[0], key_parts[1])
    dv_ref[...] += head_pick(value_parts[0], value_parts[1])


def key_gradients(key_pos, query_pos, qkv, query_all, d_out_all, stats_all):
    rows = qkv.shape[0]
    total, width = query_all.shape
    chunk = chunk_of(total)
    pairs = width // PAIR
    grad_spec = pl.BlockSpec((rows, PAIR), lambda h, c: (0, h))
    return pl.pallas_call(
        key_kernel,
        grid=(pairs, total // chunk),
        in_specs=[
            pl.BlockSpec((rows, 1), lambda h, c: (0, 0)),
            pl.BlockSpec((1, chunk), lambda h, c: (0, c)),
            pl.BlockSpec((rows, PAIR), lambda h, c: (0, h)),
            pl.BlockSpec((rows, PAIR), lambda h, c: (0, h + pairs)),
            pl.BlockSpec((chunk, PAIR), lambda h, c: (c, h)),
            pl.BlockSpec((chunk, PAIR), lambda h, c: (c, h)),
            pl.BlockSpec((1, 4, chunk), lambda h, c: (h, 0, c)),
        ],
        out_specs=[grad_spec, grad_spec],
        out_shape=[jax.ShapeDtypeStruct((rows, width), jnp.float32)] * 2,
        compiler_params=pltpu.CompilerParams(vmem_limit_bytes=40 * 2**20),
        cost_estimate=pl.CostEstimate(
            flops=16 * rows * total * width,
            bytes_accessed=4 * total * width,
            transcendentals=rows * total * H,
        ),
        name="attention_key_gradients",
    )(key_pos[:, None], query_pos[None, :], qkv, qkv, query_all, d_out_all, stats_all)


def whole_weight(weight):
    share = weight.shape[0] // lax.axis_size("ctx")
    mine = lax.dynamic_slice_in_dim(weight, lax.axis_index("ctx") * share, share, 0)
    return lax.all_gather(mine, ("fsdp", "ctx"), axis=0, tiled=True)


def gather_kernel(chips, shards, count, *refs):
    shares, wholes = refs[:count], refs[count : 2 * count]
    own_sem, z_send, z_recv, c_send, c_recv, k_send, k_recv = refs[2 * count :]
    me, row = lax.axis_index("ctx"), lax.axis_index("fsdp")
    chip, core = me // 2, me % 2
    sibling = (chip * 2 + 1 - core, row)

    def above(step):
        return (me, lax.rem(row + step, shards))

    def across(step):
        return (lax.rem(chip + step, chips) * 2 + core, row)

    barrier = pltpu.get_barrier_semaphore()
    greeted = [above(d) for d in range(1, shards)] + [across(d) for d in range(1, chips)]
    greeted.append(sibling)
    for other in greeted:
        pl.semaphore_signal(barrier, inc=1, device_id=other, device_id_type=pl.DeviceIdType.MESH)
    pl.semaphore_wait(barrier, len(greeted))

    def send(src, dst, send_sem, recv_sem, target):
        copy = pltpu.make_async_remote_copy(
            src_ref=src,
            dst_ref=dst,
            send_sem=send_sem,
            recv_sem=recv_sem,
            device_id=target,
            device_id_type=pl.DeviceIdType.MESH,
        )
        copy.start()
        return copy

    def column(item, index):
        return wholes[item].at[:, index]

    own, along, between, inside = {}, {}, {}, {}
    for i in range(count):
        own[i] = pltpu.make_async_copy(shares[i], wholes[i].at[row, me], own_sem.at[i])
        own[i].start()
        for d in range(1, shards):
            along[i, d] = send(
                shares[i],
                wholes[i].at[row, me],
                z_send.at[i, d - 1],
                z_recv.at[i, d - 1],
                above(d),
            )
    for i in range(count):
        own[i].wait()
        for d in range(1, shards):
            along[i, d].wait_recv()
        for d in range(1, chips):
            mine = column(i, me)
            between[i, d] = send(mine, mine, c_send.at[i, d - 1], c_recv.at[i, d - 1], across(d))
        inside[i, 0] = send(
            column(i, me), column(i, me), k_send.at[i, 0], k_recv.at[i, 0], sibling
        )
    for i in range(count):
        for d in range(1, chips):
            between[i, d].wait_recv()
            came = column(i, lax.rem(chip - d + chips, chips) * 2 + core)
            inside[i, d] = send(came, came, k_send.at[i, d], k_recv.at[i, d], sibling)
    for copy in inside.values():
        copy.wait_recv()
    for copies in (along, between, inside):
        for copy in copies.values():
            copy.wait_send()


def whole_weights(weights):
    ctx_count, shards = lax.axis_size("ctx"), lax.axis_size("fsdp")
    chips = ctx_count // 2
    if ctx_count != 8:
        return [whole_weight(item) for item in weights]
    count = len(weights)
    mine = []
    for item in weights:
        share = item.shape[0] // ctx_count
        mine.append(
            lax.dynamic_slice_in_dim(item, lax.axis_index("ctx") * share, share, 0)
        )
    anywhere = pl.BlockSpec(memory_space=pl.ANY)
    dma = pltpu.SemaphoreType.DMA
    wholes = pl.pallas_call(
        partial(gather_kernel, chips, shards, count),
        in_specs=[anywhere] * count,
        out_specs=[anywhere] * count,
        out_shape=[
            jax.ShapeDtypeStruct((shards, ctx_count) + item.shape, item.dtype) for item in mine
        ],
        scratch_shapes=[
            dma((count,)),
            dma((count, shards - 1)),
            dma((count, shards - 1)),
            dma((count, chips - 1)),
            dma((count, chips - 1)),
            dma((count, chips)),
            dma((count, chips)),
        ],
        compiler_params=pltpu.CompilerParams(collective_id=0, has_side_effects=True),
        name="gather_weights",
    )(*mine)
    return [
        whole.reshape(item.shape[0] * shards, item.shape[1])
        for whole, item in zip(wholes, weights)
    ]


def scatter_kernel(chips, shards, spans, packed, out, own, k_land, c_land, z_land, *sems):
    local, k_send, k_recv, c_send, c_recv, z_send, z_recv = sems
    me, row = lax.axis_index("ctx"), lax.axis_index("fsdp")
    chip, core = me // 2, me % 2
    sibling = (chip * 2 + 1 - core, row)

    def above(step):
        return (me, lax.rem(row + step, shards))

    def across(step):
        return (lax.rem(chip + step, chips) * 2 + core, row)

    barrier = pltpu.get_barrier_semaphore()
    greeted = [above(d) for d in range(1, shards)] + [across(d) for d in range(1, chips)]
    greeted.append(sibling)
    for other in greeted:
        pl.semaphore_signal(barrier, inc=1, device_id=other, device_id_type=pl.DeviceIdType.MESH)
    pl.semaphore_wait(barrier, len(greeted))

    def send(src, dst, send_sem, recv_sem, target):
        copy = pltpu.make_async_remote_copy(
            src_ref=src,
            dst_ref=dst,
            send_sem=send_sem,
            recv_sem=recv_sem,
            device_id=target,
            device_id_type=pl.DeviceIdType.MESH,
        )
        copy.start()
        return copy

    order = list(range(1, chips)) + [0]
    kept, inside, between, along = {}, {}, {}, {}
    for i, span in enumerate(spans):
        rows = pl.ds(*span)
        for d in order:
            part = lax.rem(chip + d, chips)
            inside[i, d] = send(
                packed.at[part, 1 - core, :, rows],
                k_land.at[part, :, rows],
                k_send.at[i, d],
                k_recv.at[i, d],
                sibling,
            )
            kept[i, d] = pltpu.make_async_copy(
                packed.at[part, core, :, rows], own.at[part, :, rows], local.at[i, d]
            )
            kept[i, d].start()
    for i, span in enumerate(spans):
        rows = pl.ds(*span)
        for d in order:
            part = lax.rem(chip + d, chips)
            kept[i, d].wait()
            inside[i, d].wait_recv()

            @pl.loop(0, shards)
            def _(f):
                total = own[part, f, rows].astype(jnp.float32)
                total += k_land[part, f, rows].astype(jnp.float32)
                own[part, f, rows] = total.astype(jnp.bfloat16)

            if d:
                between[i, d] = send(
                    own.at[part, :, rows],
                    c_land.at[d - 1, :, rows],
                    c_send.at[i, d - 1],
                    c_recv.at[i, d - 1],
                    across(d),
                )
    for i, span in enumerate(spans):
        rows = pl.ds(*span)
        for d in range(1, chips):
            between[i, d].wait_recv()

        @pl.loop(0, shards)
        def _(f):
            total = own[chip, f, rows].astype(jnp.float32)
            for d in range(1, chips):
                total += c_land[d - 1, f, rows].astype(jnp.float32)
            own[chip, f, rows] = total.astype(jnp.bfloat16)

        for d in range(1, shards):
            along[i, d] = send(
                own.at[chip, lax.rem(row + d, shards), rows],
                z_land.at[d - 1, rows],
                z_send.at[i, d - 1],
                z_recv.at[i, d - 1],
                above(d),
            )
    for i, span in enumerate(spans):
        rows = pl.ds(*span)
        for d in range(1, shards):
            along[i, d].wait_recv()
        total = own[chip, row, rows].astype(jnp.float32)
        for d in range(1, shards):
            total += z_land[d - 1, rows].astype(jnp.float32)
        out[rows] = total
    for copies in (inside, between, along):
        for copy in copies.values():
            copy.wait_send()


def scatter_packed(packed):
    ctx_count, shards = lax.axis_size("ctx"), lax.axis_size("fsdp")
    _, rows, width = packed.shape
    if ctx_count != 8:
        return scatter(packed.reshape(-1, width)).astype(jnp.float32)
    chips = ctx_count // 2
    first = 16 * (-(-rows // 32))
    spans = ((0, first), (first, rows - first))
    dma = pltpu.SemaphoreType.DMA
    low = jnp.bfloat16
    return pl.pallas_call(
        partial(scatter_kernel, chips, shards, spans),
        in_specs=[pl.BlockSpec(memory_space=pl.ANY)],
        out_specs=pl.BlockSpec(memory_space=pltpu.VMEM),
        out_shape=jax.ShapeDtypeStruct((rows, width), jnp.float32),
        scratch_shapes=[
            pltpu.VMEM((chips, shards, rows, width), low),
            pltpu.VMEM((chips, shards, rows, width), low),
            pltpu.VMEM((chips - 1, shards, rows, width), low),
            pltpu.VMEM((shards - 1, rows, width), low),
            dma((2, chips)),
            dma((2, chips)),
            dma((2, chips)),
            dma((2, chips - 1)),
            dma((2, chips - 1)),
            dma((2, shards - 1)),
            dma((2, shards - 1)),
        ],
        compiler_params=pltpu.CompilerParams(
            collective_id=1, has_side_effects=True, vmem_limit_bytes=44 * 2**20
        ),
        name="sum_gradients",
    )(packed.reshape(chips, 2, shards, rows, width))


def all_positions(pair_table, ctx_count):
    column = jnp.arange(2 * BLK, dtype=jnp.int32)[None, :]
    pair = pair_table[:, None]
    lower = pair * BLK + column
    upper = (2 * ctx_count - 1 - pair) * BLK + column - BLK
    return jnp.where(column < BLK, lower, upper).reshape(-1)


def scatter(term):
    return lax.psum_scatter(term, ("ctx", "fsdp"), scatter_dimension=0, tiled=True)


class Spot:
    def __init__(self, shards):
        self.shards = shards
        self.me, self.row = lax.axis_index("ctx"), lax.axis_index("fsdp")
        chip, core = self.me // 2, self.me % 2
        y, x = chip // 2, chip % 2
        self.core = core
        self.a = (1 - core) * x + core * y
        self.b = (1 - core) * y + core * x
        self.first = self.index(1 - self.a, self.b)
        self.second = self.index(self.a, 1 - self.b)
        self.corner = self.index(1 - self.a, 1 - self.b)
        self.sibling = chip * 2 + 1 - core

    def chip_of(self, a, b):
        return (1 - self.core) * (2 * b + a) + self.core * (2 * a + b)

    def index(self, a, b):
        return self.chip_of(a, b) * 2 + self.core

    def near(self, ctx):
        return (ctx, self.row)

    def above(self, step):
        return (self.me, lax.rem(self.row + step, self.shards))

    def came(self, step):
        return lax.rem(self.row - step + self.shards, self.shards)

    def greet(self):
        barrier = pltpu.get_barrier_semaphore()
        others = [self.above(d) for d in range(1, self.shards)]
        others += [self.near(i) for i in (self.first, self.second, self.sibling)]
        for other in others:
            pl.semaphore_signal(
                barrier, inc=1, device_id=other, device_id_type=pl.DeviceIdType.MESH
            )
        pl.semaphore_wait(barrier, len(others))


def send(src, dst, send_sem, recv_sem, target):
    copy = pltpu.make_async_remote_copy(
        src_ref=src,
        dst_ref=dst,
        send_sem=send_sem,
        recv_sem=recv_sem,
        device_id=target,
        device_id_type=pl.DeviceIdType.MESH,
    )
    copy.start()
    return copy


class Gather:
    def __init__(self, spot, shard, whole, sems):
        self.spot, self.shard, self.whole, self.sems = spot, shard, whole, sems
        self.rows, columns = shard.shape
        self.half = columns // 2
        self.copies = {}

    def cols(self):
        return pl.ds(pl.multiple_of(self.spot.core * self.half, 128), self.half)

    def part(self, row, start, size):
        begin = pl.multiple_of(row * self.rows + start, 16)
        return self.whole.at[pl.ds(begin, size), self.cols()]

    def post(self, stage, d, src, dst, target):
        n = self.spot.shards - 1
        at = stage * n + d - 1
        self.copies[stage, d] = send(
            src, dst, self.sems[0].at[at], self.sems[1].at[at], target
        )

    def own(self):
        begin = pl.multiple_of(self.spot.row * self.rows, 16)
        copy = pltpu.make_async_copy(
            self.shard, self.whole.at[pl.ds(begin, self.rows)], self.sems[2]
        )
        copy.start()
        return copy

    def along(self):
        spot, quarter = self.spot, self.rows // 4
        start = (2 * spot.b + spot.a) * quarter
        src = self.shard.at[pl.ds(pl.multiple_of(start, 16), quarter), self.cols()]
        for d in range(1, spot.shards):
            self.post(0, d, src, self.part(spot.row, start, quarter), spot.above(d))

    def step_one(self):
        spot, quarter = self.spot, self.rows // 4
        start = (2 * spot.b + spot.a) * quarter
        for d in range(1, spot.shards):
            self.copies[0, d].wait_recv()
            ref = self.part(spot.came(d), start, quarter)
            self.post(1, d, ref, ref, spot.near(spot.first))

    def step_two(self):
        spot, half = self.spot, self.rows // 2
        for d in range(1, spot.shards):
            self.copies[1, d].wait_recv()
            ref = self.part(spot.came(d), spot.b * half, half)
            self.post(2, d, ref, ref, spot.near(spot.second))
            self.post(3, d, ref, ref, spot.near(spot.sibling))

    def step_three(self):
        spot, half = self.spot, self.rows // 2
        for d in range(1, spot.shards):
            self.copies[2, d].wait_recv()
            ref = self.part(spot.came(d), (1 - spot.b) * half, half)
            self.post(4, d, ref, ref, spot.near(spot.sibling))

    def finish(self):
        for d in range(1, self.spot.shards):
            self.copies[3, d].wait_recv()
            self.copies[4, d].wait_recv()

    def drain(self):
        for copy in self.copies.values():
            copy.wait_send()


class Exchange:
    def __init__(self, spot, whole, view, sems):
        self.spot, self.sems = spot, sems
        self.view = lambda device: view(whole, device)
        self.copies = {}

    def post(self, at, device, target):
        ref = self.view(device)
        self.copies[at] = send(
            ref, ref, self.sems[0].at[at], self.sems[1].at[at], self.spot.near(target)
        )

    def start(self):
        spot = self.spot
        self.post(0, spot.me, spot.first)
        self.post(1, spot.me, spot.second)
        self.post(2, spot.me, spot.sibling)

    def pass_on(self):
        spot = self.spot
        self.copies[0].wait_recv()
        self.post(3, spot.first, spot.second)
        self.post(4, spot.first, spot.sibling)

    def share(self):
        spot = self.spot
        self.copies[1].wait_recv()
        self.post(5, spot.second, spot.sibling)
        self.copies[3].wait_recv()
        self.post(6, spot.corner, spot.sibling)

    def finish(self):
        for at in (2, 4, 5, 6):
            self.copies[at].wait_recv()

    def drain(self):
        for copy in self.copies.values():
            copy.wait_send()


def front_kernel(
    shards,
    x_ref,
    gain_ref,
    shift_ref,
    qbias_ref,
    vbias_ref,
    qpos_ref,
    kpos_ref,
    qkv_shard,
    out_shard,
    fc_shard,
    proj_shard,
    first_ref,
    query_ref,
    attn_ref,
    lse_ref,
    kv_out,
    qkv_out,
    out_out,
    fc_out,
    proj_out,
    qkv_ref,
    kv_ref,
    *sems,
):
    spot = Spot(shards)
    spot.greet()
    weights = [
        Gather(spot, shard, whole, sems[3 * i : 3 * i + 3])
        for i, (shard, whole) in enumerate(
            (
                (qkv_shard, qkv_ref),
                (out_shard, out_out),
                (fc_shard, fc_out),
                (proj_shard, proj_out),
            )
        )
    ]
    key_sems, value_sems, keep_sem = sems[12:14], sems[14:16], sems[16]
    qkv, out, fc, proj = weights
    qkv.along()
    own = [item.own() for item in weights]
    normed, _ = normalize(x_ref[...].astype(jnp.float32))
    first_ref[...] = (normed * gain_ref[...] + shift_ref[...]).astype(jnp.bfloat16)
    qkv.step_one()
    out.along()
    fc.along()
    qkv.step_two()
    proj.along()
    qkv.step_three()
    own[0].wait()
    qkv.finish()
    width = x_ref.shape[1]

    def columns(start):
        def view(whole, device):
            return whole.at[device, :, pl.ds(start, width)]

        return view

    first_in = first_ref[...]
    keys = Exchange(spot, kv_ref, columns(0), key_sems)
    values = Exchange(spot, kv_ref, columns(width), value_sems)
    kv_ref[spot.me, :, pl.ds(0, width)] = dot_nn(
        first_in, qkv_ref[:, pl.ds(width, width)]
    ).astype(jnp.bfloat16)
    keys.start()
    kv_ref[spot.me, :, pl.ds(width, width)] = (
        dot_nn(first_in, qkv_ref[:, pl.ds(2 * width, width)]) + vbias_ref[...]
    ).astype(jnp.bfloat16)
    values.start()
    query_ref[...] = (
        (dot_nn(first_in, qkv_ref[:, pl.ds(0, width)]) + qbias_ref[...]).astype(jnp.bfloat16)
        * jnp.bfloat16(HEAD_DIM ** (-0.5))
    )
    keep_qkv = pltpu.make_async_copy(qkv_ref, qkv_out, keep_sem.at[0])
    keep_qkv.start()
    keys.pass_on()
    values.pass_on()
    out.step_one()
    fc.step_one()
    keys.share()
    values.share()
    out.step_two()
    proj.step_one()
    keys.finish()
    values.finish()
    keep_kv = pltpu.make_async_copy(kv_ref, kv_out, keep_sem.at[1])
    keep_kv.start()
    allowed = kpos_ref[...] <= qpos_ref[...]
    rows = x_ref.shape[0]
    total = kv_ref.shape[0] * rows

    def attend(h):
        lanes = pl.ds(pl.multiple_of(h * PAIR, PAIR), PAIR)
        value_lanes = pl.ds(pl.multiple_of(width + h * PAIR, PAIR), PAIR)
        query = query_ref[:, lanes]
        keys_all = kv_ref[:, :, lanes].reshape(total, PAIR)
        values_all = kv_ref[:, :, value_lanes].reshape(total, PAIR)
        mixed, stats = [], []
        for head in range(2):
            scores = jnp.where(allowed, dot_nt(head_only(query, head), keys_all), masked_score)
            most = jnp.max(scores, axis=-1, keepdims=True)
            expd = jnp.exp(scores - most)
            norm = jnp.sum(expd, axis=-1, keepdims=True)
            mixed.append(dot_nn(expd.astype(jnp.bfloat16), values_all) / norm)
            stats.append(most + jnp.log(norm))
        attn_ref[:, lanes] = head_pick(mixed[0], mixed[1])
        lse_ref[h] = jnp.concatenate(stats, axis=-1)

    pairs = width // PAIR
    fc.step_two()
    pl.loop(0, pairs // 2)(attend)
    out.step_three()
    proj.step_two()
    pl.loop(pairs // 2, pairs)(attend)
    fc.step_three()
    proj.step_three()
    for item in (out, fc, proj):
        item.finish()
    for copy in own[1:]:
        copy.wait()
    for item in (*weights, keys, values):
        item.drain()
    keep_qkv.wait()
    keep_kv.wait()


def front(layer_in, gain, shift, qbias, vbias, query_pos, key_pos, weights):
    shards, ctx_count = lax.axis_size("fsdp"), lax.axis_size("ctx")
    rows, width = layer_in.shape
    pairs = width // PAIR
    low, wide = jnp.bfloat16, jnp.float32
    dma = pltpu.SemaphoreType.DMA
    anywhere = pl.BlockSpec(memory_space=pl.ANY)
    inside = pl.BlockSpec(memory_space=pltpu.VMEM)
    whole = [jax.ShapeDtypeStruct((w.shape[0] * shards, w.shape[1]), low) for w in weights]
    kv_shape = (ctx_count, rows, 2 * width)
    gather_sems = [dma((5 * (shards - 1),)), dma((5 * (shards - 1),)), dma] * 4
    return pl.pallas_call(
        partial(front_kernel, shards),
        in_specs=[inside] * 7 + [anywhere] * 4,
        out_specs=[inside] * 4 + [anywhere] * 5,
        out_shape=[
            jax.ShapeDtypeStruct((rows, width), low),
            jax.ShapeDtypeStruct((rows, width), low),
            jax.ShapeDtypeStruct((rows, width), wide),
            jax.ShapeDtypeStruct((pairs, rows, 2), wide),
            jax.ShapeDtypeStruct(kv_shape, low),
        ]
        + whole,
        scratch_shapes=[
            pltpu.VMEM(whole[0].shape, low),
            pltpu.VMEM(kv_shape, low),
        ]
        + gather_sems
        + [dma((7,))] * 4
        + [dma((2,))],
        compiler_params=pltpu.CompilerParams(
            collective_id=0, has_side_effects=True, vmem_limit_bytes=48 * 2**20
        ),
        name="front",
    )(
        layer_in,
        gain[None, :],
        shift[None, :],
        qbias[None, :],
        vbias[None, :],
        query_pos[:, None],
        key_pos[None, :],
        *weights,
    )


def per_device(
    layer_in,
    qkv_weight,
    query_bias,
    value_bias,
    out_weight,
    out_bias,
    fc_weight,
    fc_bias,
    proj_weight,
    proj_bias,
    attn_norm_gain,
    attn_norm_shift,
    mlp_norm_gain,
    mlp_norm_shift,
    cotangent,
    pair_table,
):
    ctx_count = lax.axis_size("ctx")
    shards = ctx_count * lax.axis_size("fsdp")
    _, _, rows, width = layer_in.shape
    my_pos = block_positions(pair_table, lax.axis_index("ctx"), ctx_count)
    every_pos = all_positions(pair_table, ctx_count)
    flat_in = layer_in.reshape(rows, width).astype(jnp.float32)
    normed_one, inverse_one = normalize(flat_in)
    if ctx_count == 8:
        (
            first_in,
            query,
            attn_exact,
            lse,
            every_kv,
            full_qkv,
            full_out,
            full_fc,
            full_proj,
        ) = front(
            layer_in.reshape(rows, width),
            attn_norm_gain,
            attn_norm_shift,
            query_bias,
            value_bias,
            my_pos,
            every_pos,
            (qkv_weight, out_weight, fc_weight, proj_weight),
        )
        keys_values = lax.dynamic_index_in_dim(every_kv, lax.axis_index("ctx"), 0, False)
        every_kv = every_kv.reshape(-1, 2 * width)
        every_query = lax.all_gather(query, "ctx", axis=0, tiled=True)
    else:
        full_qkv, full_out, full_fc, full_proj = whole_weights(
            (qkv_weight, out_weight, fc_weight, proj_weight)
        )
        first_in = (normed_one * attn_norm_gain + attn_norm_shift).astype(jnp.bfloat16)
        keys_values = (
            jnp.dot(first_in, full_qkv[:, width:], preferred_element_type=jnp.float32)
            + jnp.concatenate([jnp.zeros_like(value_bias), value_bias])
        ).astype(jnp.bfloat16)
        every_kv = lax.all_gather(keys_values, "ctx", axis=0, tiled=True)
        query = (
            jnp.dot(first_in, full_qkv[:, :width], preferred_element_type=jnp.float32) + query_bias
        ).astype(jnp.bfloat16) * jnp.bfloat16(HEAD_DIM ** (-0.5))
        every_query = lax.all_gather(query, "ctx", axis=0, tiled=True)
        attn_exact, lse = forward_attention(my_pos, every_pos, query, every_kv)
    attended = attn_exact.astype(jnp.bfloat16)
    middle = flat_in + jnp.dot(attended, full_out, preferred_element_type=jnp.float32) + out_bias
    normed_two, inverse_two = normalize(middle)
    second_in = (normed_two * mlp_norm_gain + mlp_norm_shift).astype(jnp.bfloat16)
    pre_act = jnp.dot(second_in, full_fc, preferred_element_type=jnp.float32) + fc_bias
    activated, gelu_back = jax.vjp(partial(jax.nn.gelu, approximate=True), pre_act)
    act_low = activated.astype(jnp.bfloat16)
    result = middle + jnp.dot(act_low, full_proj, preferred_element_type=jnp.float32) + proj_bias
    layer_out = result.astype(jnp.bfloat16).reshape(layer_in.shape)
    d_result = cotangent.reshape(rows, width)
    d_act = jnp.einsum("td,fd->tf", d_result, full_proj, preferred_element_type=jnp.float32)
    (d_pre,) = gelu_back(d_act)
    d_pre_low = d_pre.astype(jnp.bfloat16)
    d_second = jnp.einsum("tf,df->td", d_pre_low, full_fc, preferred_element_type=jnp.float32)
    d_mid_norm, grad_mlp_gain, grad_mlp_shift = norm_back(
        d_second, normed_two, inverse_two, mlp_norm_gain
    )
    d_middle = d_result.astype(jnp.float32) + d_mid_norm
    d_branch = d_middle.astype(jnp.bfloat16)
    d_attended = jnp.einsum(
        "te,de->td", d_branch, full_out, preferred_element_type=jnp.float32
    ).astype(jnp.bfloat16)
    delta = jnp.sum(
        (d_attended.astype(jnp.float32) * attn_exact).reshape(rows, width // PAIR, 2, HEAD_DIM),
        axis=-1,
    )
    stats = jnp.concatenate([lse, jnp.transpose(delta, (1, 0, 2))], axis=-1)
    every_d_out = lax.all_gather(d_attended, "ctx", axis=0, tiled=True)
    every_stat = lax.all_gather(
        jnp.transpose(stats, (0, 2, 1)).reshape(-1, rows), "ctx", axis=1, tiled=True
    ).reshape(width // PAIR, 4, ctx_count * rows)
    grad_proj = jnp.einsum("tf,td->fd", act_low, d_result, preferred_element_type=jnp.float32)
    grad_fc = jnp.einsum("td,tf->df", second_in, d_pre_low, preferred_element_type=jnp.float32)
    grad_out = jnp.einsum("td,te->de", attended, d_branch, preferred_element_type=jnp.float32)
    d_query = query_gradient(my_pos, every_pos, query, d_attended, stats, every_kv)
    d_key, d_value = key_gradients(
        my_pos, every_pos, keys_values, every_query, every_d_out, every_stat
    )
    d_qkv = jnp.concatenate([d_query, d_key, d_value], axis=1).astype(jnp.bfloat16)
    grad_qkv = jnp.einsum("td,te->de", first_in, d_qkv, preferred_element_type=jnp.float32)
    d_first = jnp.einsum("te,de->td", d_qkv, full_qkv, preferred_element_type=jnp.float32)
    d_in_norm, grad_attn_gain, grad_attn_shift = norm_back(
        d_first, normed_one, inverse_one, attn_norm_gain
    )
    grad_in = (d_middle + d_in_norm).reshape(layer_in.shape)
    bias_sum = jnp.sum(d_qkv.astype(jnp.float32), axis=0)
    vectors = (
        bias_sum[:width],
        bias_sum[2 * width :],
        jnp.sum(d_middle, axis=0),
        jnp.sum(d_pre_low.astype(jnp.float32), axis=0),
        jnp.sum(d_result.astype(jnp.float32), axis=0),
        grad_attn_gain,
        grad_attn_shift,
        grad_mlp_gain,
        grad_mlp_shift,
    )
    small = jnp.concatenate([item.reshape(shards, -1) for item in vectors], axis=1)
    lines = 16 * -(-small.shape[1] // (16 * width))
    small = jnp.pad(small, ((0, 0), (0, lines * width - small.shape[1])))
    matrices = (
        [grad_qkv[:, i * width : (i + 1) * width] for i in range(3)]
        + [grad_out]
        + [grad_fc[:, i * width : (i + 1) * width] for i in range(grad_fc.shape[1] // width)]
        + [grad_proj, small.reshape(shards * lines, width)]
    )
    packed = jnp.concatenate(
        [item.astype(jnp.bfloat16).reshape(shards, -1, width) for item in matrices], axis=1
    )
    summed = scatter_packed(packed)
    pieces, start = [], 0
    for item in matrices:
        size = item.shape[0] // shards
        pieces.append(summed[start : start + size])
        start += size
    sum_qkv = jnp.concatenate(pieces[:3], axis=1)
    sum_out = pieces[3]
    sum_fc = jnp.concatenate(pieces[4:-2], axis=1)
    sum_proj = pieces[-2]
    sum_small = pieces[-1].reshape(-1)
    small, start = [], 0
    for item in vectors:
        size = item.shape[0] // shards
        small.append(sum_small[start : start + size])
        start += size
    return (
        layer_out,
        grad_in,
        sum_qkv,
        small[0],
        small[1],
        sum_out,
        small[2],
        sum_fc,
        small[3],
        sum_proj,
        small[4],
        small[5],
        small[6],
        small[7],
        small[8],
    )


def solution(mesh):
    return jax.shard_map(
        per_device,
        mesh=mesh,
        in_specs=(
            P("fsdp", "ctx", None, None),
            P("fsdp", None),
            P(),
            P(),
            P("fsdp", None),
            P(),
            P("fsdp", None),
            P(),
            P("fsdp", None),
            P(),
            P(),
            P(),
            P(),
            P(),
            P("fsdp", "ctx", None, None),
            P(),
        ),
        out_specs=(
            P("fsdp", "ctx", None, None),
            P("fsdp", "ctx", None, None),
            P(("ctx", "fsdp"), None),
            P(("ctx", "fsdp")),
            P(("ctx", "fsdp")),
            P(("ctx", "fsdp"), None),
            P(("ctx", "fsdp")),
            P(("ctx", "fsdp"), None),
            P(("ctx", "fsdp")),
            P(("ctx", "fsdp"), None),
            P(("ctx", "fsdp")),
            P(("ctx", "fsdp")),
            P(("ctx", "fsdp")),
            P(("ctx", "fsdp")),
            P(("ctx", "fsdp")),
        ),
        check_vma=False,
    )
```

```python
from functools import partial

import jax
import jax.numpy as jnp
from jax import lax
from jax.experimental import pallas as pl
from jax.experimental.pallas import tpu as pltpu
from jax.sharding import PartitionSpec as P

H = 12
HEAD_DIM = 64
BLK = 96


epsilon = 1e-05
masked_score = -1e30


def normalize(values):
    centered = values - jnp.mean(values, axis=-1, keepdims=True)
    inverse = lax.rsqrt(jnp.mean(centered * centered, axis=-1, keepdims=True) + epsilon)
    return (centered * inverse, inverse)


def norm_back(grad_out, normed, inverse, gain):
    scaled = grad_out * gain
    grad_input = inverse * (
        scaled
        - jnp.mean(scaled, axis=-1, keepdims=True)
        - normed * jnp.mean(scaled * normed, axis=-1, keepdims=True)
    )
    return (grad_input, jnp.sum(grad_out * normed, axis=0), jnp.sum(grad_out, axis=0))


def block_positions(pair_table, device, ctx_count):
    pair_index = lax.dynamic_index_in_dim(pair_table, device, 0, keepdims=False)
    column = jnp.arange(2 * BLK, dtype=jnp.int32)
    lower = pair_index * BLK + column
    upper = (2 * ctx_count - 1 - pair_index) * BLK + column - BLK
    return jnp.where(column < BLK, lower, upper)


PAIR = 2 * HEAD_DIM
CHUNK = 8 * 2 * BLK
NT = (((1,), (1,)), ((), ()))


def chunk_of(total):
    return CHUNK if total % CHUNK == 0 else total


def head_only(block, head):
    lane = lax.broadcasted_iota(jnp.int32, block.shape, 1)
    return jnp.where((lane // HEAD_DIM) == head, block, jnp.zeros_like(block))


def head_pick(first, second):
    lane = lax.broadcasted_iota(jnp.int32, first.shape, 1)
    return jnp.where(lane < HEAD_DIM, first, second)


def dot_nt(left, right):
    return lax.dot_general(left, right, NT, preferred_element_type=jnp.float32)


def dot_nn(left, right):
    return jnp.dot(left, right, preferred_element_type=jnp.float32)


def forward_kernel(qpos_ref, kpos_ref, q_ref, k_ref, v_ref, out_ref, lse_ref, max_ref, sum_ref):
    step = pl.program_id(1)
    last = pl.num_programs(1) - 1

    @pl.when(step == 0)
    def _():
        max_ref[...] = jnp.full_like(max_ref, masked_score)
        sum_ref[...] = jnp.zeros_like(sum_ref)
        out_ref[...] = jnp.zeros_like(out_ref)

    allowed = kpos_ref[...] <= qpos_ref[...]
    query, keys, values = q_ref[...], k_ref[...], v_ref[...]
    mixed, factors = [], []
    for head in range(2):
        scores = jnp.where(allowed, dot_nt(head_only(query, head), keys), masked_score)
        old_max = max_ref[head]
        new_max = jnp.maximum(old_max, jnp.max(scores, axis=-1, keepdims=True))
        expd = jnp.exp(scores - new_max)
        factor = jnp.exp(old_max - new_max)
        sum_ref[head] = sum_ref[head] * factor + jnp.sum(expd, axis=-1, keepdims=True)
        max_ref[head] = new_max
        mixed.append(dot_nn(expd.astype(jnp.bfloat16), values))
        factors.append(factor)
    rows = query.shape[0]
    scale = head_pick(*(jnp.broadcast_to(f, (rows, PAIR)) for f in factors))
    out_ref[...] = out_ref[...] * scale + head_pick(mixed[0], mixed[1])

    @pl.when(step == last)
    def _():
        total = head_pick(*(jnp.broadcast_to(sum_ref[h], (rows, PAIR)) for h in range(2)))
        out_ref[...] = out_ref[...] / total
        lse_ref[0] = jnp.concatenate(
            [max_ref[h] + jnp.log(sum_ref[h]) for h in range(2)], axis=-1
        )


def forward_attention(query_pos, key_pos, query, keys_values):
    rows, width = query.shape
    total = keys_values.shape[0]
    chunk = chunk_of(total)
    pairs = width // PAIR
    return pl.pallas_call(
        forward_kernel,
        grid=(pairs, total // chunk),
        in_specs=[
            pl.BlockSpec((rows, 1), lambda h, c: (0, 0)),
            pl.BlockSpec((1, chunk), lambda h, c: (0, c)),
            pl.BlockSpec((rows, PAIR), lambda h, c: (0, h)),
            pl.BlockSpec((chunk, PAIR), lambda h, c: (c, h)),
            pl.BlockSpec((chunk, PAIR), lambda h, c: (c, h + pairs)),
        ],
        out_specs=[
            pl.BlockSpec((rows, PAIR), lambda h, c: (0, h)),
            pl.BlockSpec((1, rows, 2), lambda h, c: (h, 0, 0)),
        ],
        out_shape=[
            jax.ShapeDtypeStruct((rows, width), jnp.float32),
            jax.ShapeDtypeStruct((pairs, rows, 2), jnp.float32),
        ],
        scratch_shapes=[
            pltpu.VMEM((2, rows, 1), jnp.float32),
            pltpu.VMEM((2, rows, 1), jnp.float32),
        ],
        compiler_params=pltpu.CompilerParams(vmem_limit_bytes=40 * 2**20),
        cost_estimate=pl.CostEstimate(
            flops=8 * rows * total * width,
            bytes_accessed=4 * total * width,
            transcendentals=rows * total * H,
        ),
        name="attention_forward",
    )(query_pos[:, None], key_pos[None, :], query, keys_values, keys_values)


def query_kernel(qpos_ref, kpos_ref, q_ref, do_ref, stat_ref, k_ref, v_ref, dq_ref):
    @pl.when(pl.program_id(1) == 0)
    def _():
        dq_ref[...] = jnp.zeros_like(dq_ref)

    allowed = kpos_ref[...] <= qpos_ref[...]
    query, d_out, keys, values = q_ref[...], do_ref[...], k_ref[...], v_ref[...]
    parts = []
    for head in range(2):
        lse = stat_ref[0, :, head : head + 1]
        delta = stat_ref[0, :, head + 2 : head + 3]
        scores = jnp.where(allowed, dot_nt(head_only(query, head), keys), masked_score)
        prob = jnp.exp(scores - lse)
        d_prob = dot_nt(head_only(d_out, head), values)
        d_score = (prob * (d_prob - delta)).astype(jnp.bfloat16)
        parts.append(dot_nn(d_score, keys))
    dq_ref[...] += head_pick(parts[0], parts[1]) * HEAD_DIM ** (-0.5)


def query_gradient(query_pos, key_pos, query, d_out, stats, keys_values):
    rows, width = query.shape
    total = keys_values.shape[0]
    chunk = chunk_of(total)
    pairs = width // PAIR
    return pl.pallas_call(
        query_kernel,
        grid=(pairs, total // chunk),
        in_specs=[
            pl.BlockSpec((rows, 1), lambda h, c: (0, 0)),
            pl.BlockSpec((1, chunk), lambda h, c: (0, c)),
            pl.BlockSpec((rows, PAIR), lambda h, c: (0, h)),
            pl.BlockSpec((rows, PAIR), lambda h, c: (0, h)),
            pl.BlockSpec((1, rows, 4), lambda h, c: (h, 0, 0)),
            pl.BlockSpec((chunk, PAIR), lambda h, c: (c, h)),
            pl.BlockSpec((chunk, PAIR), lambda h, c: (c, h + pairs)),
        ],
        out_specs=pl.BlockSpec((rows, PAIR), lambda h, c: (0, h)),
        out_shape=jax.ShapeDtypeStruct((rows, width), jnp.float32),
        compiler_params=pltpu.CompilerParams(vmem_limit_bytes=40 * 2**20),
        cost_estimate=pl.CostEstimate(
            flops=12 * rows * total * width,
            bytes_accessed=4 * total * width,
            transcendentals=rows * total * H,
        ),
        name="attention_query_gradient",
    )(query_pos[:, None], key_pos[None, :], query, d_out, stats, keys_values, keys_values)


def key_kernel(kpos_ref, qpos_ref, k_ref, v_ref, q_ref, do_ref, stat_ref, dk_ref, dv_ref):
    @pl.when(pl.program_id(1) == 0)
    def _():
        dk_ref[...] = jnp.zeros_like(dk_ref)
        dv_ref[...] = jnp.zeros_like(dv_ref)

    allowed = kpos_ref[...] <= qpos_ref[...]
    keys, values, query, d_out = k_ref[...], v_ref[...], q_ref[...], do_ref[...]
    key_parts, value_parts = [], []
    for head in range(2):
        lse = stat_ref[0, head : head + 1, :]
        delta = stat_ref[0, head + 2 : head + 3, :]
        scores = jnp.where(allowed, dot_nt(head_only(keys, head), query), masked_score)
        prob = jnp.exp(scores - lse)
        value_parts.append(dot_nn(prob.astype(jnp.bfloat16), d_out))
        d_prob = dot_nt(head_only(values, head), d_out)
        d_score = (prob * (d_prob - delta)).astype(jnp.bfloat16)
        key_parts.append(dot_nn(d_score, query))
    dk_ref[...] += head_pick(key_parts[0], key_parts[1])
    dv_ref[...] += head_pick(value_parts[0], value_parts[1])


def key_gradients(key_pos, query_pos, qkv, query_all, d_out_all, stats_all):
    rows = qkv.shape[0]
    total, width = query_all.shape
    chunk = chunk_of(total)
    pairs = width // PAIR
    grad_spec = pl.BlockSpec((rows, PAIR), lambda h, c: (0, h))
    return pl.pallas_call(
        key_kernel,
        grid=(pairs, total // chunk),
        in_specs=[
            pl.BlockSpec((rows, 1), lambda h, c: (0, 0)),
            pl.BlockSpec((1, chunk), lambda h, c: (0, c)),
            pl.BlockSpec((rows, PAIR), lambda h, c: (0, h)),
            pl.BlockSpec((rows, PAIR), lambda h, c: (0, h + pairs)),
            pl.BlockSpec((chunk, PAIR), lambda h, c: (c, h)),
            pl.BlockSpec((chunk, PAIR), lambda h, c: (c, h)),
            pl.BlockSpec((1, 4, chunk), lambda h, c: (h, 0, c)),
        ],
        out_specs=[grad_spec, grad_spec],
        out_shape=[jax.ShapeDtypeStruct((rows, width), jnp.float32)] * 2,
        compiler_params=pltpu.CompilerParams(vmem_limit_bytes=40 * 2**20),
        cost_estimate=pl.CostEstimate(
            flops=16 * rows * total * width,
            bytes_accessed=4 * total * width,
            transcendentals=rows * total * H,
        ),
        name="attention_key_gradients",
    )(key_pos[:, None], query_pos[None, :], qkv, qkv, query_all, d_out_all, stats_all)


def whole_weight(weight):
    share = weight.shape[0] // lax.axis_size("ctx")
    mine = lax.dynamic_slice_in_dim(weight, lax.axis_index("ctx") * share, share, 0)
    return lax.all_gather(mine, ("fsdp", "ctx"), axis=0, tiled=True)


def gather_kernel(chips, shards, count, *refs):
    shares, wholes = refs[:count], refs[count : 2 * count]
    own_sem, z_send, z_recv, c_send, c_recv, k_send, k_recv = refs[2 * count :]
    me, row = lax.axis_index("ctx"), lax.axis_index("fsdp")
    chip, core = me // 2, me % 2
    sibling = (chip * 2 + 1 - core, row)

    def above(step):
        return (me, lax.rem(row + step, shards))

    def across(step):
        return (lax.rem(chip + step, chips) * 2 + core, row)

    barrier = pltpu.get_barrier_semaphore()
    greeted = [above(d) for d in range(1, shards)] + [across(d) for d in range(1, chips)]
    greeted.append(sibling)
    for other in greeted:
        pl.semaphore_signal(barrier, inc=1, device_id=other, device_id_type=pl.DeviceIdType.MESH)
    pl.semaphore_wait(barrier, len(greeted))

    def send(src, dst, send_sem, recv_sem, target):
        copy = pltpu.make_async_remote_copy(
            src_ref=src,
            dst_ref=dst,
            send_sem=send_sem,
            recv_sem=recv_sem,
            device_id=target,
            device_id_type=pl.DeviceIdType.MESH,
        )
        copy.start()
        return copy

    def column(item, index):
        return wholes[item].at[:, index]

    own, along, between, inside = {}, {}, {}, {}
    for i in range(count):
        own[i] = pltpu.make_async_copy(shares[i], wholes[i].at[row, me], own_sem.at[i])
        own[i].start()
        for d in range(1, shards):
            along[i, d] = send(
                shares[i],
                wholes[i].at[row, me],
                z_send.at[i, d - 1],
                z_recv.at[i, d - 1],
                above(d),
            )
    for i in range(count):
        own[i].wait()
        for d in range(1, shards):
            along[i, d].wait_recv()
        for d in range(1, chips):
            mine = column(i, me)
            between[i, d] = send(mine, mine, c_send.at[i, d - 1], c_recv.at[i, d - 1], across(d))
        inside[i, 0] = send(
            column(i, me), column(i, me), k_send.at[i, 0], k_recv.at[i, 0], sibling
        )
    for i in range(count):
        for d in range(1, chips):
            between[i, d].wait_recv()
            came = column(i, lax.rem(chip - d + chips, chips) * 2 + core)
            inside[i, d] = send(came, came, k_send.at[i, d], k_recv.at[i, d], sibling)
    for copy in inside.values():
        copy.wait_recv()
    for copies in (along, between, inside):
        for copy in copies.values():
            copy.wait_send()


def whole_weights(weights):
    ctx_count, shards = lax.axis_size("ctx"), lax.axis_size("fsdp")
    chips = ctx_count // 2
    if ctx_count != 8:
        return [whole_weight(item) for item in weights]
    count = len(weights)
    mine = []
    for item in weights:
        share = item.shape[0] // ctx_count
        mine.append(
            lax.dynamic_slice_in_dim(item, lax.axis_index("ctx") * share, share, 0)
        )
    anywhere = pl.BlockSpec(memory_space=pl.ANY)
    dma = pltpu.SemaphoreType.DMA
    wholes = pl.pallas_call(
        partial(gather_kernel, chips, shards, count),
        in_specs=[anywhere] * count,
        out_specs=[anywhere] * count,
        out_shape=[
            jax.ShapeDtypeStruct((shards, ctx_count) + item.shape, item.dtype) for item in mine
        ],
        scratch_shapes=[
            dma((count,)),
            dma((count, shards - 1)),
            dma((count, shards - 1)),
            dma((count, chips - 1)),
            dma((count, chips - 1)),
            dma((count, chips)),
            dma((count, chips)),
        ],
        compiler_params=pltpu.CompilerParams(collective_id=0, has_side_effects=True),
        name="gather_weights",
    )(*mine)
    return [
        whole.reshape(item.shape[0] * shards, item.shape[1])
        for whole, item in zip(wholes, weights)
    ]


def scatter_kernel(chips, shards, spans, packed, out, own, k_land, c_land, z_land, *sems):
    local, k_send, k_recv, c_send, c_recv, z_send, z_recv = sems
    me, row = lax.axis_index("ctx"), lax.axis_index("fsdp")
    chip, core = me // 2, me % 2
    sibling = (chip * 2 + 1 - core, row)

    def above(step):
        return (me, lax.rem(row + step, shards))

    def across(step):
        return (lax.rem(chip + step, chips) * 2 + core, row)

    barrier = pltpu.get_barrier_semaphore()
    greeted = [above(d) for d in range(1, shards)] + [across(d) for d in range(1, chips)]
    greeted.append(sibling)
    for other in greeted:
        pl.semaphore_signal(barrier, inc=1, device_id=other, device_id_type=pl.DeviceIdType.MESH)
    pl.semaphore_wait(barrier, len(greeted))

    def send(src, dst, send_sem, recv_sem, target):
        copy = pltpu.make_async_remote_copy(
            src_ref=src,
            dst_ref=dst,
            send_sem=send_sem,
            recv_sem=recv_sem,
            device_id=target,
            device_id_type=pl.DeviceIdType.MESH,
        )
        copy.start()
        return copy

    order = list(range(1, chips)) + [0]
    kept, inside, between, along = {}, {}, {}, {}
    for i, span in enumerate(spans):
        rows = pl.ds(*span)
        for d in order:
            part = lax.rem(chip + d, chips)
            inside[i, d] = send(
                packed.at[part, 1 - core, :, rows],
                k_land.at[part, :, rows],
                k_send.at[i, d],
                k_recv.at[i, d],
                sibling,
            )
            kept[i, d] = pltpu.make_async_copy(
                packed.at[part, core, :, rows], own.at[part, :, rows], local.at[i, d]
            )
            kept[i, d].start()
    for i, span in enumerate(spans):
        rows = pl.ds(*span)
        for d in order:
            part = lax.rem(chip + d, chips)
            kept[i, d].wait()
            inside[i, d].wait_recv()

            @pl.loop(0, shards)
            def _(f):
                total = own[part, f, rows].astype(jnp.float32)
                total += k_land[part, f, rows].astype(jnp.float32)
                own[part, f, rows] = total.astype(jnp.bfloat16)

            if d:
                between[i, d] = send(
                    own.at[part, :, rows],
                    c_land.at[d - 1, :, rows],
                    c_send.at[i, d - 1],
                    c_recv.at[i, d - 1],
                    across(d),
                )
    for i, span in enumerate(spans):
        rows = pl.ds(*span)
        for d in range(1, chips):
            between[i, d].wait_recv()

        @pl.loop(0, shards)
        def _(f):
            total = own[chip, f, rows].astype(jnp.float32)
            for d in range(1, chips):
                total += c_land[d - 1, f, rows].astype(jnp.float32)
            own[chip, f, rows] = total.astype(jnp.bfloat16)

        for d in range(1, shards):
            along[i, d] = send(
                own.at[chip, lax.rem(row + d, shards), rows],
                z_land.at[d - 1, rows],
                z_send.at[i, d - 1],
                z_recv.at[i, d - 1],
                above(d),
            )
    for i, span in enumerate(spans):
        rows = pl.ds(*span)
        for d in range(1, shards):
            along[i, d].wait_recv()
        total = own[chip, row, rows].astype(jnp.float32)
        for d in range(1, shards):
            total += z_land[d - 1, rows].astype(jnp.float32)
        out[rows] = total
    for copies in (inside, between, along):
        for copy in copies.values():
            copy.wait_send()


def scatter_packed(packed):
    ctx_count, shards = lax.axis_size("ctx"), lax.axis_size("fsdp")
    _, rows, width = packed.shape
    if ctx_count != 8:
        return scatter(packed.reshape(-1, width)).astype(jnp.float32)
    chips = ctx_count // 2
    first = 16 * (-(-rows // 32))
    spans = ((0, first), (first, rows - first))
    dma = pltpu.SemaphoreType.DMA
    low = jnp.bfloat16
    return pl.pallas_call(
        partial(scatter_kernel, chips, shards, spans),
        in_specs=[pl.BlockSpec(memory_space=pl.ANY)],
        out_specs=pl.BlockSpec(memory_space=pltpu.VMEM),
        out_shape=jax.ShapeDtypeStruct((rows, width), jnp.float32),
        scratch_shapes=[
            pltpu.VMEM((chips, shards, rows, width), low),
            pltpu.VMEM((chips, shards, rows, width), low),
            pltpu.VMEM((chips - 1, shards, rows, width), low),
            pltpu.VMEM((shards - 1, rows, width), low),
            dma((2, chips)),
            dma((2, chips)),
            dma((2, chips)),
            dma((2, chips - 1)),
            dma((2, chips - 1)),
            dma((2, shards - 1)),
            dma((2, shards - 1)),
        ],
        compiler_params=pltpu.CompilerParams(
            collective_id=1, has_side_effects=True, vmem_limit_bytes=44 * 2**20
        ),
        name="sum_gradients",
    )(packed.reshape(chips, 2, shards, rows, width))


def all_positions(pair_table, ctx_count):
    column = jnp.arange(2 * BLK, dtype=jnp.int32)[None, :]
    pair = pair_table[:, None]
    lower = pair * BLK + column
    upper = (2 * ctx_count - 1 - pair) * BLK + column - BLK
    return jnp.where(column < BLK, lower, upper).reshape(-1)


def scatter(term):
    return lax.psum_scatter(term, ("ctx", "fsdp"), scatter_dimension=0, tiled=True)


class Spot:
    def __init__(self, shards):
        self.shards = shards
        self.me, self.row = lax.axis_index("ctx"), lax.axis_index("fsdp")
        chip, core = self.me // 2, self.me % 2
        y, x = chip // 2, chip % 2
        self.core = core
        self.a = (1 - core) * x + core * y
        self.b = (1 - core) * y + core * x
        self.first = self.index(1 - self.a, self.b)
        self.second = self.index(self.a, 1 - self.b)
        self.corner = self.index(1 - self.a, 1 - self.b)
        self.sibling = chip * 2 + 1 - core

    def chip_of(self, a, b):
        return (1 - self.core) * (2 * b + a) + self.core * (2 * a + b)

    def index(self, a, b):
        return self.chip_of(a, b) * 2 + self.core

    def near(self, ctx):
        return (ctx, self.row)

    def above(self, step):
        return (self.me, lax.rem(self.row + step, self.shards))

    def came(self, step):
        return lax.rem(self.row - step + self.shards, self.shards)

    def greet(self):
        barrier = pltpu.get_barrier_semaphore()
        others = [self.above(d) for d in range(1, self.shards)]
        others += [self.near(i) for i in (self.first, self.second, self.sibling)]
        for other in others:
            pl.semaphore_signal(
                barrier, inc=1, device_id=other, device_id_type=pl.DeviceIdType.MESH
            )
        pl.semaphore_wait(barrier, len(others))


def send(src, dst, send_sem, recv_sem, target):
    copy = pltpu.make_async_remote_copy(
        src_ref=src,
        dst_ref=dst,
        send_sem=send_sem,
        recv_sem=recv_sem,
        device_id=target,
        device_id_type=pl.DeviceIdType.MESH,
    )
    copy.start()
    return copy


class Gather:
    def __init__(self, spot, shard, whole, sems):
        self.spot, self.shard, self.whole, self.sems = spot, shard, whole, sems
        self.rows, columns = shard.shape
        self.half = columns // 2
        self.copies = {}

    def cols(self):
        return pl.ds(pl.multiple_of(self.spot.core * self.half, 128), self.half)

    def part(self, row, start, size):
        begin = pl.multiple_of(row * self.rows + start, 16)
        return self.whole.at[pl.ds(begin, size), self.cols()]

    def post(self, stage, d, src, dst, target):
        n = self.spot.shards - 1
        at = stage * n + d - 1
        self.copies[stage, d] = send(
            src, dst, self.sems[0].at[at], self.sems[1].at[at], target
        )

    def own(self):
        begin = pl.multiple_of(self.spot.row * self.rows, 16)
        copy = pltpu.make_async_copy(
            self.shard, self.whole.at[pl.ds(begin, self.rows)], self.sems[2]
        )
        copy.start()
        return copy

    def along(self):
        spot, quarter = self.spot, self.rows // 4
        start = (2 * spot.b + spot.a) * quarter
        src = self.shard.at[pl.ds(pl.multiple_of(start, 16), quarter), self.cols()]
        for d in range(1, spot.shards):
            self.post(0, d, src, self.part(spot.row, start, quarter), spot.above(d))

    def step_one(self):
        spot, quarter = self.spot, self.rows // 4
        start = (2 * spot.b + spot.a) * quarter
        for d in range(1, spot.shards):
            self.copies[0, d].wait_recv()
            ref = self.part(spot.came(d), start, quarter)
            self.post(1, d, ref, ref, spot.near(spot.first))

    def step_two(self):
        spot, half = self.spot, self.rows // 2
        for d in range(1, spot.shards):
            self.copies[1, d].wait_recv()
            ref = self.part(spot.came(d), spot.b * half, half)
            self.post(2, d, ref, ref, spot.near(spot.second))
            self.post(3, d, ref, ref, spot.near(spot.sibling))

    def step_three(self):
        spot, half = self.spot, self.rows // 2
        for d in range(1, spot.shards):
            self.copies[2, d].wait_recv()
            ref = self.part(spot.came(d), (1 - spot.b) * half, half)
            self.post(4, d, ref, ref, spot.near(spot.sibling))

    def finish(self):
        for d in range(1, self.spot.shards):
            self.copies[3, d].wait_recv()
            self.copies[4, d].wait_recv()

    def drain(self):
        for copy in self.copies.values():
            copy.wait_send()


class Exchange:
    def __init__(self, spot, whole, view, sems):
        self.spot, self.sems = spot, sems
        self.view = lambda device: view(whole, device)
        self.copies = {}

    def post(self, at, device, target):
        ref = self.view(device)
        self.copies[at] = send(
            ref, ref, self.sems[0].at[at], self.sems[1].at[at], self.spot.near(target)
        )

    def start(self):
        spot = self.spot
        self.post(0, spot.me, spot.first)
        self.post(1, spot.me, spot.second)
        self.post(2, spot.me, spot.sibling)

    def pass_on(self):
        spot = self.spot
        self.copies[0].wait_recv()
        self.post(3, spot.first, spot.second)
        self.post(4, spot.first, spot.sibling)

    def share(self):
        spot = self.spot
        self.copies[1].wait_recv()
        self.post(5, spot.second, spot.sibling)
        self.copies[3].wait_recv()
        self.post(6, spot.corner, spot.sibling)

    def finish(self):
        for at in (2, 4, 5, 6):
            self.copies[at].wait_recv()

    def drain(self):
        for copy in self.copies.values():
            copy.wait_send()


def front_kernel(
    shards,
    x_ref,
    gain_ref,
    shift_ref,
    qbias_ref,
    vbias_ref,
    qpos_ref,
    kpos_ref,
    qkv_shard,
    out_shard,
    fc_shard,
    proj_shard,
    first_ref,
    query_ref,
    attn_ref,
    lse_ref,
    kv_out,
    qkv_out,
    out_out,
    fc_out,
    proj_out,
    qkv_ref,
    kv_ref,
    *sems,
):
    spot = Spot(shards)
    spot.greet()
    weights = [
        Gather(spot, shard, whole, sems[3 * i : 3 * i + 3])
        for i, (shard, whole) in enumerate(
            (
                (qkv_shard, qkv_ref),
                (out_shard, out_out),
                (fc_shard, fc_out),
                (proj_shard, proj_out),
            )
        )
    ]
    key_sems, value_sems, keep_sem = sems[12:14], sems[14:16], sems[16]
    qkv, out, fc, proj = weights
    qkv.along()
    own = [item.own() for item in weights]
    normed, _ = normalize(x_ref[...].astype(jnp.float32))
    first_ref[...] = (normed * gain_ref[...] + shift_ref[...]).astype(jnp.bfloat16)
    qkv.step_one()
    out.along()
    fc.along()
    qkv.step_two()
    proj.along()
    qkv.step_three()
    own[0].wait()
    qkv.finish()
    width = x_ref.shape[1]

    def columns(start):
        def view(whole, device):
            return whole.at[device, :, pl.ds(start, width)]

        return view

    first_in = first_ref[...]
    keys = Exchange(spot, kv_ref, columns(0), key_sems)
    values = Exchange(spot, kv_ref, columns(width), value_sems)
    kv_ref[spot.me, :, pl.ds(0, width)] = dot_nn(
        first_in, qkv_ref[:, pl.ds(width, width)]
    ).astype(jnp.bfloat16)
    keys.start()
    kv_ref[spot.me, :, pl.ds(width, width)] = (
        dot_nn(first_in, qkv_ref[:, pl.ds(2 * width, width)]) + vbias_ref[...]
    ).astype(jnp.bfloat16)
    values.start()
    query_ref[...] = (
        (dot_nn(first_in, qkv_ref[:, pl.ds(0, width)]) + qbias_ref[...]).astype(jnp.bfloat16)
        * jnp.bfloat16(HEAD_DIM ** (-0.5))
    )
    keep_qkv = pltpu.make_async_copy(qkv_ref, qkv_out, keep_sem.at[0])
    keep_qkv.start()
    keys.pass_on()
    values.pass_on()
    out.step_one()
    fc.step_one()
    keys.share()
    values.share()
    out.step_two()
    proj.step_one()
    keys.finish()
    values.finish()
    keep_kv = pltpu.make_async_copy(kv_ref, kv_out, keep_sem.at[1])
    keep_kv.start()
    allowed = kpos_ref[...] <= qpos_ref[...]
    rows = x_ref.shape[0]
    total = kv_ref.shape[0] * rows

    def attend(h):
        lanes = pl.ds(pl.multiple_of(h * PAIR, PAIR), PAIR)
        value_lanes = pl.ds(pl.multiple_of(width + h * PAIR, PAIR), PAIR)
        query = query_ref[:, lanes]
        keys_all = kv_ref[:, :, lanes].reshape(total, PAIR)
        values_all = kv_ref[:, :, value_lanes].reshape(total, PAIR)
        mixed, stats = [], []
        for head in range(2):
            scores = jnp.where(allowed, dot_nt(head_only(query, head), keys_all), masked_score)
            most = jnp.max(scores, axis=-1, keepdims=True)
            expd = jnp.exp(scores - most)
            norm = jnp.sum(expd, axis=-1, keepdims=True)
            mixed.append(dot_nn(expd.astype(jnp.bfloat16), values_all) / norm)
            stats.append(most + jnp.log(norm))
        attn_ref[:, lanes] = head_pick(mixed[0], mixed[1])
        lse_ref[h] = jnp.concatenate(stats, axis=-1)

    pairs = width // PAIR
    fc.step_two()
    pl.loop(0, pairs // 2)(attend)
    out.step_three()
    proj.step_two()
    pl.loop(pairs // 2, pairs)(attend)
    fc.step_three()
    proj.step_three()
    for item in (out, fc, proj):
        item.finish()
    for copy in own[1:]:
        copy.wait()
    for item in (*weights, keys, values):
        item.drain()
    keep_qkv.wait()
    keep_kv.wait()


def front(layer_in, gain, shift, qbias, vbias, query_pos, key_pos, weights):
    shards, ctx_count = lax.axis_size("fsdp"), lax.axis_size("ctx")
    rows, width = layer_in.shape
    pairs = width // PAIR
    low, wide = jnp.bfloat16, jnp.float32
    dma = pltpu.SemaphoreType.DMA
    anywhere = pl.BlockSpec(memory_space=pl.ANY)
    inside = pl.BlockSpec(memory_space=pltpu.VMEM)
    whole = [jax.ShapeDtypeStruct((w.shape[0] * shards, w.shape[1]), low) for w in weights]
    kv_shape = (ctx_count, rows, 2 * width)
    gather_sems = [dma((5 * (shards - 1),)), dma((5 * (shards - 1),)), dma] * 4
    return pl.pallas_call(
        partial(front_kernel, shards),
        in_specs=[inside] * 7 + [anywhere] * 4,
        out_specs=[inside] * 4 + [anywhere] * 5,
        out_shape=[
            jax.ShapeDtypeStruct((rows, width), low),
            jax.ShapeDtypeStruct((rows, width), low),
            jax.ShapeDtypeStruct((rows, width), wide),
            jax.ShapeDtypeStruct((pairs, rows, 2), wide),
            jax.ShapeDtypeStruct(kv_shape, low),
        ]
        + whole,
        scratch_shapes=[
            pltpu.VMEM(whole[0].shape, low),
            pltpu.VMEM(kv_shape, low),
        ]
        + gather_sems
        + [dma((7,))] * 4
        + [dma((2,))],
        compiler_params=pltpu.CompilerParams(
            collective_id=0, has_side_effects=True, vmem_limit_bytes=48 * 2**20
        ),
        name="front",
    )(
        layer_in,
        gain[None, :],
        shift[None, :],
        qbias[None, :],
        vbias[None, :],
        query_pos[:, None],
        key_pos[None, :],
        *weights,
    )


class Unit:
    def __init__(self, spot, packed, lands, sems, store):
        self.spot, self.packed, self.sems, self.store = spot, packed, sems, store
        self.core_land, self.first_land, self.second_land, self.z_land = lands
        self.copies = {}

    def post(self, at, src, dst, target):
        self.copies[at] = send(src, dst, self.sems[0].at[at], self.sems[1].at[at], target)

    def stage(self, number):
        (self.cores, self.step_one, self.step_two, self.along, self.finish)[number]()

    def cores(self):
        spot = self.spot
        self.post(
            0, self.packed.at[:, 1 - spot.core], self.core_land, spot.near(spot.sibling)
        )

    def step_one(self):
        spot, land, packed = self.spot, self.core_land, self.packed
        self.copies[0].wait_recv()
        for k, b in enumerate((1 - spot.b, spot.b)):
            chip = spot.chip_of(1 - spot.a, b)
            land[chip] = land[chip] + packed[chip, spot.core]
            self.post(1 + k, land.at[chip], self.first_land.at[k], spot.near(spot.first))
        for b in (1 - spot.b, spot.b):
            chip = spot.chip_of(spot.a, b)
            land[chip] = land[chip] + packed[chip, spot.core]

    def step_two(self):
        spot, land = self.spot, self.first_land
        self.copies[1].wait_recv()
        land[0] = land[0] + self.core_land[spot.chip_of(spot.a, 1 - spot.b)]
        self.post(3, land.at[0], self.second_land, spot.near(spot.second))
        self.copies[2].wait_recv()
        land[1] = land[1] + self.core_land[spot.chip_of(spot.a, spot.b)]

    def along(self):
        spot, land = self.spot, self.second_land
        self.copies[3].wait_recv()
        land[...] = land[...] + self.first_land[1]
        for d in range(1, spot.shards):
            other = lax.rem(spot.row + d, spot.shards)
            self.post(3 + d, land.at[other], self.z_land.at[d - 1], spot.above(d))

    def finish(self):
        spot = self.spot
        total = self.second_land[spot.row].astype(jnp.float32)
        for d in range(1, spot.shards):
            self.copies[3 + d].wait_recv()
            total += self.z_land[d - 1].astype(jnp.float32)
        self.store(total)

    def drain(self):
        for at, copy in self.copies.items():
            if at:
                copy.wait_send()


def dot_tn(left, right):
    return lax.dot_general(
        left, right, (((0,), (0,)), ((), ())), preferred_element_type=jnp.float32
    )


PROJ_COLS, FC_COLS, TILE = 256, 1024, 256


def back_kernel(
    shards,
    x_ref,
    gain_ref,
    qpos_ref,
    kpos_ref,
    act_ref,
    d_result_ref,
    second_ref,
    d_pre_ref,
    attended_ref,
    d_branch_ref,
    d_middle_ref,
    first_ref,
    mlp_ref,
    stat_col_ref,
    query_in,
    d_out_in,
    stat_in,
    kv_in,
    qkv_in,
    grad_in_ref,
    g_qkv_ref,
    g_out_ref,
    g_fc_ref,
    g_proj_ref,
    vec_ref,
    kv_ref,
    qkv_ref,
    qd_ref,
    stat_ref,
    d_qkv_ref,
    vec_land,
    vec_part,
    proj_pack,
    fc_pack,
    mid_pack,
    *rest,
):
    spot = Spot(shards)
    rows, width = x_ref.shape
    pairs = width // PAIR
    load_sem, qd_send, qd_recv, st_send, st_recv, v_send, v_recv = rest[:7]
    rest = rest[7:]
    loads = [
        pltpu.make_async_copy(src, dst, load_sem.at[i])
        for i, (src, dst) in enumerate(
            (
                (query_in, qd_ref.at[spot.me, :, pl.ds(0, width)]),
                (d_out_in, qd_ref.at[spot.me, :, pl.ds(width, width)]),
                (stat_in, stat_ref.at[spot.me]),
                (kv_in, kv_ref),
                (qkv_in, qkv_ref),
            )
        )
    ]
    for copy in loads:
        copy.start()
    spot.greet()
    for copy in loads[:3]:
        copy.wait()
    stats = Exchange(spot, stat_ref, lambda whole, device: whole.at[device], (st_send, st_recv))
    payload = Exchange(spot, qd_ref, lambda whole, device: whole.at[device], (qd_send, qd_recv))
    payload.start()
    stats.start()

    units, makers = [], []
    packs = {"proj": proj_pack, "fc": fc_pack, "mid": mid_pack}
    used = {"proj": [], "fc": [], "mid": []}

    def make_proj(packed, n):
        def maker():
            right = d_result_ref[:, n * PROJ_COLS : (n + 1) * PROJ_COLS]

            @pl.loop(0, 4)
            def _(chip):
                share = act_ref.shape[1] // 4
                left = act_ref[:, pl.ds(pl.multiple_of(chip * share, 128), share)]
                block = dot_tn(left, right).reshape(packed.shape[1:])
                packed[chip] = block.astype(jnp.bfloat16)

        return maker

    def make_rows(packed, left_ref, right_ref, start, columns):
        def maker():
            left = left_ref[...]

            @pl.loop(0, columns // TILE)
            def _(n):
                right = right_ref[:, pl.ds(pl.multiple_of(start + n * TILE, 128), TILE)]
                block = dot_tn(left, right).reshape(packed.shape[:-1] + (TILE,))
                packed[..., pl.ds(pl.multiple_of(n * TILE, 128), TILE)] = block.astype(
                    jnp.bfloat16
                )

        return maker

    def add(kind, out_ref, n, columns, maker):
        nonlocal rest
        slot = len(used[kind]) % 2
        packed = packs[kind].at[slot]

        def store(total):
            out_ref[:, n * columns : (n + 1) * columns] = total

        unit = Unit(spot, packed, rest[:4], rest[4:6], store)
        rest = rest[6:]
        earlier = used[kind][-2] if len(used[kind]) >= 2 else None
        used[kind].append(unit)
        units.append(unit)
        make = maker(packed)

        def begin():
            if earlier is not None:
                earlier.copies[0].wait_send()
            make()

        makers.append(begin)

    for n in range(3):
        add("proj", g_proj_ref, n, PROJ_COLS, lambda p, n=n: make_proj(p, n))
    for n in range(3):
        add(
            "fc",
            g_fc_ref,
            n,
            FC_COLS,
            lambda p, n=n: make_rows(p, second_ref, d_pre_ref, n * FC_COLS, FC_COLS),
        )
    add("mid", g_out_ref, 0, width, lambda p: make_rows(p, attended_ref, d_branch_ref, 0, width))
    for n in range(3):
        add(
            "mid",
            g_qkv_ref,
            n,
            width,
            lambda p, n=n: make_rows(p, first_ref, d_qkv_ref, n * width, width),
        )

    def slot(number):
        if number < len(units):
            makers[number]()
            units[number].stage(0)
        for stage in range(4, 0, -1):
            if 0 <= number - stage < len(units):
                units[number - stage].stage(stage)

    count = kv_ref.shape[0]
    total = count * rows

    def query_pair(h):
        lanes = pl.ds(pl.multiple_of(h * PAIR, PAIR), PAIR)
        upper = pl.ds(pl.multiple_of(width + h * PAIR, PAIR), PAIR)
        allowed = kpos_ref[...] <= qpos_ref[...]
        query, d_out = qd_ref[spot.me, :, lanes], qd_ref[spot.me, :, upper]
        keys = kv_ref[:, :, lanes].reshape(total, PAIR)
        values = kv_ref[:, :, upper].reshape(total, PAIR)
        stat = stat_col_ref[h]
        parts = []
        for head in range(2):
            lse, delta = stat[:, head : head + 1], stat[:, head + 2 : head + 3]
            scores = jnp.where(allowed, dot_nt(head_only(query, head), keys), masked_score)
            prob = jnp.exp(scores - lse)
            d_prob = dot_nt(head_only(d_out, head), values)
            parts.append(dot_nn((prob * (d_prob - delta)).astype(jnp.bfloat16), keys))
        d_qkv_ref[:, lanes] = (head_pick(parts[0], parts[1]) * HEAD_DIM ** (-0.5)).astype(
            jnp.bfloat16
        )

    def key_pair(h):
        lanes = pl.ds(pl.multiple_of(h * PAIR, PAIR), PAIR)
        upper = pl.ds(pl.multiple_of(width + h * PAIR, PAIR), PAIR)
        last = pl.ds(pl.multiple_of(2 * width + h * PAIR, PAIR), PAIR)
        keys, values = kv_ref[spot.me, :, lanes], kv_ref[spot.me, :, upper]
        my_keys = [head_only(keys, head) for head in range(2)]
        my_values = [head_only(values, head) for head in range(2)]
        key_parts = [jnp.zeros((rows, PAIR), jnp.float32)] * 2
        value_parts = [jnp.zeros((rows, PAIR), jnp.float32)] * 2
        key_pos = qpos_ref[...]
        for chunk in range(2):
            part = pl.ds(chunk * count // 2, count // 2)
            span = total // 2
            query_pos = kpos_ref[:, chunk * span : (chunk + 1) * span]
            allowed = key_pos <= query_pos
            query = qd_ref[part, :, lanes].reshape(span, PAIR)
            d_out = qd_ref[part, :, upper].reshape(span, PAIR)
            for head in range(2):

                def line(index):
                    return jnp.concatenate(
                        [
                            stat_ref[chunk * count // 2 + i, pl.ds(index, 1), :]
                            for i in range(count // 2)
                        ],
                        axis=-1,
                    )

                lse, delta = line(4 * h + head), line(4 * h + 2 + head)
                scores = jnp.where(allowed, dot_nt(my_keys[head], query), masked_score)
                prob = jnp.exp(scores - lse)
                value_parts[head] = value_parts[head] + dot_nn(prob.astype(jnp.bfloat16), d_out)
                d_prob = dot_nt(my_values[head], d_out)
                d_score = (prob * (d_prob - delta)).astype(jnp.bfloat16)
                key_parts[head] = key_parts[head] + dot_nn(d_score, query)
        d_qkv_ref[:, upper] = head_pick(key_parts[0], key_parts[1]).astype(jnp.bfloat16)
        d_qkv_ref[:, last] = head_pick(value_parts[0], value_parts[1]).astype(jnp.bfloat16)

    slot(0)
    payload.pass_on()
    stats.pass_on()
    loads[3].wait()
    slot(1)
    pl.loop(0, 2)(query_pair)
    slot(2)
    pl.loop(2, 4)(query_pair)
    payload.share()
    stats.share()
    slot(3)
    pl.loop(4, pairs)(query_pair)
    slot(4)
    payload.finish()
    stats.finish()
    pl.loop(0, 2)(key_pair)
    slot(5)
    pl.loop(2, 4)(key_pair)
    slot(6)
    pl.loop(4, pairs)(key_pair)
    slot(7)
    slot(8)
    slot(9)
    loads[4].wait()
    d_qkv = d_qkv_ref[...]
    d_first = dot_nt(d_qkv, qkv_ref[...])
    normed, inverse = normalize(x_ref[...].astype(jnp.float32))
    d_norm, grad_gain, grad_shift = norm_back(d_first, normed, inverse, gain_ref[...])
    d_middle = d_middle_ref[...]
    grad_in_ref[...] = d_middle + d_norm

    def over_tokens(block):
        return jnp.sum(block.astype(jnp.float32), axis=0, keepdims=True)

    bias_fc = over_tokens(d_pre_ref[...])
    lines = [
        over_tokens(d_qkv[:, :width]),
        over_tokens(d_qkv[:, 2 * width :]),
        over_tokens(d_middle),
        over_tokens(d_result_ref[...]),
        grad_gain[None, :],
        grad_shift[None, :],
        mlp_ref[0:1],
        mlp_ref[1:2],
    ]
    lines += [bias_fc[:, i * width : (i + 1) * width] for i in range(bias_fc.shape[1] // width)]
    vec_part[0] = jnp.zeros_like(vec_part.at[0])
    for i, item in enumerate(lines):
        vec_part[0, i : i + 1] = item
    vec_copies = []
    for k, other in enumerate((spot.sibling, spot.first, spot.second)):
        copy = send(
            vec_part.at[k], vec_land.at[k], v_send.at[k], v_recv.at[k], spot.near(other)
        )
        vec_copies.append(copy)
        slot(10 + k)
        copy.wait_recv()
        vec_part[k + 1] = vec_part[k] + vec_land[k]
    for d in range(1, shards):
        vec_copies.append(
            send(
                vec_part.at[3],
                vec_land.at[2 + d],
                v_send.at[2 + d],
                v_recv.at[2 + d],
                spot.above(d),
            )
        )
    slot(13)
    summed = vec_part[3]
    for d in range(1, shards):
        vec_copies[2 + d].wait_recv()
        summed = summed + vec_land[2 + d]
    vec_ref[...] = summed
    for copy in vec_copies:
        copy.wait_send()
    for kind in used.values():
        for unit in kind[-2:]:
            unit.copies[0].wait_send()
    for unit in units:
        unit.drain()
    payload.drain()
    stats.drain()


def back(vmem_args, hbm_args):
    shards, ctx_count = lax.axis_size("fsdp"), lax.axis_size("ctx")
    rows, width = vmem_args[0].shape
    hidden = vmem_args[4].shape[1]
    low, wide = jnp.bfloat16, jnp.float32
    dma = pltpu.SemaphoreType.DMA
    chips = ctx_count // 2
    devices = ctx_count * shards
    shapes = (
        [(hidden // devices, PROJ_COLS)] * (width // PROJ_COLS)
        + [(width // devices, FC_COLS)] * (hidden // FC_COLS)
        + [(width // devices, width)] * 4
    )
    scratch = [
        pltpu.VMEM((ctx_count, rows, 2 * width), low),
        pltpu.VMEM((width, 3 * width), low),
        pltpu.VMEM((ctx_count, rows, 2 * width), low),
        pltpu.VMEM((ctx_count,) + hbm_args[2].shape, wide),
        pltpu.VMEM((rows, 3 * width), low),
        pltpu.VMEM((2 + shards, 16, width), wide),
        pltpu.VMEM((4, 16, width), wide),
    ]
    for shape in (shapes[0], shapes[width // PROJ_COLS], shapes[-1]):
        scratch.append(pltpu.VMEM((2, chips, 2, shards) + shape, low))
    scratch += [dma((5,)), dma((7,)), dma((7,)), dma((7,)), dma((7,))]
    scratch += [dma((2 + shards,)), dma((2 + shards,))]
    for shape in shapes:
        scratch += [
            pltpu.VMEM((chips, shards) + shape, low),
            pltpu.VMEM((2, shards) + shape, low),
            pltpu.VMEM((shards,) + shape, low),
            pltpu.VMEM((shards - 1,) + shape, low),
            dma((3 + shards,)),
            dma((3 + shards,)),
        ]
    inside = pl.BlockSpec(memory_space=pltpu.VMEM)
    anywhere = pl.BlockSpec(memory_space=pl.ANY)
    return pl.pallas_call(
        partial(back_kernel, shards),
        in_specs=[inside] * len(vmem_args) + [anywhere] * len(hbm_args),
        out_specs=[inside] * 6,
        out_shape=[
            jax.ShapeDtypeStruct((rows, width), wide),
            jax.ShapeDtypeStruct((width // devices, 3 * width), wide),
            jax.ShapeDtypeStruct((width // devices, width), wide),
            jax.ShapeDtypeStruct((width // devices, hidden), wide),
            jax.ShapeDtypeStruct((hidden // devices, width), wide),
            jax.ShapeDtypeStruct((16, width), wide),
        ],
        scratch_shapes=scratch,
        compiler_params=pltpu.CompilerParams(
            collective_id=1, has_side_effects=True, vmem_limit_bytes=58 * 2**20
        ),
        name="back",
    )(*vmem_args, *hbm_args)


def per_device(
    layer_in,
    qkv_weight,
    query_bias,
    value_bias,
    out_weight,
    out_bias,
    fc_weight,
    fc_bias,
    proj_weight,
    proj_bias,
    attn_norm_gain,
    attn_norm_shift,
    mlp_norm_gain,
    mlp_norm_shift,
    cotangent,
    pair_table,
):
    ctx_count = lax.axis_size("ctx")
    shards = ctx_count * lax.axis_size("fsdp")
    _, _, rows, width = layer_in.shape
    my_pos = block_positions(pair_table, lax.axis_index("ctx"), ctx_count)
    every_pos = all_positions(pair_table, ctx_count)
    flat_in = layer_in.reshape(rows, width).astype(jnp.float32)
    normed_one, inverse_one = normalize(flat_in)
    if ctx_count == 8:
        (
            first_in,
            query,
            attn_exact,
            lse,
            every_kv,
            full_qkv,
            full_out,
            full_fc,
            full_proj,
        ) = front(
            layer_in.reshape(rows, width),
            attn_norm_gain,
            attn_norm_shift,
            query_bias,
            value_bias,
            my_pos,
            every_pos,
            (qkv_weight, out_weight, fc_weight, proj_weight),
        )
    else:
        full_qkv, full_out, full_fc, full_proj = whole_weights(
            (qkv_weight, out_weight, fc_weight, proj_weight)
        )
        first_in = (normed_one * attn_norm_gain + attn_norm_shift).astype(jnp.bfloat16)
        keys_values = (
            jnp.dot(first_in, full_qkv[:, width:], preferred_element_type=jnp.float32)
            + jnp.concatenate([jnp.zeros_like(value_bias), value_bias])
        ).astype(jnp.bfloat16)
        every_kv = lax.all_gather(keys_values, "ctx", axis=0, tiled=True)
        query = (
            jnp.dot(first_in, full_qkv[:, :width], preferred_element_type=jnp.float32) + query_bias
        ).astype(jnp.bfloat16) * jnp.bfloat16(HEAD_DIM ** (-0.5))
        every_query = lax.all_gather(query, "ctx", axis=0, tiled=True)
        attn_exact, lse = forward_attention(my_pos, every_pos, query, every_kv)
    attended = attn_exact.astype(jnp.bfloat16)
    middle = flat_in + jnp.dot(attended, full_out, preferred_element_type=jnp.float32) + out_bias
    normed_two, inverse_two = normalize(middle)
    second_in = (normed_two * mlp_norm_gain + mlp_norm_shift).astype(jnp.bfloat16)
    pre_act = jnp.dot(second_in, full_fc, preferred_element_type=jnp.float32) + fc_bias
    activated, gelu_back = jax.vjp(partial(jax.nn.gelu, approximate=True), pre_act)
    act_low = activated.astype(jnp.bfloat16)
    result = middle + jnp.dot(act_low, full_proj, preferred_element_type=jnp.float32) + proj_bias
    layer_out = result.astype(jnp.bfloat16).reshape(layer_in.shape)
    d_result = cotangent.reshape(rows, width)
    d_act = jnp.einsum("td,fd->tf", d_result, full_proj, preferred_element_type=jnp.float32)
    (d_pre,) = gelu_back(d_act)
    d_pre_low = d_pre.astype(jnp.bfloat16)
    d_second = jnp.einsum("tf,df->td", d_pre_low, full_fc, preferred_element_type=jnp.float32)
    d_mid_norm, grad_mlp_gain, grad_mlp_shift = norm_back(
        d_second, normed_two, inverse_two, mlp_norm_gain
    )
    d_middle = d_result.astype(jnp.float32) + d_mid_norm
    d_branch = d_middle.astype(jnp.bfloat16)
    d_attended = jnp.einsum(
        "te,de->td", d_branch, full_out, preferred_element_type=jnp.float32
    ).astype(jnp.bfloat16)
    delta = jnp.sum(
        (d_attended.astype(jnp.float32) * attn_exact).reshape(rows, width // PAIR, 2, HEAD_DIM),
        axis=-1,
    )
    stats = jnp.concatenate([lse, jnp.transpose(delta, (1, 0, 2))], axis=-1)
    if ctx_count == 8:
        grad_in, sum_qkv, sum_out, sum_fc, sum_proj, sums = back(
            (
                layer_in.reshape(rows, width),
                attn_norm_gain[None, :],
                my_pos[:, None],
                every_pos[None, :],
                act_low,
                d_result,
                second_in,
                d_pre_low,
                attended,
                d_branch,
                d_middle,
                first_in,
                jnp.stack([grad_mlp_gain, grad_mlp_shift]),
                stats,
            ),
            (
                query,
                d_attended,
                jnp.transpose(stats, (0, 2, 1)).reshape(-1, rows),
                every_kv,
                full_qkv,
            ),
        )
        share = width // shards
        device = lax.axis_index("ctx") * lax.axis_size("fsdp") + lax.axis_index("fsdp")
        mine = lax.dynamic_slice_in_dim(sums, device * share, share, 1)
        fc_share = d_pre.shape[1] // shards
        fc_sum = lax.dynamic_slice_in_dim(sums[8:12].reshape(-1), device * fc_share, fc_share)
        return (
            layer_out,
            grad_in.reshape(layer_in.shape),
            sum_qkv,
            mine[0],
            mine[1],
            sum_out,
            mine[2],
            sum_fc,
            fc_sum,
            sum_proj,
            mine[3],
            mine[4],
            mine[5],
            mine[6],
            mine[7],
        )
    every_d_out = lax.all_gather(d_attended, "ctx", axis=0, tiled=True)
    every_stat = lax.all_gather(
        jnp.transpose(stats, (0, 2, 1)).reshape(-1, rows), "ctx", axis=1, tiled=True
    ).reshape(width // PAIR, 4, ctx_count * rows)
    grad_proj = jnp.einsum("tf,td->fd", act_low, d_result, preferred_element_type=jnp.float32)
    grad_fc = jnp.einsum("td,tf->df", second_in, d_pre_low, preferred_element_type=jnp.float32)
    grad_out = jnp.einsum("td,te->de", attended, d_branch, preferred_element_type=jnp.float32)
    d_query = query_gradient(my_pos, every_pos, query, d_attended, stats, every_kv)
    d_key, d_value = key_gradients(
        my_pos, every_pos, keys_values, every_query, every_d_out, every_stat
    )
    d_qkv = jnp.concatenate([d_query, d_key, d_value], axis=1).astype(jnp.bfloat16)
    grad_qkv = jnp.einsum("td,te->de", first_in, d_qkv, preferred_element_type=jnp.float32)
    d_first = jnp.einsum("te,de->td", d_qkv, full_qkv, preferred_element_type=jnp.float32)
    d_in_norm, grad_attn_gain, grad_attn_shift = norm_back(
        d_first, normed_one, inverse_one, attn_norm_gain
    )
    grad_in = (d_middle + d_in_norm).reshape(layer_in.shape)
    bias_sum = jnp.sum(d_qkv.astype(jnp.float32), axis=0)
    vectors = (
        bias_sum[:width],
        bias_sum[2 * width :],
        jnp.sum(d_middle, axis=0),
        jnp.sum(d_pre_low.astype(jnp.float32), axis=0),
        jnp.sum(d_result.astype(jnp.float32), axis=0),
        grad_attn_gain,
        grad_attn_shift,
        grad_mlp_gain,
        grad_mlp_shift,
    )
    small = jnp.concatenate([item.reshape(shards, -1) for item in vectors], axis=1)
    lines = 16 * -(-small.shape[1] // (16 * width))
    small = jnp.pad(small, ((0, 0), (0, lines * width - small.shape[1])))
    matrices = (
        [grad_qkv[:, i * width : (i + 1) * width] for i in range(3)]
        + [grad_out]
        + [grad_fc[:, i * width : (i + 1) * width] for i in range(grad_fc.shape[1] // width)]
        + [grad_proj, small.reshape(shards * lines, width)]
    )
    packed = jnp.concatenate(
        [item.astype(jnp.bfloat16).reshape(shards, -1, width) for item in matrices], axis=1
    )
    summed = scatter_packed(packed)
    pieces, start = [], 0
    for item in matrices:
        size = item.shape[0] // shards
        pieces.append(summed[start : start + size])
        start += size
    sum_qkv = jnp.concatenate(pieces[:3], axis=1)
    sum_out = pieces[3]
    sum_fc = jnp.concatenate(pieces[4:-2], axis=1)
    sum_proj = pieces[-2]
    sum_small = pieces[-1].reshape(-1)
    small, start = [], 0
    for item in vectors:
        size = item.shape[0] // shards
        small.append(sum_small[start : start + size])
        start += size
    return (
        layer_out,
        grad_in,
        sum_qkv,
        small[0],
        small[1],
        sum_out,
        small[2],
        sum_fc,
        small[3],
        sum_proj,
        small[4],
        small[5],
        small[6],
        small[7],
        small[8],
    )


def solution(mesh):
    return jax.shard_map(
        per_device,
        mesh=mesh,
        in_specs=(
            P("fsdp", "ctx", None, None),
            P("fsdp", None),
            P(),
            P(),
            P("fsdp", None),
            P(),
            P("fsdp", None),
            P(),
            P("fsdp", None),
            P(),
            P(),
            P(),
            P(),
            P(),
            P("fsdp", "ctx", None, None),
            P(),
        ),
        out_specs=(
            P("fsdp", "ctx", None, None),
            P("fsdp", "ctx", None, None),
            P(("ctx", "fsdp"), None),
            P(("ctx", "fsdp")),
            P(("ctx", "fsdp")),
            P(("ctx", "fsdp"), None),
            P(("ctx", "fsdp")),
            P(("ctx", "fsdp"), None),
            P(("ctx", "fsdp")),
            P(("ctx", "fsdp"), None),
            P(("ctx", "fsdp")),
            P(("ctx", "fsdp")),
            P(("ctx", "fsdp")),
            P(("ctx", "fsdp")),
            P(("ctx", "fsdp")),
        ),
        check_vma=False,
    )
```

```python
from functools import partial
from types import SimpleNamespace

import jax
import jax.numpy as jnp
from jax import lax
from jax.experimental import pallas as pl
from jax.experimental.pallas import tpu as pltpu
from jax.sharding import PartitionSpec as P

H = 12
HEAD_DIM = 64
BLK = 96


epsilon = 1e-05
masked_score = -1e30


def normalize(values):
    centered = values - jnp.mean(values, axis=-1, keepdims=True)
    inverse = lax.rsqrt(jnp.mean(centered * centered, axis=-1, keepdims=True) + epsilon)
    return (centered * inverse, inverse)


def norm_back(grad_out, normed, inverse, gain):
    scaled = grad_out * gain
    grad_input = inverse * (
        scaled
        - jnp.mean(scaled, axis=-1, keepdims=True)
        - normed * jnp.mean(scaled * normed, axis=-1, keepdims=True)
    )
    return (grad_input, jnp.sum(grad_out * normed, axis=0), jnp.sum(grad_out, axis=0))


def block_positions(pair_table, device, ctx_count):
    pair_index = lax.dynamic_index_in_dim(pair_table, device, 0, keepdims=False)
    column = jnp.arange(2 * BLK, dtype=jnp.int32)
    lower = pair_index * BLK + column
    upper = (2 * ctx_count - 1 - pair_index) * BLK + column - BLK
    return jnp.where(column < BLK, lower, upper)


PAIR = 2 * HEAD_DIM
CHUNK = 8 * 2 * BLK
NT = (((1,), (1,)), ((), ()))


def chunk_of(total):
    return CHUNK if total % CHUNK == 0 else total


def head_only(block, head):
    lane = lax.broadcasted_iota(jnp.int32, block.shape, 1)
    return jnp.where((lane // HEAD_DIM) == head, block, jnp.zeros_like(block))


def head_pick(first, second):
    lane = lax.broadcasted_iota(jnp.int32, first.shape, 1)
    return jnp.where(lane < HEAD_DIM, first, second)


def dot_nt(left, right):
    return lax.dot_general(left, right, NT, preferred_element_type=jnp.float32)


def dot_nn(left, right):
    return jnp.dot(left, right, preferred_element_type=jnp.float32)


def forward_kernel(qpos_ref, kpos_ref, q_ref, k_ref, v_ref, out_ref, lse_ref, max_ref, sum_ref):
    step = pl.program_id(1)
    last = pl.num_programs(1) - 1

    @pl.when(step == 0)
    def _():
        max_ref[...] = jnp.full_like(max_ref, masked_score)
        sum_ref[...] = jnp.zeros_like(sum_ref)
        out_ref[...] = jnp.zeros_like(out_ref)

    allowed = kpos_ref[...] <= qpos_ref[...]
    query, keys, values = q_ref[...], k_ref[...], v_ref[...]
    mixed, factors = [], []
    for head in range(2):
        scores = jnp.where(allowed, dot_nt(head_only(query, head), keys), masked_score)
        old_max = max_ref[head]
        new_max = jnp.maximum(old_max, jnp.max(scores, axis=-1, keepdims=True))
        expd = jnp.exp(scores - new_max)
        factor = jnp.exp(old_max - new_max)
        sum_ref[head] = sum_ref[head] * factor + jnp.sum(expd, axis=-1, keepdims=True)
        max_ref[head] = new_max
        mixed.append(dot_nn(expd.astype(jnp.bfloat16), values))
        factors.append(factor)
    rows = query.shape[0]
    scale = head_pick(*(jnp.broadcast_to(f, (rows, PAIR)) for f in factors))
    out_ref[...] = out_ref[...] * scale + head_pick(mixed[0], mixed[1])

    @pl.when(step == last)
    def _():
        total = head_pick(*(jnp.broadcast_to(sum_ref[h], (rows, PAIR)) for h in range(2)))
        out_ref[...] = out_ref[...] / total
        lse_ref[0] = jnp.concatenate(
            [max_ref[h] + jnp.log(sum_ref[h]) for h in range(2)], axis=-1
        )


def forward_attention(query_pos, key_pos, query, keys_values):
    rows, width = query.shape
    total = keys_values.shape[0]
    chunk = chunk_of(total)
    pairs = width // PAIR
    return pl.pallas_call(
        forward_kernel,
        grid=(pairs, total // chunk),
        in_specs=[
            pl.BlockSpec((rows, 1), lambda h, c: (0, 0)),
            pl.BlockSpec((1, chunk), lambda h, c: (0, c)),
            pl.BlockSpec((rows, PAIR), lambda h, c: (0, h)),
            pl.BlockSpec((chunk, PAIR), lambda h, c: (c, h)),
            pl.BlockSpec((chunk, PAIR), lambda h, c: (c, h + pairs)),
        ],
        out_specs=[
            pl.BlockSpec((rows, PAIR), lambda h, c: (0, h)),
            pl.BlockSpec((1, rows, 2), lambda h, c: (h, 0, 0)),
        ],
        out_shape=[
            jax.ShapeDtypeStruct((rows, width), jnp.float32),
            jax.ShapeDtypeStruct((pairs, rows, 2), jnp.float32),
        ],
        scratch_shapes=[
            pltpu.VMEM((2, rows, 1), jnp.float32),
            pltpu.VMEM((2, rows, 1), jnp.float32),
        ],
        compiler_params=pltpu.CompilerParams(vmem_limit_bytes=40 * 2**20),
        cost_estimate=pl.CostEstimate(
            flops=8 * rows * total * width,
            bytes_accessed=4 * total * width,
            transcendentals=rows * total * H,
        ),
        name="attention_forward",
    )(query_pos[:, None], key_pos[None, :], query, keys_values, keys_values)


def query_kernel(qpos_ref, kpos_ref, q_ref, do_ref, stat_ref, k_ref, v_ref, dq_ref):
    @pl.when(pl.program_id(1) == 0)
    def _():
        dq_ref[...] = jnp.zeros_like(dq_ref)

    allowed = kpos_ref[...] <= qpos_ref[...]
    query, d_out, keys, values = q_ref[...], do_ref[...], k_ref[...], v_ref[...]
    parts = []
    for head in range(2):
        lse = stat_ref[0, :, head : head + 1]
        delta = stat_ref[0, :, head + 2 : head + 3]
        scores = jnp.where(allowed, dot_nt(head_only(query, head), keys), masked_score)
        prob = jnp.exp(scores - lse)
        d_prob = dot_nt(head_only(d_out, head), values)
        d_score = (prob * (d_prob - delta)).astype(jnp.bfloat16)
        parts.append(dot_nn(d_score, keys))
    dq_ref[...] += head_pick(parts[0], parts[1]) * HEAD_DIM ** (-0.5)


def query_gradient(query_pos, key_pos, query, d_out, stats, keys_values):
    rows, width = query.shape
    total = keys_values.shape[0]
    chunk = chunk_of(total)
    pairs = width // PAIR
    return pl.pallas_call(
        query_kernel,
        grid=(pairs, total // chunk),
        in_specs=[
            pl.BlockSpec((rows, 1), lambda h, c: (0, 0)),
            pl.BlockSpec((1, chunk), lambda h, c: (0, c)),
            pl.BlockSpec((rows, PAIR), lambda h, c: (0, h)),
            pl.BlockSpec((rows, PAIR), lambda h, c: (0, h)),
            pl.BlockSpec((1, rows, 4), lambda h, c: (h, 0, 0)),
            pl.BlockSpec((chunk, PAIR), lambda h, c: (c, h)),
            pl.BlockSpec((chunk, PAIR), lambda h, c: (c, h + pairs)),
        ],
        out_specs=pl.BlockSpec((rows, PAIR), lambda h, c: (0, h)),
        out_shape=jax.ShapeDtypeStruct((rows, width), jnp.float32),
        compiler_params=pltpu.CompilerParams(vmem_limit_bytes=40 * 2**20),
        cost_estimate=pl.CostEstimate(
            flops=12 * rows * total * width,
            bytes_accessed=4 * total * width,
            transcendentals=rows * total * H,
        ),
        name="attention_query_gradient",
    )(query_pos[:, None], key_pos[None, :], query, d_out, stats, keys_values, keys_values)


def key_kernel(kpos_ref, qpos_ref, k_ref, v_ref, q_ref, do_ref, stat_ref, dk_ref, dv_ref):
    @pl.when(pl.program_id(1) == 0)
    def _():
        dk_ref[...] = jnp.zeros_like(dk_ref)
        dv_ref[...] = jnp.zeros_like(dv_ref)

    allowed = kpos_ref[...] <= qpos_ref[...]
    keys, values, query, d_out = k_ref[...], v_ref[...], q_ref[...], do_ref[...]
    key_parts, value_parts = [], []
    for head in range(2):
        lse = stat_ref[0, head : head + 1, :]
        delta = stat_ref[0, head + 2 : head + 3, :]
        scores = jnp.where(allowed, dot_nt(head_only(keys, head), query), masked_score)
        prob = jnp.exp(scores - lse)
        value_parts.append(dot_nn(prob.astype(jnp.bfloat16), d_out))
        d_prob = dot_nt(head_only(values, head), d_out)
        d_score = (prob * (d_prob - delta)).astype(jnp.bfloat16)
        key_parts.append(dot_nn(d_score, query))
    dk_ref[...] += head_pick(key_parts[0], key_parts[1])
    dv_ref[...] += head_pick(value_parts[0], value_parts[1])


def key_gradients(key_pos, query_pos, qkv, query_all, d_out_all, stats_all):
    rows = qkv.shape[0]
    total, width = query_all.shape
    chunk = chunk_of(total)
    pairs = width // PAIR
    grad_spec = pl.BlockSpec((rows, PAIR), lambda h, c: (0, h))
    return pl.pallas_call(
        key_kernel,
        grid=(pairs, total // chunk),
        in_specs=[
            pl.BlockSpec((rows, 1), lambda h, c: (0, 0)),
            pl.BlockSpec((1, chunk), lambda h, c: (0, c)),
            pl.BlockSpec((rows, PAIR), lambda h, c: (0, h)),
            pl.BlockSpec((rows, PAIR), lambda h, c: (0, h + pairs)),
            pl.BlockSpec((chunk, PAIR), lambda h, c: (c, h)),
            pl.BlockSpec((chunk, PAIR), lambda h, c: (c, h)),
            pl.BlockSpec((1, 4, chunk), lambda h, c: (h, 0, c)),
        ],
        out_specs=[grad_spec, grad_spec],
        out_shape=[jax.ShapeDtypeStruct((rows, width), jnp.float32)] * 2,
        compiler_params=pltpu.CompilerParams(vmem_limit_bytes=40 * 2**20),
        cost_estimate=pl.CostEstimate(
            flops=16 * rows * total * width,
            bytes_accessed=4 * total * width,
            transcendentals=rows * total * H,
        ),
        name="attention_key_gradients",
    )(key_pos[:, None], query_pos[None, :], qkv, qkv, query_all, d_out_all, stats_all)


def whole_weight(weight):
    share = weight.shape[0] // lax.axis_size("ctx")
    mine = lax.dynamic_slice_in_dim(weight, lax.axis_index("ctx") * share, share, 0)
    return lax.all_gather(mine, ("fsdp", "ctx"), axis=0, tiled=True)


def gather_kernel(chips, shards, count, *refs):
    shares, wholes = refs[:count], refs[count : 2 * count]
    own_sem, z_send, z_recv, c_send, c_recv, k_send, k_recv = refs[2 * count :]
    me, row = lax.axis_index("ctx"), lax.axis_index("fsdp")
    chip, core = me // 2, me % 2
    sibling = (chip * 2 + 1 - core, row)

    def above(step):
        return (me, lax.rem(row + step, shards))

    def across(step):
        return (lax.rem(chip + step, chips) * 2 + core, row)

    barrier = pltpu.get_barrier_semaphore()
    greeted = [above(d) for d in range(1, shards)] + [across(d) for d in range(1, chips)]
    greeted.append(sibling)
    for other in greeted:
        pl.semaphore_signal(barrier, inc=1, device_id=other, device_id_type=pl.DeviceIdType.MESH)
    pl.semaphore_wait(barrier, len(greeted))

    def send(src, dst, send_sem, recv_sem, target):
        copy = pltpu.make_async_remote_copy(
            src_ref=src,
            dst_ref=dst,
            send_sem=send_sem,
            recv_sem=recv_sem,
            device_id=target,
            device_id_type=pl.DeviceIdType.MESH,
        )
        copy.start()
        return copy

    def column(item, index):
        return wholes[item].at[:, index]

    own, along, between, inside = {}, {}, {}, {}
    for i in range(count):
        own[i] = pltpu.make_async_copy(shares[i], wholes[i].at[row, me], own_sem.at[i])
        own[i].start()
        for d in range(1, shards):
            along[i, d] = send(
                shares[i],
                wholes[i].at[row, me],
                z_send.at[i, d - 1],
                z_recv.at[i, d - 1],
                above(d),
            )
    for i in range(count):
        own[i].wait()
        for d in range(1, shards):
            along[i, d].wait_recv()
        for d in range(1, chips):
            mine = column(i, me)
            between[i, d] = send(mine, mine, c_send.at[i, d - 1], c_recv.at[i, d - 1], across(d))
        inside[i, 0] = send(
            column(i, me), column(i, me), k_send.at[i, 0], k_recv.at[i, 0], sibling
        )
    for i in range(count):
        for d in range(1, chips):
            between[i, d].wait_recv()
            came = column(i, lax.rem(chip - d + chips, chips) * 2 + core)
            inside[i, d] = send(came, came, k_send.at[i, d], k_recv.at[i, d], sibling)
    for copy in inside.values():
        copy.wait_recv()
    for copies in (along, between, inside):
        for copy in copies.values():
            copy.wait_send()


def whole_weights(weights):
    ctx_count, shards = lax.axis_size("ctx"), lax.axis_size("fsdp")
    chips = ctx_count // 2
    if ctx_count != 8:
        return [whole_weight(item) for item in weights]
    count = len(weights)
    mine = []
    for item in weights:
        share = item.shape[0] // ctx_count
        mine.append(
            lax.dynamic_slice_in_dim(item, lax.axis_index("ctx") * share, share, 0)
        )
    anywhere = pl.BlockSpec(memory_space=pl.ANY)
    dma = pltpu.SemaphoreType.DMA
    wholes = pl.pallas_call(
        partial(gather_kernel, chips, shards, count),
        in_specs=[anywhere] * count,
        out_specs=[anywhere] * count,
        out_shape=[
            jax.ShapeDtypeStruct((shards, ctx_count) + item.shape, item.dtype) for item in mine
        ],
        scratch_shapes=[
            dma((count,)),
            dma((count, shards - 1)),
            dma((count, shards - 1)),
            dma((count, chips - 1)),
            dma((count, chips - 1)),
            dma((count, chips)),
            dma((count, chips)),
        ],
        compiler_params=pltpu.CompilerParams(collective_id=0, has_side_effects=True),
        name="gather_weights",
    )(*mine)
    return [
        whole.reshape(item.shape[0] * shards, item.shape[1])
        for whole, item in zip(wholes, weights)
    ]


def scatter_kernel(chips, shards, spans, packed, out, own, k_land, c_land, z_land, *sems):
    local, k_send, k_recv, c_send, c_recv, z_send, z_recv = sems
    me, row = lax.axis_index("ctx"), lax.axis_index("fsdp")
    chip, core = me // 2, me % 2
    sibling = (chip * 2 + 1 - core, row)

    def above(step):
        return (me, lax.rem(row + step, shards))

    def across(step):
        return (lax.rem(chip + step, chips) * 2 + core, row)

    barrier = pltpu.get_barrier_semaphore()
    greeted = [above(d) for d in range(1, shards)] + [across(d) for d in range(1, chips)]
    greeted.append(sibling)
    for other in greeted:
        pl.semaphore_signal(barrier, inc=1, device_id=other, device_id_type=pl.DeviceIdType.MESH)
    pl.semaphore_wait(barrier, len(greeted))

    def send(src, dst, send_sem, recv_sem, target):
        copy = pltpu.make_async_remote_copy(
            src_ref=src,
            dst_ref=dst,
            send_sem=send_sem,
            recv_sem=recv_sem,
            device_id=target,
            device_id_type=pl.DeviceIdType.MESH,
        )
        copy.start()
        return copy

    order = list(range(1, chips)) + [0]
    kept, inside, between, along = {}, {}, {}, {}
    for i, span in enumerate(spans):
        rows = pl.ds(*span)
        for d in order:
            part = lax.rem(chip + d, chips)
            inside[i, d] = send(
                packed.at[part, 1 - core, :, rows],
                k_land.at[part, :, rows],
                k_send.at[i, d],
                k_recv.at[i, d],
                sibling,
            )
            kept[i, d] = pltpu.make_async_copy(
                packed.at[part, core, :, rows], own.at[part, :, rows], local.at[i, d]
            )
            kept[i, d].start()
    for i, span in enumerate(spans):
        rows = pl.ds(*span)
        for d in order:
            part = lax.rem(chip + d, chips)
            kept[i, d].wait()
            inside[i, d].wait_recv()

            @pl.loop(0, shards)
            def _(f):
                total = own[part, f, rows].astype(jnp.float32)
                total += k_land[part, f, rows].astype(jnp.float32)
                own[part, f, rows] = total.astype(jnp.bfloat16)

            if d:
                between[i, d] = send(
                    own.at[part, :, rows],
                    c_land.at[d - 1, :, rows],
                    c_send.at[i, d - 1],
                    c_recv.at[i, d - 1],
                    across(d),
                )
    for i, span in enumerate(spans):
        rows = pl.ds(*span)
        for d in range(1, chips):
            between[i, d].wait_recv()

        @pl.loop(0, shards)
        def _(f):
            total = own[chip, f, rows].astype(jnp.float32)
            for d in range(1, chips):
                total += c_land[d - 1, f, rows].astype(jnp.float32)
            own[chip, f, rows] = total.astype(jnp.bfloat16)

        for d in range(1, shards):
            along[i, d] = send(
                own.at[chip, lax.rem(row + d, shards), rows],
                z_land.at[d - 1, rows],
                z_send.at[i, d - 1],
                z_recv.at[i, d - 1],
                above(d),
            )
    for i, span in enumerate(spans):
        rows = pl.ds(*span)
        for d in range(1, shards):
            along[i, d].wait_recv()
        total = own[chip, row, rows].astype(jnp.float32)
        for d in range(1, shards):
            total += z_land[d - 1, rows].astype(jnp.float32)
        out[rows] = total
    for copies in (inside, between, along):
        for copy in copies.values():
            copy.wait_send()


def scatter_packed(packed):
    ctx_count, shards = lax.axis_size("ctx"), lax.axis_size("fsdp")
    _, rows, width = packed.shape
    if ctx_count != 8:
        return scatter(packed.reshape(-1, width)).astype(jnp.float32)
    chips = ctx_count // 2
    first = 16 * (-(-rows // 32))
    spans = ((0, first), (first, rows - first))
    dma = pltpu.SemaphoreType.DMA
    low = jnp.bfloat16
    return pl.pallas_call(
        partial(scatter_kernel, chips, shards, spans),
        in_specs=[pl.BlockSpec(memory_space=pl.ANY)],
        out_specs=pl.BlockSpec(memory_space=pltpu.VMEM),
        out_shape=jax.ShapeDtypeStruct((rows, width), jnp.float32),
        scratch_shapes=[
            pltpu.VMEM((chips, shards, rows, width), low),
            pltpu.VMEM((chips, shards, rows, width), low),
            pltpu.VMEM((chips - 1, shards, rows, width), low),
            pltpu.VMEM((shards - 1, rows, width), low),
            dma((2, chips)),
            dma((2, chips)),
            dma((2, chips)),
            dma((2, chips - 1)),
            dma((2, chips - 1)),
            dma((2, shards - 1)),
            dma((2, shards - 1)),
        ],
        compiler_params=pltpu.CompilerParams(
            collective_id=1, has_side_effects=True, vmem_limit_bytes=44 * 2**20
        ),
        name="sum_gradients",
    )(packed.reshape(chips, 2, shards, rows, width))


def all_positions(pair_table, ctx_count):
    column = jnp.arange(2 * BLK, dtype=jnp.int32)[None, :]
    pair = pair_table[:, None]
    lower = pair * BLK + column
    upper = (2 * ctx_count - 1 - pair) * BLK + column - BLK
    return jnp.where(column < BLK, lower, upper).reshape(-1)


def scatter(term):
    return lax.psum_scatter(term, ("ctx", "fsdp"), scatter_dimension=0, tiled=True)


class Spot:
    def __init__(self, shards):
        self.shards = shards
        self.me, self.row = lax.axis_index("ctx"), lax.axis_index("fsdp")
        chip, core = self.me // 2, self.me % 2
        y, x = chip // 2, chip % 2
        self.core = core
        self.a = (1 - core) * x + core * y
        self.b = (1 - core) * y + core * x
        self.first = self.index(1 - self.a, self.b)
        self.second = self.index(self.a, 1 - self.b)
        self.corner = self.index(1 - self.a, 1 - self.b)
        self.sibling = chip * 2 + 1 - core

    def chip_of(self, a, b):
        return (1 - self.core) * (2 * b + a) + self.core * (2 * a + b)

    def index(self, a, b):
        return self.chip_of(a, b) * 2 + self.core

    def near(self, ctx):
        return (ctx, self.row)

    def above(self, step):
        return (self.me, lax.rem(self.row + step, self.shards))

    def came(self, step):
        return lax.rem(self.row - step + self.shards, self.shards)

    def greet(self):
        barrier = pltpu.get_barrier_semaphore()
        others = [self.above(d) for d in range(1, self.shards)]
        others += [self.near(i) for i in (self.first, self.second, self.sibling)]
        for other in others:
            pl.semaphore_signal(
                barrier, inc=1, device_id=other, device_id_type=pl.DeviceIdType.MESH
            )
        pl.semaphore_wait(barrier, len(others))


def send(src, dst, send_sem, recv_sem, target):
    copy = pltpu.make_async_remote_copy(
        src_ref=src,
        dst_ref=dst,
        send_sem=send_sem,
        recv_sem=recv_sem,
        device_id=target,
        device_id_type=pl.DeviceIdType.MESH,
    )
    copy.start()
    return copy


class Gather:
    def __init__(self, spot, shard, whole, begin, columns, direct, sems):
        self.spot, self.shard, self.whole, self.sems = spot, shard, whole, sems
        self.direct = direct
        self.rows, self.begin, self.half = shard.shape[0], begin, columns // 2
        self.copies = {}

    def cols(self):
        return pl.ds(pl.multiple_of(self.begin + self.spot.core * self.half, 128), self.half)

    def part(self, row, start, size):
        begin = pl.multiple_of(row * self.rows + start, 16)
        return self.whole.at[pl.ds(begin, size), self.cols()]

    def post(self, stage, d, src, dst, target):
        at = stage * (self.spot.shards - 1) + d - 1
        self.copies[stage, d] = send(
            src, dst, self.sems[0].at[at], self.sems[1].at[at], target
        )

    def along(self):
        spot, quarter = self.spot, self.rows // 4
        start = (2 * spot.b + spot.a) * quarter
        if self.direct:
            quarter, start = self.rows, 0
        src = self.shard.at[pl.ds(pl.multiple_of(start, 16), quarter), self.cols()]
        for d in range(1, spot.shards):
            self.post(0, d, src, self.part(spot.row, start, quarter), spot.above(d))

    def step_one(self):
        spot, quarter = self.spot, self.rows // 4
        if self.direct:
            return
        start = (2 * spot.b + spot.a) * quarter
        for d in range(1, spot.shards):
            self.copies[0, d].wait_recv()
            ref = self.part(spot.came(d), start, quarter)
            self.post(1, d, ref, ref, spot.near(spot.first))

    def step_two(self):
        spot, half = self.spot, self.rows // 2
        if self.direct:
            return
        for d in range(1, spot.shards):
            self.copies[1, d].wait_recv()
            ref = self.part(spot.came(d), spot.b * half, half)
            self.post(2, d, ref, ref, spot.near(spot.second))
            self.post(3, d, ref, ref, spot.near(spot.sibling))

    def step_three(self, d):
        spot, half = self.spot, self.rows // 2
        if self.direct:
            self.copies[0, d].wait_recv()
            ref = self.part(spot.came(d), 0, self.rows)
            self.post(4, d, ref, ref, spot.near(spot.sibling))
            return
        self.copies[2, d].wait_recv()
        ref = self.part(spot.came(d), (1 - spot.b) * half, half)
        self.post(4, d, ref, ref, spot.near(spot.sibling))

    def finish(self, d):
        if not self.direct:
            self.copies[3, d].wait_recv()
        self.copies[4, d].wait_recv()

    def complete(self):
        for d in range(1, self.spot.shards):
            self.step_three(d)
        for d in range(1, self.spot.shards):
            self.finish(d)

    def drain(self):
        for copy in self.copies.values():
            copy.wait_send()


class Exchange:
    def __init__(self, spot, view, sems):
        self.spot, self.sems, self.view = spot, sems, view
        self.copies = {}

    def post(self, at, device, target):
        ref = self.view(device)
        self.copies[at] = send(
            ref, ref, self.sems[0].at[at], self.sems[1].at[at], self.spot.near(target)
        )

    def start(self):
        spot = self.spot
        self.post(0, spot.me, spot.first)
        self.post(1, spot.me, spot.second)
        self.post(2, spot.me, spot.sibling)

    def pass_on(self):
        spot = self.spot
        self.copies[0].wait_recv()
        self.post(3, spot.first, spot.second)
        self.post(4, spot.first, spot.sibling)

    def share(self):
        spot = self.spot
        self.copies[1].wait_recv()
        self.post(5, spot.second, spot.sibling)
        self.copies[3].wait_recv()
        self.post(6, spot.corner, spot.sibling)

    def finish(self):
        for at in (2, 4, 5, 6):
            self.copies[at].wait_recv()

    def drain(self):
        for copy in self.copies.values():
            copy.wait_send()


class Unit:
    def __init__(self, spot, packed, lands, sems, store):
        self.spot, self.packed, self.sems, self.store = spot, packed, sems, store
        self.core_land, self.first_land, self.second_land, self.z_land = lands
        self.copies = {}

    def post(self, at, src, dst, target):
        self.copies[at] = send(src, dst, self.sems[0].at[at], self.sems[1].at[at], target)

    def cores(self):
        spot = self.spot
        self.post(
            0, self.packed.at[:, 1 - spot.core], self.core_land, spot.near(spot.sibling)
        )

    def step_one(self):
        spot, land, packed = self.spot, self.core_land, self.packed
        self.copies[0].wait_recv()
        for k, b in enumerate((1 - spot.b, spot.b)):
            chip = spot.chip_of(1 - spot.a, b)
            land[chip] = land[chip] + packed[chip, spot.core]
            self.post(1 + k, land.at[chip], self.first_land.at[k], spot.near(spot.first))
        for b in (1 - spot.b, spot.b):
            chip = spot.chip_of(spot.a, b)
            land[chip] = land[chip] + packed[chip, spot.core]

    def step_two(self):
        spot, land = self.spot, self.first_land
        self.copies[1].wait_recv()
        land[0] = land[0] + self.core_land[spot.chip_of(spot.a, 1 - spot.b)]
        self.post(3, land.at[0], self.second_land, spot.near(spot.second))
        self.copies[2].wait_recv()
        land[1] = land[1] + self.core_land[spot.chip_of(spot.a, spot.b)]

    def along(self):
        spot, land = self.spot, self.second_land
        self.copies[3].wait_recv()
        land[...] = land[...] + self.first_land[1]
        for d in range(1, spot.shards):
            other = lax.rem(spot.row + d, spot.shards)
            self.post(3 + d, land.at[other], self.z_land.at[d - 1], spot.above(d))

    def finish(self):
        spot = self.spot
        total = self.second_land[spot.row].astype(jnp.float32)
        for d in range(1, spot.shards):
            self.copies[3 + d].wait_recv()
            total += self.z_land[d - 1].astype(jnp.float32)
        self.store(total)

    def drain(self):
        for at, copy in self.copies.items():
            if at:
                copy.wait_send()


class UnitAlongFirst(Unit):
    def step_one(self):
        spot, land, packed = self.spot, self.core_land, self.packed
        self.copies[0].wait_recv()
        for chip in range(land.shape[0]):
            land[chip] = land[chip] + packed[chip, spot.core]
        for d in range(1, spot.shards):
            other = lax.rem(spot.row + d, spot.shards)
            self.post(d, land.at[:, other], self.z_land.at[d - 1], spot.above(d))

    def step_two(self):
        spot, land, low = self.spot, self.z_land, self.z_land.dtype
        for d in range(1, spot.shards):
            self.copies[d].wait_recv()

        def add(chip):
            total = self.core_land[chip, spot.row].astype(jnp.float32)
            for d in range(1, spot.shards):
                total += land[d - 1, chip].astype(jnp.float32)
            land[0, chip] = total.astype(low)

        for k, b in enumerate((1 - spot.b, spot.b)):
            chip = spot.chip_of(1 - spot.a, b)
            add(chip)
            at = spot.shards + k
            self.post(at, land.at[0, chip], self.first_land.at[k], spot.near(spot.first))
        for b in (1 - spot.b, spot.b):
            add(spot.chip_of(spot.a, b))

    def along(self):
        spot, land, at = self.spot, self.first_land, self.spot.shards
        self.copies[at].wait_recv()
        land[0] = land[0] + self.z_land[0, spot.chip_of(spot.a, 1 - spot.b)]
        self.post(at + 2, land.at[0], self.second_land, spot.near(spot.second))

    def finish(self):
        spot, at = self.spot, self.spot.shards
        total = self.z_land[0, spot.chip_of(spot.a, spot.b)].astype(jnp.float32)
        self.copies[at + 1].wait_recv()
        total += self.first_land[1].astype(jnp.float32)
        self.copies[at + 2].wait_recv()
        self.store(total + self.second_land[...].astype(jnp.float32))


def dot_tn(left, right):
    return lax.dot_general(
        left, right, (((0,), (0,)), ((), ())), preferred_element_type=jnp.float32
    )


def gelu_pair(u):
    inner = 0.7978845608028654
    cubic = 0.044715
    square = u * u
    bend = jnp.tanh(inner * (u + cubic * (u * square)))
    half = 0.5 * (1.0 + bend)
    slope = half + 0.5 * u * (1.0 - bend * bend) * (inner * (1.0 + 3.0 * cubic * square))
    return u * half, slope


PROJ_COLS, TILE = 256, 256
DELAYS = (0, 1, 3, 4, 5)
DELAYS_ALONG = (0, 1, 5, 6, 7)
ALONG_FIRST = (0, 1)
DIRECT = ()


def layer_kernel(shards, names, *refs):
    r = SimpleNamespace(**dict(zip(names, refs)))
    landings = refs[len(names) :]
    spot = Spot(shards)
    rows, width = r.x.shape
    low = jnp.bfloat16
    pairs = width // PAIR
    kv, qd, stat = r.kv, r.qd, r.stat
    count = kv.shape[0]
    total = count * rows
    own = []
    shards_here = (r.qkv_shard, r.out_shard, r.fc_shard, r.proj_shard)
    for i, (shard, whole) in enumerate(zip(shards_here, (r.qkv, r.out, r.fc, r.proj))):
        size = shard.shape[0]
        begin = pl.multiple_of(spot.row * size, 16)
        own.append(
            pltpu.make_async_copy(shard, whole.at[pl.ds(begin, size)], r.own_sem.at[i])
        )
        own[-1].start()
    spot.greet()

    def gather(shard, whole, number, begin, columns):
        sems = r.gather_send.at[number], r.gather_recv.at[number]
        return Gather(spot, shard, whole, begin, columns, number in DIRECT, sems)

    hidden = r.fc.shape[1]
    w_kv = gather(r.qkv_shard, r.qkv, 0, width, 2 * width)
    w_q = gather(r.qkv_shard, r.qkv, 1, 0, width)
    w_out = gather(r.out_shard, r.out, 2, 0, width)
    w_fc = gather(r.fc_shard, r.fc, 3, 0, hidden)
    w_proj = gather(r.proj_shard, r.proj, 4, 0, width)

    def exchange(number, view):
        return Exchange(spot, view, (r.ex_send.at[number], r.ex_recv.at[number]))

    def columns_of(ref, start):
        return lambda device: ref.at[device, :, pl.ds(start, width)]

    x_keys = exchange(0, columns_of(kv, 0))
    x_values = exchange(1, columns_of(kv, width))
    x_query = exchange(2, columns_of(qd, 0))
    x_d_out = exchange(3, columns_of(qd, width))
    x_stat = exchange(4, lambda device: stat.at[device])

    def vector(ref):
        return ref[...].reshape(1, -1)

    w_kv.along()
    w_q.along()
    table = r.table

    def spread(position, pair):
        lower = pair * BLK + position
        upper = (2 * count - 1 - pair) * BLK + position - BLK
        return jnp.where(position < BLK, lower, upper)

    r.qpos[...] = spread(
        lax.broadcasted_iota(jnp.int32, (rows, 1), 0), table[spot.me]
    )
    lane = lax.broadcasted_iota(jnp.int32, (1, total), 1)
    key_pos = jnp.zeros((1, total), jnp.int32)
    for device in range(count):
        local = lane - device * rows
        key_pos = jnp.where(
            (local >= 0) & (local < rows), spread(local, table[device]), key_pos
        )
    r.kpos[...] = key_pos
    normed, _ = normalize(r.x[...].astype(jnp.float32))
    r.first[...] = (normed * vector(r.attn_gain) + vector(r.attn_shift)).astype(low)
    first_in = r.first[...]
    w_kv.step_one()
    w_out.along()
    w_fc.along()
    w_kv.step_two()
    w_q.step_one()
    own[0].wait()
    w_kv.complete()
    kv[spot.me, :, pl.ds(0, width)] = dot_nn(
        first_in, r.qkv[:, pl.ds(width, width)]
    ).astype(low)
    x_keys.start()
    kv[spot.me, :, pl.ds(width, width)] = (
        dot_nn(first_in, r.qkv[:, pl.ds(2 * width, width)]) + vector(r.value_bias)
    ).astype(low)
    x_values.start()
    w_proj.along()
    w_q.step_two()
    x_keys.pass_on()
    w_out.step_one()
    x_values.pass_on()
    w_q.complete()
    qd[spot.me, :, pl.ds(0, width)] = (
        (dot_nn(first_in, r.qkv[:, pl.ds(0, width)]) + vector(r.query_bias)).astype(low)
        * jnp.bfloat16(HEAD_DIM ** (-0.5))
    )
    w_out.step_two()
    w_fc.step_one()
    x_keys.share()
    x_values.share()
    w_proj.step_one()
    w_fc.step_two()
    x_keys.finish()
    x_values.finish()

    stat_lane = lax.broadcasted_iota(jnp.int32, r.stat_mine.shape, 1)

    def put_stat(index, column):
        r.stat_mine[...] = jnp.where(stat_lane == index, column, r.stat_mine[...])

    def take_stat(index):
        return jnp.sum(
            jnp.where(stat_lane == index, r.stat_mine[...], 0.0), axis=-1, keepdims=True
        )

    r.stat_mine[...] = jnp.zeros_like(r.stat_mine)

    def lanes_of(h, start=0):
        return pl.ds(pl.multiple_of(start + h * PAIR, PAIR), PAIR)

    def attend(h):
        allowed = r.kpos[...] <= r.qpos[...]
        query = qd[spot.me, :, lanes_of(h)]
        keys = kv[:, :, lanes_of(h)].reshape(total, PAIR)
        values = kv[:, :, lanes_of(h, width)].reshape(total, PAIR)
        mixed = []
        for head in range(2):
            scores = jnp.where(allowed, dot_nt(head_only(query, head), keys), masked_score)
            most = jnp.max(scores, axis=-1, keepdims=True)
            expd = jnp.exp(scores - most)
            norm = jnp.sum(expd, axis=-1, keepdims=True)
            mixed.append(dot_nn(expd.astype(low), values) / norm)
            put_stat(4 * h + head, most + jnp.log(norm))
        r.attn[:, lanes_of(h)] = head_pick(mixed[0], mixed[1])

    pl.loop(0, 2)(attend)
    w_out.complete()
    w_proj.step_two()
    pl.loop(2, 4)(attend)
    x_query.start()
    pl.loop(4, pairs)(attend)
    own[1].wait()
    attended = r.attn[...].astype(low)
    middle = r.x[...].astype(jnp.float32) + dot_nn(attended, r.out[...]) + vector(r.out_bias)
    r.middle[...] = middle
    normed, _ = normalize(middle)
    r.second[...] = (normed * vector(r.mlp_gain) + vector(r.mlp_shift)).astype(low)
    r.fc_line[...] = vector(r.fc_bias)
    own[2].wait()
    w_fc.complete()
    own[3].wait()
    piece = hidden // shards
    for d in range(shards):
        if d:
            w_proj.finish(d)
        n = spot.came(d)
        lanes = pl.ds(pl.multiple_of(n * piece, 128), piece)
        share = pl.ds(pl.multiple_of(n * piece, 16), piece)
        pre = dot_nn(r.second[...], r.fc[:, lanes]) + r.fc_line[:, lanes]
        activated, slope = gelu_pair(pre)
        activated = activated.astype(low)
        r.act[:, lanes] = activated
        result = dot_nn(activated, r.proj[share])
        d_act = dot_nt(r.cot[...], r.proj[share])
        d_pre = (d_act * slope).astype(low)
        r.d_pre[:, lanes] = d_pre
        d_second = dot_nt(d_pre, r.fc[:, lanes])
        if d:
            r.result[...] += result
            r.d_second[...] += d_second
        else:
            r.result[...] = result
            r.d_second[...] = d_second
            for k in range(1, shards):
                w_proj.step_three(k)
            x_query.pass_on()

    units, makers = [], []
    used = ([], [])

    def make_proj(packed, n):
        right = r.cot[:, n * PROJ_COLS : (n + 1) * PROJ_COLS]

        @pl.loop(0, 4)
        def _(chip):
            share = hidden // 4
            left = r.act[:, pl.ds(pl.multiple_of(chip * share, 128), share)]
            packed[chip] = dot_tn(left, right).reshape(packed.shape[1:]).astype(low)

    def make_rows(packed, left_ref, right_ref, start):
        left = left_ref[...]

        @pl.loop(0, width // TILE)
        def _(n):
            right = right_ref[:, pl.ds(pl.multiple_of(start + n * TILE, 128), TILE)]
            block = dot_tn(left, right).reshape(packed.shape[:-1] + (TILE,))
            packed[..., pl.ds(pl.multiple_of(n * TILE, 128), TILE)] = block.astype(low)

    def add(kind, out_ref, start, columns, make):
        packs = (r.mid_pack, r.proj_pack)[kind]
        slots = packs.shape[0]
        packed = packs.at[len(used[kind]) % slots]
        number = len(units)

        def store(total):
            out_ref[:, start : start + columns] = total

        lands = landings[4 * number : 4 * number + 4]
        sems = r.unit_send.at[number], r.unit_recv.at[number]
        kind_of = UnitAlongFirst if number in ALONG_FIRST else Unit
        unit = kind_of(spot, packed, lands, sems, store)
        earlier = used[kind][-slots] if len(used[kind]) >= slots else None
        used[kind].append(unit)
        units.append(unit)

        def begin():
            if earlier is not None:
                earlier.copies[0].wait_send()
            make(packed)
            unit.cores()

        makers.append(begin)

    for n in range(hidden // width):
        add(0, r.g_fc, n * width, width, lambda p, n=n: make_rows(p, r.second, r.d_pre, n * width))
    for n in range(width // PROJ_COLS):
        add(1, r.g_proj, n * PROJ_COLS, PROJ_COLS, lambda p, n=n: make_proj(p, n))
    add(0, r.g_out, 0, width, lambda p: make_rows(p, r.attended, r.d_branch, 0))
    for n in range(3):
        add(0, r.g_qkv, n * width, width, lambda p, n=n: make_rows(p, r.first, r.d_qkv, n * width))

    def slot(number):
        if number < len(units):
            makers[number]()
        for stage in range(1, 5):
            for i, unit in enumerate(units):
                delays = DELAYS_ALONG if i in ALONG_FIRST else DELAYS
                if number - i == delays[stage]:
                    (unit.step_one, unit.step_two, unit.along, unit.finish)[stage - 1]()

    slot(0)
    middle = r.middle[...]
    r.layer_out[...] = (middle + r.result[...] + vector(r.proj_bias)).astype(low)
    normed, inverse = normalize(middle)
    d_norm, grad_mlp_gain, grad_mlp_shift = norm_back(
        r.d_second[...], normed, inverse, vector(r.mlp_gain)
    )
    d_middle = r.cot[...].astype(jnp.float32) + d_norm
    r.d_middle[...] = d_middle
    d_branch = d_middle.astype(low)
    r.d_branch[...] = d_branch
    d_attended = dot_nt(d_branch, r.out[...]).astype(low)
    qd[spot.me, :, pl.ds(width, width)] = d_attended
    x_d_out.start()
    r.attended[...] = r.attn[...].astype(low)

    def deltas(h):
        d_out = qd[spot.me, :, lanes_of(h, width)].astype(jnp.float32)
        both = d_out * r.attn[:, lanes_of(h)]
        for head in range(2):
            put_stat(4 * h + 2 + head, jnp.sum(head_only(both, head), axis=-1, keepdims=True))

    pl.loop(0, pairs)(deltas)
    stat[spot.me] = jnp.transpose(r.stat_mine[...])[: stat.shape[1]]
    x_stat.start()
    x_query.share()
    slot(1)
    x_d_out.pass_on()
    x_stat.pass_on()

    def query_pair(h):
        allowed = r.kpos[...] <= r.qpos[...]
        query, d_out = qd[spot.me, :, lanes_of(h)], qd[spot.me, :, lanes_of(h, width)]
        keys = kv[:, :, lanes_of(h)].reshape(total, PAIR)
        values = kv[:, :, lanes_of(h, width)].reshape(total, PAIR)
        parts = []
        for head in range(2):
            lse, delta = take_stat(4 * h + head), take_stat(4 * h + 2 + head)
            scores = jnp.where(allowed, dot_nt(head_only(query, head), keys), masked_score)
            prob = jnp.exp(scores - lse)
            d_prob = dot_nt(head_only(d_out, head), values)
            parts.append(dot_nn((prob * (d_prob - delta)).astype(low), keys))
        d_query = head_pick(parts[0], parts[1]) * HEAD_DIM ** (-0.5)
        r.d_qkv[:, lanes_of(h)] = d_query.astype(low)

    def key_pair(h):
        keys, values = kv[spot.me, :, lanes_of(h)], kv[spot.me, :, lanes_of(h, width)]
        my_keys = [head_only(keys, head) for head in range(2)]
        my_values = [head_only(values, head) for head in range(2)]
        key_parts = [jnp.zeros((rows, PAIR), jnp.float32)] * 2
        value_parts = [jnp.zeros((rows, PAIR), jnp.float32)] * 2
        half = count // 2
        span = half * rows
        for chunk in range(2):
            part = pl.ds(chunk * half, half)
            allowed = r.qpos[...] <= r.kpos[:, chunk * span : (chunk + 1) * span]
            query = qd[part, :, lanes_of(h)].reshape(span, PAIR)
            d_out = qd[part, :, lanes_of(h, width)].reshape(span, PAIR)

            def line(index):
                parts = [stat[chunk * half + i, pl.ds(index, 1), :] for i in range(half)]
                return jnp.concatenate(parts, axis=-1)

            for head in range(2):
                lse, delta = line(4 * h + head), line(4 * h + 2 + head)
                scores = jnp.where(allowed, dot_nt(my_keys[head], query), masked_score)
                prob = jnp.exp(scores - lse)
                value_parts[head] = value_parts[head] + dot_nn(prob.astype(low), d_out)
                d_prob = dot_nt(my_values[head], d_out)
                d_score = (prob * (d_prob - delta)).astype(low)
                key_parts[head] = key_parts[head] + dot_nn(d_score, query)
        r.d_qkv[:, lanes_of(h, width)] = head_pick(*key_parts).astype(low)
        r.d_qkv[:, lanes_of(h, 2 * width)] = head_pick(*value_parts).astype(low)

    slot(2)
    pl.loop(0, 2)(query_pair)
    x_d_out.share()
    x_stat.share()
    slot(3)
    pl.loop(2, 4)(query_pair)
    slot(4)
    pl.loop(4, pairs)(query_pair)
    x_query.finish()
    x_d_out.finish()
    x_stat.finish()
    slot(5)
    pl.loop(0, 2)(key_pair)
    slot(6)
    pl.loop(2, 4)(key_pair)
    slot(7)
    pl.loop(4, pairs)(key_pair)
    for number in range(8, 11):
        slot(number)
    d_qkv = r.d_qkv[...]
    d_first = dot_nt(d_qkv, r.qkv[...])
    normed, inverse = normalize(r.x[...].astype(jnp.float32))
    d_norm, grad_gain, grad_shift = norm_back(d_first, normed, inverse, vector(r.attn_gain))
    d_middle = r.d_middle[...]
    r.grad_in[...] = d_middle + d_norm

    def over_tokens(block):
        return jnp.sum(block.astype(jnp.float32), axis=0, keepdims=True)

    bias_fc = over_tokens(r.d_pre[...])
    lines = [
        over_tokens(d_qkv[:, :width]),
        over_tokens(d_qkv[:, 2 * width :]),
        over_tokens(d_middle),
        over_tokens(r.cot[...]),
        grad_gain.reshape(1, -1),
        grad_shift.reshape(1, -1),
        grad_mlp_gain.reshape(1, -1),
        grad_mlp_shift.reshape(1, -1),
    ]
    lines += [bias_fc[:, i * width : (i + 1) * width] for i in range(hidden // width)]
    vec_land, vec_part = r.vec_land, r.vec_part
    vec_part[0] = jnp.zeros(vec_part.shape[1:], jnp.float32)
    for i, item in enumerate(lines):
        vec_part[0, i : i + 1] = item
    vec_copies = []

    def vec_post(k, src, target):
        copy = send(src, vec_land.at[k], r.vec_send.at[k], r.vec_recv.at[k], target)
        vec_copies.append(copy)
        return copy

    for k, other in enumerate((spot.sibling, spot.first, spot.second)):
        copy = vec_post(k, vec_part.at[k], spot.near(other))
        slot(len(units) + k)
        copy.wait_recv()
        vec_part[k + 1] = vec_part[k] + vec_land[k]
    for d in range(1, shards):
        vec_post(2 + d, vec_part.at[3], spot.above(d))
    for number in range(len(units) + 3, len(units) + DELAYS[-1]):
        slot(number)
    summed = vec_part[3]
    for d in range(1, shards):
        vec_copies[2 + d].wait_recv()
        summed = summed + vec_land[2 + d]
    r.sums[...] = summed
    for copy in vec_copies:
        copy.wait_send()
    for kind, packs in zip(used, (r.mid_pack, r.proj_pack)):
        for unit in kind[-packs.shape[0] :]:
            unit.copies[0].wait_send()
    for item in units + [w_kv, w_q, w_out, w_fc, w_proj]:
        item.drain()
    for item in (x_keys, x_values, x_query, x_d_out, x_stat):
        item.drain()


def whole_layer(**inputs):
    shards, ctx_count = lax.axis_size("fsdp"), lax.axis_size("ctx")
    rows, width = inputs.get("x").shape
    hidden = inputs.get("fc_shard").shape[1]
    low, wide = jnp.bfloat16, jnp.float32
    dma = pltpu.SemaphoreType.DMA
    chips, devices = ctx_count // 2, ctx_count * shards
    mid = (width // devices, width)
    tall = (hidden // devices, PROJ_COLS)
    shapes = [mid] * (hidden // width) + [tall] * (width // PROJ_COLS) + [mid] * 4
    vmem = pltpu.VMEM
    scratch = dict(
        qkv=vmem((width, 3 * width), low),
        out=vmem((width, width), low),
        fc=vmem((width, hidden), low),
        proj=vmem((hidden, width), low),
        kv=vmem((ctx_count, rows, 2 * width), low),
        qd=vmem((ctx_count, rows, 2 * width), low),
        stat=vmem((ctx_count, 4 * width // PAIR, rows), wide),
        stat_mine=vmem((rows, 128), wide),
        qpos=vmem((rows, 1), jnp.int32),
        kpos=vmem((1, ctx_count * rows), jnp.int32),
        first=vmem((rows, width), low),
        attn=vmem((rows, width), wide),
        attended=vmem((rows, width), low),
        middle=vmem((rows, width), wide),
        second=vmem((rows, width), low),
        fc_line=vmem((1, hidden), wide),
        act=vmem((rows, hidden), low),
        d_pre=vmem((rows, hidden), low),
        result=vmem((rows, width), wide),
        d_second=vmem((rows, width), wide),
        d_middle=vmem((rows, width), wide),
        d_branch=vmem((rows, width), low),
        d_qkv=vmem((rows, 3 * width), low),
        vec_land=vmem((2 + shards, 16, width), wide),
        vec_part=vmem((4, 16, width), wide),
        mid_pack=vmem((3, chips, 2, shards) + mid, low),
        proj_pack=vmem((2, chips, 2, shards) + tall, low),
        own_sem=dma((4,)),
        gather_send=dma((5, 5 * (shards - 1))),
        gather_recv=dma((5, 5 * (shards - 1))),
        ex_send=dma((5, 7)),
        ex_recv=dma((5, 7)),
        unit_send=dma((len(shapes), 3 + shards)),
        unit_recv=dma((len(shapes), 3 + shards)),
        vec_send=dma((2 + shards,)),
        vec_recv=dma((2 + shards,)),
    )
    landings = []
    for i, shape in enumerate(shapes):
        if i in ALONG_FIRST:
            landings += [
                vmem((chips, shards) + shape, low),
                vmem((2,) + shape, low),
                vmem(shape, low),
                vmem((shards - 1, chips) + shape, low),
            ]
            continue
        landings += [
            vmem((chips, shards) + shape, low),
            vmem((2, shards) + shape, low),
            vmem((shards,) + shape, low),
            vmem((shards - 1,) + shape, low),
        ]
    outputs = dict(
        layer_out=jax.ShapeDtypeStruct((rows, width), low),
        grad_in=jax.ShapeDtypeStruct((rows, width), wide),
        g_qkv=jax.ShapeDtypeStruct((width // devices, 3 * width), wide),
        g_out=jax.ShapeDtypeStruct((width // devices, width), wide),
        g_fc=jax.ShapeDtypeStruct((width // devices, hidden), wide),
        g_proj=jax.ShapeDtypeStruct((hidden // devices, width), wide),
        sums=jax.ShapeDtypeStruct((16, width), wide),
    )
    inside = pl.BlockSpec(memory_space=pltpu.VMEM)
    anywhere = pl.BlockSpec(memory_space=pl.ANY)
    return pl.pallas_call(
        partial(layer_kernel, shards, (*inputs, *outputs, *scratch)),
        in_specs=[pl.BlockSpec(memory_space=pltpu.SMEM)]
        + [inside] * (len(inputs) - 5)
        + [anywhere] * 4,
        out_specs=[inside] * len(outputs),
        out_shape=list(outputs.values()),
        scratch_shapes=list(scratch.values()) + landings,
        compiler_params=pltpu.CompilerParams(
            collective_id=0, has_side_effects=True, vmem_limit_bytes=VMEM_LIMIT
        ),
        name="whole",
    )(*inputs.values())


VMEM_LIMIT = 62 * 2**20


def finish_kernel(*refs):
    ins, outs = refs[:7], refs[7:]
    for src, dst in zip(ins[:6], outs[:6]):
        dst[...] = src[...]
    sums, small = ins[6], outs[6:]
    shards = lax.axis_size("fsdp")
    devices = lax.axis_size("ctx") * shards
    device = lax.axis_index("ctx") * shards + lax.axis_index("fsdp")
    width = sums.shape[1]

    def piece(rows, start, size):
        return pltpu.roll(rows, lax.rem(width - start, width), 1)[:, :size]

    share = width // devices
    lines = piece(sums[0:8], device * share, share)
    for i in range(8):
        small[i][...] = lines[i : i + 1]
    share = small[8].shape[1]
    fit = width // share
    line = sums[pl.ds(8 + device // fit, 1), :]
    eight = jnp.broadcast_to(line, (8, width))
    small[8][...] = piece(eight, lax.rem(device, fit) * share, share)[0:1]


def device_slices(*parts, shape):
    devices = lax.axis_size("ctx") * lax.axis_size("fsdp")
    width = parts[6].shape[1]
    inside = pl.BlockSpec(memory_space=pltpu.VMEM)
    shares = [width // devices] * 8 + [parts[4].shape[1] // devices]
    outs = pl.pallas_call(
        finish_kernel,
        in_specs=[inside] * 7,
        out_specs=[inside] * 15,
        out_shape=[jax.ShapeDtypeStruct(p.shape, p.dtype) for p in parts[:6]]
        + [jax.ShapeDtypeStruct((1, share), jnp.float32) for share in shares],
        name="finish",
    )(*parts)
    layer_out, grad_in, g_qkv, g_out, g_fc, g_proj = outs[:6]
    small = [item.reshape(-1) for item in outs[6:]]
    return (
        layer_out.reshape(shape),
        grad_in.reshape(shape),
        g_qkv,
        small[0],
        small[1],
        g_out,
        small[2],
        g_fc,
        small[8],
        g_proj,
        *small[3:8],
    )


def per_device(
    layer_in,
    qkv_weight,
    query_bias,
    value_bias,
    out_weight,
    out_bias,
    fc_weight,
    fc_bias,
    proj_weight,
    proj_bias,
    attn_norm_gain,
    attn_norm_shift,
    mlp_norm_gain,
    mlp_norm_shift,
    cotangent,
    pair_table,
):
    ctx_count = lax.axis_size("ctx")
    shards = ctx_count * lax.axis_size("fsdp")
    _, _, rows, width = layer_in.shape
    if ctx_count == 8:
        outs = whole_layer(
            table=pair_table,
            x=layer_in.reshape(rows, width),
            cot=cotangent.reshape(rows, width),
            attn_gain=attn_norm_gain,
            attn_shift=attn_norm_shift,
            mlp_gain=mlp_norm_gain,
            mlp_shift=mlp_norm_shift,
            query_bias=query_bias,
            value_bias=value_bias,
            out_bias=out_bias,
            proj_bias=proj_bias,
            fc_bias=fc_bias,
            qkv_shard=qkv_weight,
            out_shard=out_weight,
            fc_shard=fc_weight,
            proj_shard=proj_weight,
        )
        return device_slices(*outs, shape=layer_in.shape)
    my_pos = block_positions(pair_table, lax.axis_index("ctx"), ctx_count)
    every_pos = all_positions(pair_table, ctx_count)
    flat_in = layer_in.reshape(rows, width).astype(jnp.float32)
    full_qkv, full_out, full_fc, full_proj = whole_weights(
        (qkv_weight, out_weight, fc_weight, proj_weight)
    )
    normed_one, inverse_one = normalize(flat_in)
    first_in = (normed_one * attn_norm_gain + attn_norm_shift).astype(jnp.bfloat16)
    keys_values = (
        jnp.dot(first_in, full_qkv[:, width:], preferred_element_type=jnp.float32)
        + jnp.concatenate([jnp.zeros_like(value_bias), value_bias])
    ).astype(jnp.bfloat16)
    every_kv = lax.all_gather(keys_values, "ctx", axis=0, tiled=True)
    query = (
        jnp.dot(first_in, full_qkv[:, :width], preferred_element_type=jnp.float32) + query_bias
    ).astype(jnp.bfloat16) * jnp.bfloat16(HEAD_DIM ** (-0.5))
    every_query = lax.all_gather(query, "ctx", axis=0, tiled=True)
    attn_exact, lse = forward_attention(my_pos, every_pos, query, every_kv)
    attended = attn_exact.astype(jnp.bfloat16)
    middle = flat_in + jnp.dot(attended, full_out, preferred_element_type=jnp.float32) + out_bias
    normed_two, inverse_two = normalize(middle)
    second_in = (normed_two * mlp_norm_gain + mlp_norm_shift).astype(jnp.bfloat16)
    pre_act = jnp.dot(second_in, full_fc, preferred_element_type=jnp.float32) + fc_bias
    activated, gelu_back = jax.vjp(partial(jax.nn.gelu, approximate=True), pre_act)
    act_low = activated.astype(jnp.bfloat16)
    result = middle + jnp.dot(act_low, full_proj, preferred_element_type=jnp.float32) + proj_bias
    layer_out = result.astype(jnp.bfloat16).reshape(layer_in.shape)
    d_result = cotangent.reshape(rows, width)
    d_act = jnp.einsum("td,fd->tf", d_result, full_proj, preferred_element_type=jnp.float32)
    (d_pre,) = gelu_back(d_act)
    d_pre_low = d_pre.astype(jnp.bfloat16)
    d_second = jnp.einsum("tf,df->td", d_pre_low, full_fc, preferred_element_type=jnp.float32)
    d_mid_norm, grad_mlp_gain, grad_mlp_shift = norm_back(
        d_second, normed_two, inverse_two, mlp_norm_gain
    )
    d_middle = d_result.astype(jnp.float32) + d_mid_norm
    d_branch = d_middle.astype(jnp.bfloat16)
    d_attended = jnp.einsum(
        "te,de->td", d_branch, full_out, preferred_element_type=jnp.float32
    ).astype(jnp.bfloat16)
    delta = jnp.sum(
        (d_attended.astype(jnp.float32) * attn_exact).reshape(rows, width // PAIR, 2, HEAD_DIM),
        axis=-1,
    )
    stats = jnp.concatenate([lse, jnp.transpose(delta, (1, 0, 2))], axis=-1)
    every_d_out = lax.all_gather(d_attended, "ctx", axis=0, tiled=True)
    every_stat = lax.all_gather(
        jnp.transpose(stats, (0, 2, 1)).reshape(-1, rows), "ctx", axis=1, tiled=True
    ).reshape(width // PAIR, 4, ctx_count * rows)
    grad_proj = jnp.einsum("tf,td->fd", act_low, d_result, preferred_element_type=jnp.float32)
    grad_fc = jnp.einsum("td,tf->df", second_in, d_pre_low, preferred_element_type=jnp.float32)
    grad_out = jnp.einsum("td,te->de", attended, d_branch, preferred_element_type=jnp.float32)
    d_query = query_gradient(my_pos, every_pos, query, d_attended, stats, every_kv)
    d_key, d_value = key_gradients(
        my_pos, every_pos, keys_values, every_query, every_d_out, every_stat
    )
    d_qkv = jnp.concatenate([d_query, d_key, d_value], axis=1).astype(jnp.bfloat16)
    grad_qkv = jnp.einsum("td,te->de", first_in, d_qkv, preferred_element_type=jnp.float32)
    d_first = jnp.einsum("te,de->td", d_qkv, full_qkv, preferred_element_type=jnp.float32)
    d_in_norm, grad_attn_gain, grad_attn_shift = norm_back(
        d_first, normed_one, inverse_one, attn_norm_gain
    )
    grad_in = (d_middle + d_in_norm).reshape(layer_in.shape)
    bias_sum = jnp.sum(d_qkv.astype(jnp.float32), axis=0)
    vectors = (
        bias_sum[:width],
        bias_sum[2 * width :],
        jnp.sum(d_middle, axis=0),
        jnp.sum(d_pre_low.astype(jnp.float32), axis=0),
        jnp.sum(d_result.astype(jnp.float32), axis=0),
        grad_attn_gain,
        grad_attn_shift,
        grad_mlp_gain,
        grad_mlp_shift,
    )
    small = jnp.concatenate([item.reshape(shards, -1) for item in vectors], axis=1)
    lines = 16 * -(-small.shape[1] // (16 * width))
    small = jnp.pad(small, ((0, 0), (0, lines * width - small.shape[1])))
    matrices = (
        [grad_qkv[:, i * width : (i + 1) * width] for i in range(3)]
        + [grad_out]
        + [grad_fc[:, i * width : (i + 1) * width] for i in range(grad_fc.shape[1] // width)]
        + [grad_proj, small.reshape(shards * lines, width)]
    )
    packed = jnp.concatenate(
        [item.astype(jnp.bfloat16).reshape(shards, -1, width) for item in matrices], axis=1
    )
    summed = scatter_packed(packed)
    pieces, start = [], 0
    for item in matrices:
        size = item.shape[0] // shards
        pieces.append(summed[start : start + size])
        start += size
    sum_qkv = jnp.concatenate(pieces[:3], axis=1)
    sum_out = pieces[3]
    sum_fc = jnp.concatenate(pieces[4:-2], axis=1)
    sum_proj = pieces[-2]
    sum_small = pieces[-1].reshape(-1)
    small, start = [], 0
    for item in vectors:
        size = item.shape[0] // shards
        small.append(sum_small[start : start + size])
        start += size
    return (
        layer_out,
        grad_in,
        sum_qkv,
        small[0],
        small[1],
        sum_out,
        small[2],
        sum_fc,
        small[3],
        sum_proj,
        small[4],
        small[5],
        small[6],
        small[7],
        small[8],
    )


def solution(mesh):
    return jax.shard_map(
        per_device,
        mesh=mesh,
        in_specs=(
            P("fsdp", "ctx", None, None),
            P("fsdp", None),
            P(),
            P(),
            P("fsdp", None),
            P(),
            P("fsdp", None),
            P(),
            P("fsdp", None),
            P(),
            P(),
            P(),
            P(),
            P(),
            P("fsdp", "ctx", None, None),
            P(),
        ),
        out_specs=(
            P("fsdp", "ctx", None, None),
            P("fsdp", "ctx", None, None),
            P(("ctx", "fsdp"), None),
            P(("ctx", "fsdp")),
            P(("ctx", "fsdp")),
            P(("ctx", "fsdp"), None),
            P(("ctx", "fsdp")),
            P(("ctx", "fsdp"), None),
            P(("ctx", "fsdp")),
            P(("ctx", "fsdp"), None),
            P(("ctx", "fsdp")),
            P(("ctx", "fsdp")),
            P(("ctx", "fsdp")),
            P(("ctx", "fsdp")),
            P(("ctx", "fsdp")),
        ),
        check_vma=False,
    )
```

```python
from functools import partial
from types import SimpleNamespace

import jax
import jax.numpy as jnp
from jax import lax
from jax.experimental import pallas as pl
from jax.experimental.pallas import tpu as pltpu
from jax.sharding import PartitionSpec as P

H = 12
HEAD_DIM = 64
BLK = 96


epsilon = 1e-05
masked_score = -1e30


def normalize(values):
    centered = values - jnp.mean(values, axis=-1, keepdims=True)
    inverse = lax.rsqrt(jnp.mean(centered * centered, axis=-1, keepdims=True) + epsilon)
    return (centered * inverse, inverse)


def norm_back(grad_out, normed, inverse, gain):
    scaled = grad_out * gain
    grad_input = inverse * (
        scaled
        - jnp.mean(scaled, axis=-1, keepdims=True)
        - normed * jnp.mean(scaled * normed, axis=-1, keepdims=True)
    )
    return (grad_input, jnp.sum(grad_out * normed, axis=0), jnp.sum(grad_out, axis=0))


def block_positions(pair_table, device, ctx_count):
    pair_index = lax.dynamic_index_in_dim(pair_table, device, 0, keepdims=False)
    column = jnp.arange(2 * BLK, dtype=jnp.int32)
    lower = pair_index * BLK + column
    upper = (2 * ctx_count - 1 - pair_index) * BLK + column - BLK
    return jnp.where(column < BLK, lower, upper)


PAIR = 2 * HEAD_DIM
CHUNK = 8 * 2 * BLK
NT = (((1,), (1,)), ((), ()))


def chunk_of(total):
    return CHUNK if total % CHUNK == 0 else total


def head_only(block, head):
    lane = lax.broadcasted_iota(jnp.int32, block.shape, 1)
    return jnp.where((lane // HEAD_DIM) == head, block, jnp.zeros_like(block))


def head_pick(first, second):
    lane = lax.broadcasted_iota(jnp.int32, first.shape, 1)
    return jnp.where(lane < HEAD_DIM, first, second)


def dot_nt(left, right):
    return lax.dot_general(left, right, NT, preferred_element_type=jnp.float32)


def dot_nn(left, right):
    return jnp.dot(left, right, preferred_element_type=jnp.float32)


def forward_kernel(qpos_ref, kpos_ref, q_ref, k_ref, v_ref, out_ref, lse_ref, max_ref, sum_ref):
    step = pl.program_id(1)
    last = pl.num_programs(1) - 1

    @pl.when(step == 0)
    def _():
        max_ref[...] = jnp.full_like(max_ref, masked_score)
        sum_ref[...] = jnp.zeros_like(sum_ref)
        out_ref[...] = jnp.zeros_like(out_ref)

    allowed = kpos_ref[...] <= qpos_ref[...]
    query, keys, values = q_ref[...], k_ref[...], v_ref[...]
    mixed, factors = [], []
    for head in range(2):
        scores = jnp.where(allowed, dot_nt(head_only(query, head), keys), masked_score)
        old_max = max_ref[head]
        new_max = jnp.maximum(old_max, jnp.max(scores, axis=-1, keepdims=True))
        expd = jnp.exp(scores - new_max)
        factor = jnp.exp(old_max - new_max)
        sum_ref[head] = sum_ref[head] * factor + jnp.sum(expd, axis=-1, keepdims=True)
        max_ref[head] = new_max
        mixed.append(dot_nn(expd.astype(jnp.bfloat16), values))
        factors.append(factor)
    rows = query.shape[0]
    scale = head_pick(*(jnp.broadcast_to(f, (rows, PAIR)) for f in factors))
    out_ref[...] = out_ref[...] * scale + head_pick(mixed[0], mixed[1])

    @pl.when(step == last)
    def _():
        total = head_pick(*(jnp.broadcast_to(sum_ref[h], (rows, PAIR)) for h in range(2)))
        out_ref[...] = out_ref[...] / total
        lse_ref[0] = jnp.concatenate(
            [max_ref[h] + jnp.log(sum_ref[h]) for h in range(2)], axis=-1
        )


def forward_attention(query_pos, key_pos, query, keys_values):
    rows, width = query.shape
    total = keys_values.shape[0]
    chunk = chunk_of(total)
    pairs = width // PAIR
    return pl.pallas_call(
        forward_kernel,
        grid=(pairs, total // chunk),
        in_specs=[
            pl.BlockSpec((rows, 1), lambda h, c: (0, 0)),
            pl.BlockSpec((1, chunk), lambda h, c: (0, c)),
            pl.BlockSpec((rows, PAIR), lambda h, c: (0, h)),
            pl.BlockSpec((chunk, PAIR), lambda h, c: (c, h)),
            pl.BlockSpec((chunk, PAIR), lambda h, c: (c, h + pairs)),
        ],
        out_specs=[
            pl.BlockSpec((rows, PAIR), lambda h, c: (0, h)),
            pl.BlockSpec((1, rows, 2), lambda h, c: (h, 0, 0)),
        ],
        out_shape=[
            jax.ShapeDtypeStruct((rows, width), jnp.float32),
            jax.ShapeDtypeStruct((pairs, rows, 2), jnp.float32),
        ],
        scratch_shapes=[
            pltpu.VMEM((2, rows, 1), jnp.float32),
            pltpu.VMEM((2, rows, 1), jnp.float32),
        ],
        compiler_params=pltpu.CompilerParams(vmem_limit_bytes=40 * 2**20),
        cost_estimate=pl.CostEstimate(
            flops=8 * rows * total * width,
            bytes_accessed=4 * total * width,
            transcendentals=rows * total * H,
        ),
        name="attention_forward",
    )(query_pos[:, None], key_pos[None, :], query, keys_values, keys_values)


def query_kernel(qpos_ref, kpos_ref, q_ref, do_ref, stat_ref, k_ref, v_ref, dq_ref):
    @pl.when(pl.program_id(1) == 0)
    def _():
        dq_ref[...] = jnp.zeros_like(dq_ref)

    allowed = kpos_ref[...] <= qpos_ref[...]
    query, d_out, keys, values = q_ref[...], do_ref[...], k_ref[...], v_ref[...]
    parts = []
    for head in range(2):
        lse = stat_ref[0, :, head : head + 1]
        delta = stat_ref[0, :, head + 2 : head + 3]
        scores = jnp.where(allowed, dot_nt(head_only(query, head), keys), masked_score)
        prob = jnp.exp(scores - lse)
        d_prob = dot_nt(head_only(d_out, head), values)
        d_score = (prob * (d_prob - delta)).astype(jnp.bfloat16)
        parts.append(dot_nn(d_score, keys))
    dq_ref[...] += head_pick(parts[0], parts[1]) * HEAD_DIM ** (-0.5)


def query_gradient(query_pos, key_pos, query, d_out, stats, keys_values):
    rows, width = query.shape
    total = keys_values.shape[0]
    chunk = chunk_of(total)
    pairs = width // PAIR
    return pl.pallas_call(
        query_kernel,
        grid=(pairs, total // chunk),
        in_specs=[
            pl.BlockSpec((rows, 1), lambda h, c: (0, 0)),
            pl.BlockSpec((1, chunk), lambda h, c: (0, c)),
            pl.BlockSpec((rows, PAIR), lambda h, c: (0, h)),
            pl.BlockSpec((rows, PAIR), lambda h, c: (0, h)),
            pl.BlockSpec((1, rows, 4), lambda h, c: (h, 0, 0)),
            pl.BlockSpec((chunk, PAIR), lambda h, c: (c, h)),
            pl.BlockSpec((chunk, PAIR), lambda h, c: (c, h + pairs)),
        ],
        out_specs=pl.BlockSpec((rows, PAIR), lambda h, c: (0, h)),
        out_shape=jax.ShapeDtypeStruct((rows, width), jnp.float32),
        compiler_params=pltpu.CompilerParams(vmem_limit_bytes=40 * 2**20),
        cost_estimate=pl.CostEstimate(
            flops=12 * rows * total * width,
            bytes_accessed=4 * total * width,
            transcendentals=rows * total * H,
        ),
        name="attention_query_gradient",
    )(query_pos[:, None], key_pos[None, :], query, d_out, stats, keys_values, keys_values)


def key_kernel(kpos_ref, qpos_ref, k_ref, v_ref, q_ref, do_ref, stat_ref, dk_ref, dv_ref):
    @pl.when(pl.program_id(1) == 0)
    def _():
        dk_ref[...] = jnp.zeros_like(dk_ref)
        dv_ref[...] = jnp.zeros_like(dv_ref)

    allowed = kpos_ref[...] <= qpos_ref[...]
    keys, values, query, d_out = k_ref[...], v_ref[...], q_ref[...], do_ref[...]
    key_parts, value_parts = [], []
    for head in range(2):
        lse = stat_ref[0, head : head + 1, :]
        delta = stat_ref[0, head + 2 : head + 3, :]
        scores = jnp.where(allowed, dot_nt(head_only(keys, head), query), masked_score)
        prob = jnp.exp(scores - lse)
        value_parts.append(dot_nn(prob.astype(jnp.bfloat16), d_out))
        d_prob = dot_nt(head_only(values, head), d_out)
        d_score = (prob * (d_prob - delta)).astype(jnp.bfloat16)
        key_parts.append(dot_nn(d_score, query))
    dk_ref[...] += head_pick(key_parts[0], key_parts[1])
    dv_ref[...] += head_pick(value_parts[0], value_parts[1])


def key_gradients(key_pos, query_pos, qkv, query_all, d_out_all, stats_all):
    rows = qkv.shape[0]
    total, width = query_all.shape
    chunk = chunk_of(total)
    pairs = width // PAIR
    grad_spec = pl.BlockSpec((rows, PAIR), lambda h, c: (0, h))
    return pl.pallas_call(
        key_kernel,
        grid=(pairs, total // chunk),
        in_specs=[
            pl.BlockSpec((rows, 1), lambda h, c: (0, 0)),
            pl.BlockSpec((1, chunk), lambda h, c: (0, c)),
            pl.BlockSpec((rows, PAIR), lambda h, c: (0, h)),
            pl.BlockSpec((rows, PAIR), lambda h, c: (0, h + pairs)),
            pl.BlockSpec((chunk, PAIR), lambda h, c: (c, h)),
            pl.BlockSpec((chunk, PAIR), lambda h, c: (c, h)),
            pl.BlockSpec((1, 4, chunk), lambda h, c: (h, 0, c)),
        ],
        out_specs=[grad_spec, grad_spec],
        out_shape=[jax.ShapeDtypeStruct((rows, width), jnp.float32)] * 2,
        compiler_params=pltpu.CompilerParams(vmem_limit_bytes=40 * 2**20),
        cost_estimate=pl.CostEstimate(
            flops=16 * rows * total * width,
            bytes_accessed=4 * total * width,
            transcendentals=rows * total * H,
        ),
        name="attention_key_gradients",
    )(key_pos[:, None], query_pos[None, :], qkv, qkv, query_all, d_out_all, stats_all)


def whole_weight(weight):
    share = weight.shape[0] // lax.axis_size("ctx")
    mine = lax.dynamic_slice_in_dim(weight, lax.axis_index("ctx") * share, share, 0)
    return lax.all_gather(mine, ("fsdp", "ctx"), axis=0, tiled=True)


def gather_kernel(chips, shards, count, *refs):
    shares, wholes = refs[:count], refs[count : 2 * count]
    own_sem, z_send, z_recv, c_send, c_recv, k_send, k_recv = refs[2 * count :]
    me, row = lax.axis_index("ctx"), lax.axis_index("fsdp")
    chip, core = me // 2, me % 2
    sibling = (chip * 2 + 1 - core, row)

    def above(step):
        return (me, lax.rem(row + step, shards))

    def across(step):
        return (lax.rem(chip + step, chips) * 2 + core, row)

    barrier = pltpu.get_barrier_semaphore()
    greeted = [above(d) for d in range(1, shards)] + [across(d) for d in range(1, chips)]
    greeted.append(sibling)
    for other in greeted:
        pl.semaphore_signal(barrier, inc=1, device_id=other, device_id_type=pl.DeviceIdType.MESH)
    pl.semaphore_wait(barrier, len(greeted))

    def send(src, dst, send_sem, recv_sem, target):
        copy = pltpu.make_async_remote_copy(
            src_ref=src,
            dst_ref=dst,
            send_sem=send_sem,
            recv_sem=recv_sem,
            device_id=target,
            device_id_type=pl.DeviceIdType.MESH,
        )
        copy.start()
        return copy

    def column(item, index):
        return wholes[item].at[:, index]

    own, along, between, inside = {}, {}, {}, {}
    for i in range(count):
        own[i] = pltpu.make_async_copy(shares[i], wholes[i].at[row, me], own_sem.at[i])
        own[i].start()
        for d in range(1, shards):
            along[i, d] = send(
                shares[i],
                wholes[i].at[row, me],
                z_send.at[i, d - 1],
                z_recv.at[i, d - 1],
                above(d),
            )
    for i in range(count):
        own[i].wait()
        for d in range(1, shards):
            along[i, d].wait_recv()
        for d in range(1, chips):
            mine = column(i, me)
            between[i, d] = send(mine, mine, c_send.at[i, d - 1], c_recv.at[i, d - 1], across(d))
        inside[i, 0] = send(
            column(i, me), column(i, me), k_send.at[i, 0], k_recv.at[i, 0], sibling
        )
    for i in range(count):
        for d in range(1, chips):
            between[i, d].wait_recv()
            came = column(i, lax.rem(chip - d + chips, chips) * 2 + core)
            inside[i, d] = send(came, came, k_send.at[i, d], k_recv.at[i, d], sibling)
    for copy in inside.values():
        copy.wait_recv()
    for copies in (along, between, inside):
        for copy in copies.values():
            copy.wait_send()


def whole_weights(weights):
    ctx_count, shards = lax.axis_size("ctx"), lax.axis_size("fsdp")
    chips = ctx_count // 2
    if ctx_count != 8:
        return [whole_weight(item) for item in weights]
    count = len(weights)
    mine = []
    for item in weights:
        share = item.shape[0] // ctx_count
        mine.append(
            lax.dynamic_slice_in_dim(item, lax.axis_index("ctx") * share, share, 0)
        )
    anywhere = pl.BlockSpec(memory_space=pl.ANY)
    dma = pltpu.SemaphoreType.DMA
    wholes = pl.pallas_call(
        partial(gather_kernel, chips, shards, count),
        in_specs=[anywhere] * count,
        out_specs=[anywhere] * count,
        out_shape=[
            jax.ShapeDtypeStruct((shards, ctx_count) + item.shape, item.dtype) for item in mine
        ],
        scratch_shapes=[
            dma((count,)),
            dma((count, shards - 1)),
            dma((count, shards - 1)),
            dma((count, chips - 1)),
            dma((count, chips - 1)),
            dma((count, chips)),
            dma((count, chips)),
        ],
        compiler_params=pltpu.CompilerParams(collective_id=0, has_side_effects=True),
        name="gather_weights",
    )(*mine)
    return [
        whole.reshape(item.shape[0] * shards, item.shape[1])
        for whole, item in zip(wholes, weights)
    ]


def scatter_kernel(chips, shards, spans, packed, out, own, k_land, c_land, z_land, *sems):
    local, k_send, k_recv, c_send, c_recv, z_send, z_recv = sems
    me, row = lax.axis_index("ctx"), lax.axis_index("fsdp")
    chip, core = me // 2, me % 2
    sibling = (chip * 2 + 1 - core, row)

    def above(step):
        return (me, lax.rem(row + step, shards))

    def across(step):
        return (lax.rem(chip + step, chips) * 2 + core, row)

    barrier = pltpu.get_barrier_semaphore()
    greeted = [above(d) for d in range(1, shards)] + [across(d) for d in range(1, chips)]
    greeted.append(sibling)
    for other in greeted:
        pl.semaphore_signal(barrier, inc=1, device_id=other, device_id_type=pl.DeviceIdType.MESH)
    pl.semaphore_wait(barrier, len(greeted))

    def send(src, dst, send_sem, recv_sem, target):
        copy = pltpu.make_async_remote_copy(
            src_ref=src,
            dst_ref=dst,
            send_sem=send_sem,
            recv_sem=recv_sem,
            device_id=target,
            device_id_type=pl.DeviceIdType.MESH,
        )
        copy.start()
        return copy

    order = list(range(1, chips)) + [0]
    kept, inside, between, along = {}, {}, {}, {}
    for i, span in enumerate(spans):
        rows = pl.ds(*span)
        for d in order:
            part = lax.rem(chip + d, chips)
            inside[i, d] = send(
                packed.at[part, 1 - core, :, rows],
                k_land.at[part, :, rows],
                k_send.at[i, d],
                k_recv.at[i, d],
                sibling,
            )
            kept[i, d] = pltpu.make_async_copy(
                packed.at[part, core, :, rows], own.at[part, :, rows], local.at[i, d]
            )
            kept[i, d].start()
    for i, span in enumerate(spans):
        rows = pl.ds(*span)
        for d in order:
            part = lax.rem(chip + d, chips)
            kept[i, d].wait()
            inside[i, d].wait_recv()

            @pl.loop(0, shards)
            def _(f):
                total = own[part, f, rows].astype(jnp.float32)
                total += k_land[part, f, rows].astype(jnp.float32)
                own[part, f, rows] = total.astype(jnp.bfloat16)

            if d:
                between[i, d] = send(
                    own.at[part, :, rows],
                    c_land.at[d - 1, :, rows],
                    c_send.at[i, d - 1],
                    c_recv.at[i, d - 1],
                    across(d),
                )
    for i, span in enumerate(spans):
        rows = pl.ds(*span)
        for d in range(1, chips):
            between[i, d].wait_recv()

        @pl.loop(0, shards)
        def _(f):
            total = own[chip, f, rows].astype(jnp.float32)
            for d in range(1, chips):
                total += c_land[d - 1, f, rows].astype(jnp.float32)
            own[chip, f, rows] = total.astype(jnp.bfloat16)

        for d in range(1, shards):
            along[i, d] = send(
                own.at[chip, lax.rem(row + d, shards), rows],
                z_land.at[d - 1, rows],
                z_send.at[i, d - 1],
                z_recv.at[i, d - 1],
                above(d),
            )
    for i, span in enumerate(spans):
        rows = pl.ds(*span)
        for d in range(1, shards):
            along[i, d].wait_recv()
        total = own[chip, row, rows].astype(jnp.float32)
        for d in range(1, shards):
            total += z_land[d - 1, rows].astype(jnp.float32)
        out[rows] = total
    for copies in (inside, between, along):
        for copy in copies.values():
            copy.wait_send()


def scatter_packed(packed):
    ctx_count, shards = lax.axis_size("ctx"), lax.axis_size("fsdp")
    _, rows, width = packed.shape
    if ctx_count != 8:
        return scatter(packed.reshape(-1, width)).astype(jnp.float32)
    chips = ctx_count // 2
    first = 16 * (-(-rows // 32))
    spans = ((0, first), (first, rows - first))
    dma = pltpu.SemaphoreType.DMA
    low = jnp.bfloat16
    return pl.pallas_call(
        partial(scatter_kernel, chips, shards, spans),
        in_specs=[pl.BlockSpec(memory_space=pl.ANY)],
        out_specs=pl.BlockSpec(memory_space=pltpu.VMEM),
        out_shape=jax.ShapeDtypeStruct((rows, width), jnp.float32),
        scratch_shapes=[
            pltpu.VMEM((chips, shards, rows, width), low),
            pltpu.VMEM((chips, shards, rows, width), low),
            pltpu.VMEM((chips - 1, shards, rows, width), low),
            pltpu.VMEM((shards - 1, rows, width), low),
            dma((2, chips)),
            dma((2, chips)),
            dma((2, chips)),
            dma((2, chips - 1)),
            dma((2, chips - 1)),
            dma((2, shards - 1)),
            dma((2, shards - 1)),
        ],
        compiler_params=pltpu.CompilerParams(
            collective_id=1, has_side_effects=True, vmem_limit_bytes=44 * 2**20
        ),
        name="sum_gradients",
    )(packed.reshape(chips, 2, shards, rows, width))


def all_positions(pair_table, ctx_count):
    column = jnp.arange(2 * BLK, dtype=jnp.int32)[None, :]
    pair = pair_table[:, None]
    lower = pair * BLK + column
    upper = (2 * ctx_count - 1 - pair) * BLK + column - BLK
    return jnp.where(column < BLK, lower, upper).reshape(-1)


def scatter(term):
    return lax.psum_scatter(term, ("ctx", "fsdp"), scatter_dimension=0, tiled=True)


class Spot:
    def __init__(self, shards):
        self.shards = shards
        self.me, self.row = lax.axis_index("ctx"), lax.axis_index("fsdp")
        chip, core = self.me // 2, self.me % 2
        y, x = chip // 2, chip % 2
        self.core = core
        self.a = (1 - core) * x + core * y
        self.b = (1 - core) * y + core * x
        self.first = self.index(1 - self.a, self.b)
        self.second = self.index(self.a, 1 - self.b)
        self.corner = self.index(1 - self.a, 1 - self.b)
        self.sibling = chip * 2 + 1 - core

    def chip_of(self, a, b):
        return (1 - self.core) * (2 * b + a) + self.core * (2 * a + b)

    def index(self, a, b):
        return self.chip_of(a, b) * 2 + self.core

    def near(self, ctx):
        return (ctx, self.row)

    def above(self, step):
        return (self.me, lax.rem(self.row + step, self.shards))

    def came(self, step):
        return lax.rem(self.row - step + self.shards, self.shards)

    def greet(self):
        barrier = pltpu.get_barrier_semaphore()
        others = [self.above(d) for d in range(1, self.shards)]
        others += [self.near(i) for i in (self.first, self.second, self.sibling)]
        for other in others:
            pl.semaphore_signal(
                barrier, inc=1, device_id=other, device_id_type=pl.DeviceIdType.MESH
            )
        pl.semaphore_wait(barrier, len(others))


def send(src, dst, send_sem, recv_sem, target):
    copy = pltpu.make_async_remote_copy(
        src_ref=src,
        dst_ref=dst,
        send_sem=send_sem,
        recv_sem=recv_sem,
        device_id=target,
        device_id_type=pl.DeviceIdType.MESH,
    )
    copy.start()
    return copy


class Gather:
    def __init__(self, spot, shard, whole, begin, columns, direct, sems):
        self.spot, self.shard, self.whole, self.sems = spot, shard, whole, sems
        self.direct = direct
        self.rows, self.begin, self.half = shard.shape[0], begin, columns // 2
        self.copies = {}

    def cols(self):
        return pl.ds(pl.multiple_of(self.begin + self.spot.core * self.half, 128), self.half)

    def part(self, row, start, size):
        begin = pl.multiple_of(row * self.rows + start, 16)
        return self.whole.at[pl.ds(begin, size), self.cols()]

    def post(self, stage, d, src, dst, target):
        at = stage * (self.spot.shards - 1) + d - 1
        self.copies[stage, d] = send(
            src, dst, self.sems[0].at[at], self.sems[1].at[at], target
        )

    def along(self):
        spot, quarter = self.spot, self.rows // 4
        start = (2 * spot.b + spot.a) * quarter
        if self.direct:
            quarter, start = self.rows, 0
        src = self.shard.at[pl.ds(pl.multiple_of(start, 16), quarter), self.cols()]
        for d in range(1, spot.shards):
            self.post(0, d, src, self.part(spot.row, start, quarter), spot.above(d))

    def step_one(self):
        spot, quarter = self.spot, self.rows // 4
        if self.direct:
            return
        start = (2 * spot.b + spot.a) * quarter
        for d in range(1, spot.shards):
            self.copies[0, d].wait_recv()
            ref = self.part(spot.came(d), start, quarter)
            self.post(1, d, ref, ref, spot.near(spot.first))

    def step_two(self):
        spot, half = self.spot, self.rows // 2
        if self.direct:
            return
        for d in range(1, spot.shards):
            self.copies[1, d].wait_recv()
            ref = self.part(spot.came(d), spot.b * half, half)
            self.post(2, d, ref, ref, spot.near(spot.second))
            self.post(3, d, ref, ref, spot.near(spot.sibling))

    def step_three(self, d):
        spot, half = self.spot, self.rows // 2
        if self.direct:
            self.copies[0, d].wait_recv()
            ref = self.part(spot.came(d), 0, self.rows)
            self.post(4, d, ref, ref, spot.near(spot.sibling))
            return
        self.copies[2, d].wait_recv()
        ref = self.part(spot.came(d), (1 - spot.b) * half, half)
        self.post(4, d, ref, ref, spot.near(spot.sibling))

    def finish(self, d):
        if not self.direct:
            self.copies[3, d].wait_recv()
        self.copies[4, d].wait_recv()

    def complete(self):
        for d in range(1, self.spot.shards):
            self.step_three(d)
        for d in range(1, self.spot.shards):
            self.finish(d)

    def drain(self):
        for copy in self.copies.values():
            copy.wait_send()


class Exchange:
    def __init__(self, spot, view, sems):
        self.spot, self.sems, self.view = spot, sems, view
        self.copies = {}

    def post(self, at, device, target):
        ref = self.view(device)
        self.copies[at] = send(
            ref, ref, self.sems[0].at[at], self.sems[1].at[at], self.spot.near(target)
        )

    def start(self):
        spot = self.spot
        self.post(0, spot.me, spot.first)
        self.post(1, spot.me, spot.second)
        self.post(2, spot.me, spot.sibling)

    def pass_on(self):
        spot = self.spot
        self.copies[0].wait_recv()
        self.post(3, spot.first, spot.second)
        self.post(4, spot.first, spot.sibling)

    def share(self):
        spot = self.spot
        self.copies[1].wait_recv()
        self.post(5, spot.second, spot.sibling)
        self.copies[3].wait_recv()
        self.post(6, spot.corner, spot.sibling)

    def finish(self):
        for at in (2, 4, 5, 6):
            self.copies[at].wait_recv()

    def drain(self):
        for copy in self.copies.values():
            copy.wait_send()


class Unit:
    def __init__(self, spot, packed, lands, sems, store):
        self.spot, self.packed, self.sems, self.store = spot, packed, sems, store
        self.core_land, self.first_land, self.second_land, self.z_land = lands
        self.copies = {}

    def post(self, at, src, dst, target):
        self.copies[at] = send(src, dst, self.sems[0].at[at], self.sems[1].at[at], target)

    def cores(self):
        spot = self.spot
        self.post(
            0, self.packed.at[:, 1 - spot.core], self.core_land, spot.near(spot.sibling)
        )

    def step_one(self):
        spot, land, packed = self.spot, self.core_land, self.packed
        self.copies[0].wait_recv()
        for k, b in enumerate((1 - spot.b, spot.b)):
            chip = spot.chip_of(1 - spot.a, b)
            land[chip] = land[chip] + packed[chip, spot.core]
            self.post(1 + k, land.at[chip], self.first_land.at[k], spot.near(spot.first))
        for b in (1 - spot.b, spot.b):
            chip = spot.chip_of(spot.a, b)
            land[chip] = land[chip] + packed[chip, spot.core]

    def step_two(self):
        spot, land = self.spot, self.first_land
        self.copies[1].wait_recv()
        land[0] = land[0] + self.core_land[spot.chip_of(spot.a, 1 - spot.b)]
        self.post(3, land.at[0], self.second_land, spot.near(spot.second))
        self.copies[2].wait_recv()
        land[1] = land[1] + self.core_land[spot.chip_of(spot.a, spot.b)]

    def along(self):
        spot, land = self.spot, self.second_land
        self.copies[3].wait_recv()
        land[...] = land[...] + self.first_land[1]
        for d in range(1, spot.shards):
            other = lax.rem(spot.row + d, spot.shards)
            self.post(3 + d, land.at[other], self.z_land.at[d - 1], spot.above(d))

    def finish(self):
        spot = self.spot
        total = self.second_land[spot.row].astype(jnp.float32)
        for d in range(1, spot.shards):
            self.copies[3 + d].wait_recv()
            total += self.z_land[d - 1].astype(jnp.float32)
        self.store(total)

    def drain(self):
        for at, copy in self.copies.items():
            if at:
                copy.wait_send()


class UnitAlongFirst(Unit):
    def step_one(self):
        spot, land, packed = self.spot, self.core_land, self.packed
        self.copies[0].wait_recv()
        for chip in range(land.shape[0]):
            land[chip] = land[chip] + packed[chip, spot.core]
        for d in range(1, spot.shards):
            other = lax.rem(spot.row + d, spot.shards)
            self.post(d, land.at[:, other], self.z_land.at[d - 1], spot.above(d))

    def step_two(self):
        spot, land, low = self.spot, self.z_land, self.z_land.dtype
        for d in range(1, spot.shards):
            self.copies[d].wait_recv()

        def add(chip):
            total = self.core_land[chip, spot.row].astype(jnp.float32)
            for d in range(1, spot.shards):
                total += land[d - 1, chip].astype(jnp.float32)
            land[0, chip] = total.astype(low)

        for k, b in enumerate((1 - spot.b, spot.b)):
            chip = spot.chip_of(1 - spot.a, b)
            add(chip)
            at = spot.shards + k
            self.post(at, land.at[0, chip], self.first_land.at[k], spot.near(spot.first))
        for b in (1 - spot.b, spot.b):
            add(spot.chip_of(spot.a, b))

    def along(self):
        spot, land, at = self.spot, self.first_land, self.spot.shards
        self.copies[at].wait_recv()
        land[0] = land[0] + self.z_land[0, spot.chip_of(spot.a, 1 - spot.b)]
        self.post(at + 2, land.at[0], self.second_land, spot.near(spot.second))

    def finish(self):
        spot, at = self.spot, self.spot.shards
        total = self.z_land[0, spot.chip_of(spot.a, spot.b)].astype(jnp.float32)
        self.copies[at + 1].wait_recv()
        total += self.first_land[1].astype(jnp.float32)
        self.copies[at + 2].wait_recv()
        self.store(total + self.second_land[...].astype(jnp.float32))


def dot_tn(left, right):
    return lax.dot_general(
        left, right, (((0,), (0,)), ((), ())), preferred_element_type=jnp.float32
    )


def gelu_pair(u):
    inner = 0.7978845608028654
    cubic = 0.044715
    square = u * u
    bend = jnp.tanh(inner * (u + cubic * (u * square)))
    half = 0.5 * (1.0 + bend)
    slope = half + 0.5 * u * (1.0 - bend * bend) * (inner * (1.0 + 3.0 * cubic * square))
    return u * half, slope


PROJ_COLS, TILE = 256, 256
DELAYS = (0, 1, 3, 5, 7)
DELAYS_ALONG = (0, 1, 5, 7, 9)
ALONG_FIRST = (0, 1)
DIRECT = ()


def layer_kernel(shards, names, *refs):
    r = SimpleNamespace(**dict(zip(names, refs)))
    landings = refs[len(names) :]
    spot = Spot(shards)
    rows, width = r.x.shape
    low = jnp.bfloat16
    pairs = width // PAIR
    kv, qd, stat = r.kv, r.qd, r.stat
    count = kv.shape[0]
    total = count * rows
    own = []
    shards_here = (r.qkv_shard, r.out_shard, r.fc_shard, r.proj_shard)
    for i, (shard, whole) in enumerate(zip(shards_here, (r.qkv, r.out, r.fc, r.proj))):
        size = shard.shape[0]
        begin = pl.multiple_of(spot.row * size, 16)
        own.append(
            pltpu.make_async_copy(shard, whole.at[pl.ds(begin, size)], r.own_sem.at[i])
        )
        own[-1].start()
    every_in = r.every_in
    every_in[spot.me] = r.x[...]
    spot.greet()

    def gather(shard, whole, number, begin, columns):
        sems = r.gather_send.at[number], r.gather_recv.at[number]
        return Gather(spot, shard, whole, begin, columns, number in DIRECT, sems)

    hidden = r.fc.shape[1]
    w_k = gather(r.qkv_shard, r.qkv, 0, width, width)
    w_v = gather(r.qkv_shard, r.qkv, 1, 2 * width, width)
    w_q = gather(r.qkv_shard, r.qkv, 2, 0, width)
    w_out = gather(r.out_shard, r.out, 3, 0, width)
    w_fc = gather(r.fc_shard, r.fc, 4, 0, hidden)
    w_proj = gather(r.proj_shard, r.proj, 5, 0, width)
    gathers = (w_k, w_v, w_q, w_out, w_fc, w_proj)

    def exchange(number, view):
        return Exchange(spot, view, (r.ex_send.at[number], r.ex_recv.at[number]))

    def columns_of(ref, start):
        return lambda device: ref.at[device, :, pl.ds(start, width)]

    x_in = exchange(0, lambda device: r.every_in.at[device])
    x_d_out = exchange(1, columns_of(qd, width))
    x_stat = exchange(2, lambda device: stat.at[device])

    def vector(ref):
        return ref[...].reshape(1, -1)

    x_in.start()
    for item in gathers:
        item.along()
    table = r.table

    def spread(position, pair):
        lower = pair * BLK + position
        upper = (2 * count - 1 - pair) * BLK + position - BLK
        return jnp.where(position < BLK, lower, upper)

    r.qpos[...] = spread(
        lax.broadcasted_iota(jnp.int32, (rows, 1), 0), table[spot.me]
    )
    lane = lax.broadcasted_iota(jnp.int32, (1, total), 1)
    key_pos = jnp.zeros((1, total), jnp.int32)
    for device in range(count):
        local = lane - device * rows
        key_pos = jnp.where(
            (local >= 0) & (local < rows), spread(local, table[device]), key_pos
        )
    r.kpos[...] = key_pos
    x_in.pass_on()
    w_k.step_one()
    w_v.step_one()
    x_in.share()
    w_k.step_two()
    w_q.step_one()
    w_v.step_two()
    x_in.finish()
    x_in.drain()

    @pl.loop(0, count)
    def _(device):
        normed, _ = normalize(every_in[device].astype(jnp.float32))
        every_in[device] = (normed * vector(r.attn_gain) + vector(r.attn_shift)).astype(low)

    def project(start, finish):
        @pl.loop(0, count // 2)
        def _(i):
            two = pl.ds(2 * i, 2)
            block = dot_nn(
                every_in[two].reshape(2 * rows, width), r.qkv[:, pl.ds(start, width)]
            )
            finish(two, block)

    def put_keys(two, block):
        kv[two, :, pl.ds(0, width)] = block.astype(low).reshape(2, rows, width)

    def put_values(two, block):
        block = block + vector(r.value_bias)
        kv[two, :, pl.ds(width, width)] = block.astype(low).reshape(2, rows, width)

    def put_query(two, block):
        block = (block + vector(r.query_bias)).astype(low) * jnp.bfloat16(HEAD_DIM ** (-0.5))
        qd[two, :, pl.ds(0, width)] = block.reshape(2, rows, width)

    w_out.step_one()
    w_q.step_two()
    own[0].wait()
    w_k.complete()
    project(width, put_keys)
    w_fc.step_one()
    w_v.complete()
    w_out.step_two()
    project(2 * width, put_values)
    w_q.complete()
    w_fc.step_two()
    project(0, put_query)
    w_proj.step_one()

    stat_lane = lax.broadcasted_iota(jnp.int32, r.stat_mine.shape, 1)

    def put_stat(index, column):
        r.stat_mine[...] = jnp.where(stat_lane == index, column, r.stat_mine[...])

    def take_stat(index):
        return jnp.sum(
            jnp.where(stat_lane == index, r.stat_mine[...], 0.0), axis=-1, keepdims=True
        )

    r.stat_mine[...] = jnp.zeros_like(r.stat_mine)

    def lanes_of(h, start=0):
        return pl.ds(pl.multiple_of(start + h * PAIR, PAIR), PAIR)

    def attend(h):
        allowed = r.kpos[...] <= r.qpos[...]
        query = qd[spot.me, :, lanes_of(h)]
        keys = kv[:, :, lanes_of(h)].reshape(total, PAIR)
        values = kv[:, :, lanes_of(h, width)].reshape(total, PAIR)
        mixed = []
        for head in range(2):
            scores = jnp.where(allowed, dot_nt(head_only(query, head), keys), masked_score)
            most = jnp.max(scores, axis=-1, keepdims=True)
            expd = jnp.exp(scores - most)
            norm = jnp.sum(expd, axis=-1, keepdims=True)
            mixed.append(dot_nn(expd.astype(low), values) / norm)
            put_stat(4 * h + head, most + jnp.log(norm))
        r.attn[:, lanes_of(h)] = head_pick(mixed[0], mixed[1])

    pl.loop(0, 2)(attend)
    w_out.complete()
    w_proj.step_two()
    pl.loop(2, 4)(attend)
    for d in range(1, shards):
        w_fc.step_three(d)
    pl.loop(4, pairs)(attend)
    own[1].wait()
    attended = r.attn[...].astype(low)
    middle = r.x[...].astype(jnp.float32) + dot_nn(attended, r.out[...]) + vector(r.out_bias)
    r.middle[...] = middle
    normed, _ = normalize(middle)
    r.second[...] = (normed * vector(r.mlp_gain) + vector(r.mlp_shift)).astype(low)
    r.fc_line[...] = vector(r.fc_bias)
    own[2].wait()
    for d in range(1, shards):
        w_fc.finish(d)
    own[3].wait()
    piece = hidden // shards
    for d in range(shards):
        if d:
            w_proj.finish(d)
        n = spot.came(d)
        lanes = pl.ds(pl.multiple_of(n * piece, 128), piece)
        share = pl.ds(pl.multiple_of(n * piece, 16), piece)
        pre = dot_nn(r.second[...], r.fc[:, lanes]) + r.fc_line[:, lanes]
        activated, slope = gelu_pair(pre)
        activated = activated.astype(low)
        r.act[:, lanes] = activated
        result = dot_nn(activated, r.proj[share])
        d_act = dot_nt(r.cot[...], r.proj[share])
        d_pre = (d_act * slope).astype(low)
        r.d_pre[:, lanes] = d_pre
        d_second = dot_nt(d_pre, r.fc[:, lanes])
        if d:
            r.result[...] += result
            r.d_second[...] += d_second
        else:
            r.result[...] = result
            r.d_second[...] = d_second
            for k in range(1, shards):
                w_proj.step_three(k)

    units, makers = [], []
    used = ([], [])

    def make_proj(packed, n):
        right = r.cot[:, n * PROJ_COLS : (n + 1) * PROJ_COLS]

        @pl.loop(0, 4)
        def _(chip):
            share = hidden // 4
            left = r.act[:, pl.ds(pl.multiple_of(chip * share, 128), share)]
            packed[chip] = dot_tn(left, right).reshape(packed.shape[1:]).astype(low)

    def make_rows(packed, left_ref, right_ref, start):
        left = left_ref[...]

        @pl.loop(0, width // TILE)
        def _(n):
            right = right_ref[:, pl.ds(pl.multiple_of(start + n * TILE, 128), TILE)]
            block = dot_tn(left, right).reshape(packed.shape[:-1] + (TILE,))
            packed[..., pl.ds(pl.multiple_of(n * TILE, 128), TILE)] = block.astype(low)

    def add(kind, out_ref, start, columns, make):
        packs = (r.mid_pack, r.proj_pack)[kind]
        slots = packs.shape[0]
        packed = packs.at[len(used[kind]) % slots]
        number = len(units)

        def store(total):
            out_ref[:, start : start + columns] = total

        lands = landings[4 * number : 4 * number + 4]
        sems = r.unit_send.at[number], r.unit_recv.at[number]
        kind_of = UnitAlongFirst if number in ALONG_FIRST else Unit
        unit = kind_of(spot, packed, lands, sems, store)
        earlier = used[kind][-slots] if len(used[kind]) >= slots else None
        used[kind].append(unit)
        units.append(unit)

        def begin():
            if earlier is not None:
                earlier.copies[0].wait_send()
            make(packed)
            unit.cores()

        makers.append(begin)

    for n in range(hidden // width):
        add(0, r.g_fc, n * width, width, lambda p, n=n: make_rows(p, r.second, r.d_pre, n * width))
    for n in range(width // PROJ_COLS):
        add(1, r.g_proj, n * PROJ_COLS, PROJ_COLS, lambda p, n=n: make_proj(p, n))
    add(0, r.g_out, 0, width, lambda p: make_rows(p, r.attended, r.d_branch, 0))
    for n in range(3):
        add(0, r.g_qkv, n * width, width, lambda p, n=n: make_rows(p, every_in.at[spot.me], r.d_qkv, n * width))

    def slot(number):
        if number < len(units):
            makers[number]()
        for stage in range(1, 5):
            for i, unit in enumerate(units):
                delays = DELAYS_ALONG if i in ALONG_FIRST else DELAYS
                if number - i == delays[stage]:
                    (unit.step_one, unit.step_two, unit.along, unit.finish)[stage - 1]()

    slot(0)
    middle = r.middle[...]
    r.layer_out[...] = (middle + r.result[...] + vector(r.proj_bias)).astype(low)
    normed, inverse = normalize(middle)
    d_norm, grad_mlp_gain, grad_mlp_shift = norm_back(
        r.d_second[...], normed, inverse, vector(r.mlp_gain)
    )
    d_middle = r.cot[...].astype(jnp.float32) + d_norm
    r.d_middle[...] = d_middle
    d_branch = d_middle.astype(low)
    r.d_branch[...] = d_branch
    d_attended = dot_nt(d_branch, r.out[...]).astype(low)
    qd[spot.me, :, pl.ds(width, width)] = d_attended
    x_d_out.start()
    r.attended[...] = r.attn[...].astype(low)

    def deltas(h):
        d_out = qd[spot.me, :, lanes_of(h, width)].astype(jnp.float32)
        both = d_out * r.attn[:, lanes_of(h)]
        for head in range(2):
            put_stat(4 * h + 2 + head, jnp.sum(head_only(both, head), axis=-1, keepdims=True))

    pl.loop(0, pairs)(deltas)
    stat[spot.me] = jnp.transpose(r.stat_mine[...])[: stat.shape[1]]
    x_stat.start()
    slot(1)
    x_d_out.pass_on()
    x_stat.pass_on()

    def query_pair(h):
        allowed = r.kpos[...] <= r.qpos[...]
        query, d_out = qd[spot.me, :, lanes_of(h)], qd[spot.me, :, lanes_of(h, width)]
        keys = kv[:, :, lanes_of(h)].reshape(total, PAIR)
        values = kv[:, :, lanes_of(h, width)].reshape(total, PAIR)
        parts = []
        for head in range(2):
            lse, delta = take_stat(4 * h + head), take_stat(4 * h + 2 + head)
            scores = jnp.where(allowed, dot_nt(head_only(query, head), keys), masked_score)
            prob = jnp.exp(scores - lse)
            d_prob = dot_nt(head_only(d_out, head), values)
            parts.append(dot_nn((prob * (d_prob - delta)).astype(low), keys))
        d_query = head_pick(parts[0], parts[1]) * HEAD_DIM ** (-0.5)
        r.d_qkv[:, lanes_of(h)] = d_query.astype(low)

    def key_pair(h):
        keys, values = kv[spot.me, :, lanes_of(h)], kv[spot.me, :, lanes_of(h, width)]
        my_keys = [head_only(keys, head) for head in range(2)]
        my_values = [head_only(values, head) for head in range(2)]
        key_parts = [jnp.zeros((rows, PAIR), jnp.float32)] * 2
        value_parts = [jnp.zeros((rows, PAIR), jnp.float32)] * 2
        half = count // 2
        span = half * rows
        for chunk in range(2):
            part = pl.ds(chunk * half, half)
            allowed = r.qpos[...] <= r.kpos[:, chunk * span : (chunk + 1) * span]
            query = qd[part, :, lanes_of(h)].reshape(span, PAIR)
            d_out = qd[part, :, lanes_of(h, width)].reshape(span, PAIR)

            def line(index):
                parts = [stat[chunk * half + i, pl.ds(index, 1), :] for i in range(half)]
                return jnp.concatenate(parts, axis=-1)

            for head in range(2):
                lse, delta = line(4 * h + head), line(4 * h + 2 + head)
                scores = jnp.where(allowed, dot_nt(my_keys[head], query), masked_score)
                prob = jnp.exp(scores - lse)
                value_parts[head] = value_parts[head] + dot_nn(prob.astype(low), d_out)
                d_prob = dot_nt(my_values[head], d_out)
                d_score = (prob * (d_prob - delta)).astype(low)
                key_parts[head] = key_parts[head] + dot_nn(d_score, query)
        r.d_qkv[:, lanes_of(h, width)] = head_pick(*key_parts).astype(low)
        r.d_qkv[:, lanes_of(h, 2 * width)] = head_pick(*value_parts).astype(low)

    slot(2)
    slot(3)
    pl.loop(0, 2)(query_pair)
    x_d_out.share()
    x_stat.share()
    slot(4)
    pl.loop(2, 4)(query_pair)
    slot(5)
    pl.loop(4, pairs)(query_pair)
    x_d_out.finish()
    x_stat.finish()
    slot(6)
    pl.loop(0, 2)(key_pair)
    slot(7)
    pl.loop(2, 4)(key_pair)
    slot(8)
    pl.loop(4, pairs)(key_pair)
    slot(9)
    slot(10)
    slot(11)
    d_qkv = r.d_qkv[...]
    d_first = dot_nt(d_qkv, r.qkv[...])
    normed, inverse = normalize(r.x[...].astype(jnp.float32))
    d_norm, grad_gain, grad_shift = norm_back(d_first, normed, inverse, vector(r.attn_gain))
    d_middle = r.d_middle[...]
    r.grad_in[...] = d_middle + d_norm

    def over_tokens(block):
        return jnp.sum(block.astype(jnp.float32), axis=0, keepdims=True)

    bias_fc = over_tokens(r.d_pre[...])
    lines = [
        over_tokens(d_qkv[:, :width]),
        over_tokens(d_qkv[:, 2 * width :]),
        over_tokens(d_middle),
        over_tokens(r.cot[...]),
        grad_gain.reshape(1, -1),
        grad_shift.reshape(1, -1),
        grad_mlp_gain.reshape(1, -1),
        grad_mlp_shift.reshape(1, -1),
    ]
    lines += [bias_fc[:, i * width : (i + 1) * width] for i in range(hidden // width)]
    vec_land, vec_part = r.vec_land, r.vec_part
    vec_part[0] = jnp.zeros(vec_part.shape[1:], jnp.float32)
    for i, item in enumerate(lines):
        vec_part[0, i : i + 1] = item
    vec_copies = []

    def vec_post(k, src, target):
        copy = send(src, vec_land.at[k], r.vec_send.at[k], r.vec_recv.at[k], target)
        vec_copies.append(copy)
        return copy

    for k, other in enumerate((spot.sibling, spot.first, spot.second)):
        copy = vec_post(k, vec_part.at[k], spot.near(other))
        slot(len(units) + 1 + k)
        copy.wait_recv()
        vec_part[k + 1] = vec_part[k] + vec_land[k]
    for d in range(1, shards):
        vec_post(2 + d, vec_part.at[3], spot.above(d))
    for number in range(len(units) + 4, len(units) + DELAYS[-1]):
        slot(number)
    summed = vec_part[3]
    for d in range(1, shards):
        vec_copies[2 + d].wait_recv()
        summed = summed + vec_land[2 + d]
    r.sums[...] = summed
    for copy in vec_copies:
        copy.wait_send()
    for kind, packs in zip(used, (r.mid_pack, r.proj_pack)):
        for unit in kind[-packs.shape[0] :]:
            unit.copies[0].wait_send()
    for item in (*units, *gathers):
        item.drain()
    for item in (x_d_out, x_stat):
        item.drain()


def whole_layer(**inputs):
    shards, ctx_count = lax.axis_size("fsdp"), lax.axis_size("ctx")
    rows, width = inputs.get("x").shape
    hidden = inputs.get("fc_shard").shape[1]
    low, wide = jnp.bfloat16, jnp.float32
    dma = pltpu.SemaphoreType.DMA
    chips, devices = ctx_count // 2, ctx_count * shards
    mid = (width // devices, width)
    tall = (hidden // devices, PROJ_COLS)
    shapes = [mid] * (hidden // width) + [tall] * (width // PROJ_COLS) + [mid] * 4
    vmem = pltpu.VMEM
    scratch = dict(
        qkv=vmem((width, 3 * width), low),
        out=vmem((width, width), low),
        fc=vmem((width, hidden), low),
        proj=vmem((hidden, width), low),
        kv=vmem((ctx_count, rows, 2 * width), low),
        qd=vmem((ctx_count, rows, 2 * width), low),
        stat=vmem((ctx_count, 4 * width // PAIR, rows), wide),
        stat_mine=vmem((rows, 128), wide),
        qpos=vmem((rows, 1), jnp.int32),
        kpos=vmem((1, ctx_count * rows), jnp.int32),
        every_in=vmem((ctx_count, rows, width), low),
        attn=vmem((rows, width), wide),
        attended=vmem((rows, width), low),
        middle=vmem((rows, width), wide),
        second=vmem((rows, width), low),
        fc_line=vmem((1, hidden), wide),
        act=vmem((rows, hidden), low),
        d_pre=vmem((rows, hidden), low),
        result=vmem((rows, width), wide),
        d_second=vmem((rows, width), wide),
        d_middle=vmem((rows, width), wide),
        d_branch=vmem((rows, width), low),
        d_qkv=vmem((rows, 3 * width), low),
        vec_land=vmem((2 + shards, 16, width), wide),
        vec_part=vmem((4, 16, width), wide),
        mid_pack=vmem((3, chips, 2, shards) + mid, low),
        proj_pack=vmem((2, chips, 2, shards) + tall, low),
        own_sem=dma((4,)),
        gather_send=dma((6, 5 * (shards - 1))),
        gather_recv=dma((6, 5 * (shards - 1))),
        ex_send=dma((3, 7)),
        ex_recv=dma((3, 7)),
        unit_send=dma((len(shapes), 3 + shards)),
        unit_recv=dma((len(shapes), 3 + shards)),
        vec_send=dma((2 + shards,)),
        vec_recv=dma((2 + shards,)),
    )
    landings = []
    for i, shape in enumerate(shapes):
        if i in ALONG_FIRST:
            landings += [
                vmem((chips, shards) + shape, low),
                vmem((2,) + shape, low),
                vmem(shape, low),
                vmem((shards - 1, chips) + shape, low),
            ]
            continue
        landings += [
            vmem((chips, shards) + shape, low),
            vmem((2, shards) + shape, low),
            vmem((shards,) + shape, low),
            vmem((shards - 1,) + shape, low),
        ]
    outputs = dict(
        layer_out=jax.ShapeDtypeStruct((rows, width), low),
        grad_in=jax.ShapeDtypeStruct((rows, width), wide),
        g_qkv=jax.ShapeDtypeStruct((width // devices, 3 * width), wide),
        g_out=jax.ShapeDtypeStruct((width // devices, width), wide),
        g_fc=jax.ShapeDtypeStruct((width // devices, hidden), wide),
        g_proj=jax.ShapeDtypeStruct((hidden // devices, width), wide),
        sums=jax.ShapeDtypeStruct((16, width), wide),
    )
    inside = pl.BlockSpec(memory_space=pltpu.VMEM)
    anywhere = pl.BlockSpec(memory_space=pl.ANY)
    return pl.pallas_call(
        partial(layer_kernel, shards, (*inputs, *outputs, *scratch)),
        in_specs=[pl.BlockSpec(memory_space=pltpu.SMEM)]
        + [inside] * (len(inputs) - 5)
        + [anywhere] * 4,
        out_specs=[inside] * len(outputs),
        out_shape=list(outputs.values()),
        scratch_shapes=list(scratch.values()) + landings,
        compiler_params=pltpu.CompilerParams(
            collective_id=0, has_side_effects=True, vmem_limit_bytes=VMEM_LIMIT
        ),
        name="whole",
    )(*inputs.values())


VMEM_LIMIT = 62 * 2**20


def finish_kernel(*refs):
    ins, outs = refs[:7], refs[7:]
    for src, dst in zip(ins[:6], outs[:6]):
        dst[...] = src[...]
    sums, small = ins[6], outs[6:]
    shards = lax.axis_size("fsdp")
    devices = lax.axis_size("ctx") * shards
    device = lax.axis_index("ctx") * shards + lax.axis_index("fsdp")
    width = sums.shape[1]

    def piece(rows, start, size):
        return pltpu.roll(rows, lax.rem(width - start, width), 1)[:, :size]

    share = width // devices
    lines = piece(sums[0:8], device * share, share)
    for i in range(8):
        small[i][...] = lines[i : i + 1]
    share = small[8].shape[1]
    fit = width // share
    line = sums[pl.ds(8 + device // fit, 1), :]
    eight = jnp.broadcast_to(line, (8, width))
    small[8][...] = piece(eight, lax.rem(device, fit) * share, share)[0:1]


def device_slices(*parts, shape):
    devices = lax.axis_size("ctx") * lax.axis_size("fsdp")
    width = parts[6].shape[1]
    inside = pl.BlockSpec(memory_space=pltpu.VMEM)
    shares = [width // devices] * 8 + [parts[4].shape[1] // devices]
    outs = pl.pallas_call(
        finish_kernel,
        in_specs=[inside] * 7,
        out_specs=[inside] * 15,
        out_shape=[jax.ShapeDtypeStruct(p.shape, p.dtype) for p in parts[:6]]
        + [jax.ShapeDtypeStruct((1, share), jnp.float32) for share in shares],
        name="finish",
    )(*parts)
    layer_out, grad_in, g_qkv, g_out, g_fc, g_proj = outs[:6]
    small = [item.reshape(-1) for item in outs[6:]]
    return (
        layer_out.reshape(shape),
        grad_in.reshape(shape),
        g_qkv,
        small[0],
        small[1],
        g_out,
        small[2],
        g_fc,
        small[8],
        g_proj,
        *small[3:8],
    )


def per_device(
    layer_in,
    qkv_weight,
    query_bias,
    value_bias,
    out_weight,
    out_bias,
    fc_weight,
    fc_bias,
    proj_weight,
    proj_bias,
    attn_norm_gain,
    attn_norm_shift,
    mlp_norm_gain,
    mlp_norm_shift,
    cotangent,
    pair_table,
):
    ctx_count = lax.axis_size("ctx")
    shards = ctx_count * lax.axis_size("fsdp")
    _, _, rows, width = layer_in.shape
    if ctx_count == 8:
        outs = whole_layer(
            table=pair_table,
            x=layer_in.reshape(rows, width),
            cot=cotangent.reshape(rows, width),
            attn_gain=attn_norm_gain,
            attn_shift=attn_norm_shift,
            mlp_gain=mlp_norm_gain,
            mlp_shift=mlp_norm_shift,
            query_bias=query_bias,
            value_bias=value_bias,
            out_bias=out_bias,
            proj_bias=proj_bias,
            fc_bias=fc_bias,
            qkv_shard=qkv_weight,
            out_shard=out_weight,
            fc_shard=fc_weight,
            proj_shard=proj_weight,
        )
        return device_slices(*outs, shape=layer_in.shape)
    my_pos = block_positions(pair_table, lax.axis_index("ctx"), ctx_count)
    every_pos = all_positions(pair_table, ctx_count)
    flat_in = layer_in.reshape(rows, width).astype(jnp.float32)
    full_qkv, full_out, full_fc, full_proj = whole_weights(
        (qkv_weight, out_weight, fc_weight, proj_weight)
    )
    normed_one, inverse_one = normalize(flat_in)
    first_in = (normed_one * attn_norm_gain + attn_norm_shift).astype(jnp.bfloat16)
    keys_values = (
        jnp.dot(first_in, full_qkv[:, width:], preferred_element_type=jnp.float32)
        + jnp.concatenate([jnp.zeros_like(value_bias), value_bias])
    ).astype(jnp.bfloat16)
    every_kv = lax.all_gather(keys_values, "ctx", axis=0, tiled=True)
    query = (
        jnp.dot(first_in, full_qkv[:, :width], preferred_element_type=jnp.float32) + query_bias
    ).astype(jnp.bfloat16) * jnp.bfloat16(HEAD_DIM ** (-0.5))
    every_query = lax.all_gather(query, "ctx", axis=0, tiled=True)
    attn_exact, lse = forward_attention(my_pos, every_pos, query, every_kv)
    attended = attn_exact.astype(jnp.bfloat16)
    middle = flat_in + jnp.dot(attended, full_out, preferred_element_type=jnp.float32) + out_bias
    normed_two, inverse_two = normalize(middle)
    second_in = (normed_two * mlp_norm_gain + mlp_norm_shift).astype(jnp.bfloat16)
    pre_act = jnp.dot(second_in, full_fc, preferred_element_type=jnp.float32) + fc_bias
    activated, gelu_back = jax.vjp(partial(jax.nn.gelu, approximate=True), pre_act)
    act_low = activated.astype(jnp.bfloat16)
    result = middle + jnp.dot(act_low, full_proj, preferred_element_type=jnp.float32) + proj_bias
    layer_out = result.astype(jnp.bfloat16).reshape(layer_in.shape)
    d_result = cotangent.reshape(rows, width)
    d_act = jnp.einsum("td,fd->tf", d_result, full_proj, preferred_element_type=jnp.float32)
    (d_pre,) = gelu_back(d_act)
    d_pre_low = d_pre.astype(jnp.bfloat16)
    d_second = jnp.einsum("tf,df->td", d_pre_low, full_fc, preferred_element_type=jnp.float32)
    d_mid_norm, grad_mlp_gain, grad_mlp_shift = norm_back(
        d_second, normed_two, inverse_two, mlp_norm_gain
    )
    d_middle = d_result.astype(jnp.float32) + d_mid_norm
    d_branch = d_middle.astype(jnp.bfloat16)
    d_attended = jnp.einsum(
        "te,de->td", d_branch, full_out, preferred_element_type=jnp.float32
    ).astype(jnp.bfloat16)
    delta = jnp.sum(
        (d_attended.astype(jnp.float32) * attn_exact).reshape(rows, width // PAIR, 2, HEAD_DIM),
        axis=-1,
    )
    stats = jnp.concatenate([lse, jnp.transpose(delta, (1, 0, 2))], axis=-1)
    every_d_out = lax.all_gather(d_attended, "ctx", axis=0, tiled=True)
    every_stat = lax.all_gather(
        jnp.transpose(stats, (0, 2, 1)).reshape(-1, rows), "ctx", axis=1, tiled=True
    ).reshape(width // PAIR, 4, ctx_count * rows)
    grad_proj = jnp.einsum("tf,td->fd", act_low, d_result, preferred_element_type=jnp.float32)
    grad_fc = jnp.einsum("td,tf->df", second_in, d_pre_low, preferred_element_type=jnp.float32)
    grad_out = jnp.einsum("td,te->de", attended, d_branch, preferred_element_type=jnp.float32)
    d_query = query_gradient(my_pos, every_pos, query, d_attended, stats, every_kv)
    d_key, d_value = key_gradients(
        my_pos, every_pos, keys_values, every_query, every_d_out, every_stat
    )
    d_qkv = jnp.concatenate([d_query, d_key, d_value], axis=1).astype(jnp.bfloat16)
    grad_qkv = jnp.einsum("td,te->de", first_in, d_qkv, preferred_element_type=jnp.float32)
    d_first = jnp.einsum("te,de->td", d_qkv, full_qkv, preferred_element_type=jnp.float32)
    d_in_norm, grad_attn_gain, grad_attn_shift = norm_back(
        d_first, normed_one, inverse_one, attn_norm_gain
    )
    grad_in = (d_middle + d_in_norm).reshape(layer_in.shape)
    bias_sum = jnp.sum(d_qkv.astype(jnp.float32), axis=0)
    vectors = (
        bias_sum[:width],
        bias_sum[2 * width :],
        jnp.sum(d_middle, axis=0),
        jnp.sum(d_pre_low.astype(jnp.float32), axis=0),
        jnp.sum(d_result.astype(jnp.float32), axis=0),
        grad_attn_gain,
        grad_attn_shift,
        grad_mlp_gain,
        grad_mlp_shift,
    )
    small = jnp.concatenate([item.reshape(shards, -1) for item in vectors], axis=1)
    lines = 16 * -(-small.shape[1] // (16 * width))
    small = jnp.pad(small, ((0, 0), (0, lines * width - small.shape[1])))
    matrices = (
        [grad_qkv[:, i * width : (i + 1) * width] for i in range(3)]
        + [grad_out]
        + [grad_fc[:, i * width : (i + 1) * width] for i in range(grad_fc.shape[1] // width)]
        + [grad_proj, small.reshape(shards * lines, width)]
    )
    packed = jnp.concatenate(
        [item.astype(jnp.bfloat16).reshape(shards, -1, width) for item in matrices], axis=1
    )
    summed = scatter_packed(packed)
    pieces, start = [], 0
    for item in matrices:
        size = item.shape[0] // shards
        pieces.append(summed[start : start + size])
        start += size
    sum_qkv = jnp.concatenate(pieces[:3], axis=1)
    sum_out = pieces[3]
    sum_fc = jnp.concatenate(pieces[4:-2], axis=1)
    sum_proj = pieces[-2]
    sum_small = pieces[-1].reshape(-1)
    small, start = [], 0
    for item in vectors:
        size = item.shape[0] // shards
        small.append(sum_small[start : start + size])
        start += size
    return (
        layer_out,
        grad_in,
        sum_qkv,
        small[0],
        small[1],
        sum_out,
        small[2],
        sum_fc,
        small[3],
        sum_proj,
        small[4],
        small[5],
        small[6],
        small[7],
        small[8],
    )


def solution(mesh):
    return jax.shard_map(
        per_device,
        mesh=mesh,
        in_specs=(
            P("fsdp", "ctx", None, None),
            P("fsdp", None),
            P(),
            P(),
            P("fsdp", None),
            P(),
            P("fsdp", None),
            P(),
            P("fsdp", None),
            P(),
            P(),
            P(),
            P(),
            P(),
            P("fsdp", "ctx", None, None),
            P(),
        ),
        out_specs=(
            P("fsdp", "ctx", None, None),
            P("fsdp", "ctx", None, None),
            P(("ctx", "fsdp"), None),
            P(("ctx", "fsdp")),
            P(("ctx", "fsdp")),
            P(("ctx", "fsdp"), None),
            P(("ctx", "fsdp")),
            P(("ctx", "fsdp"), None),
            P(("ctx", "fsdp")),
            P(("ctx", "fsdp"), None),
            P(("ctx", "fsdp")),
            P(("ctx", "fsdp")),
            P(("ctx", "fsdp")),
            P(("ctx", "fsdp")),
            P(("ctx", "fsdp")),
        ),
        check_vma=False,
    )
```

```python
from functools import partial
from types import SimpleNamespace

import jax
import jax.numpy as jnp
from jax import lax
from jax.experimental import pallas as pl
from jax.experimental.pallas import tpu as pltpu
from jax.sharding import PartitionSpec as P

H = 12
HEAD_DIM = 64
BLK = 96


epsilon = 1e-05
masked_score = -1e30


def normalize(values):
    centered = values - jnp.mean(values, axis=-1, keepdims=True)
    inverse = lax.rsqrt(jnp.mean(centered * centered, axis=-1, keepdims=True) + epsilon)
    return (centered * inverse, inverse)


def norm_back(grad_out, normed, inverse, gain):
    scaled = grad_out * gain
    grad_input = inverse * (
        scaled
        - jnp.mean(scaled, axis=-1, keepdims=True)
        - normed * jnp.mean(scaled * normed, axis=-1, keepdims=True)
    )
    return (grad_input, jnp.sum(grad_out * normed, axis=0), jnp.sum(grad_out, axis=0))


def block_positions(pair_table, device, ctx_count):
    pair_index = lax.dynamic_index_in_dim(pair_table, device, 0, keepdims=False)
    column = jnp.arange(2 * BLK, dtype=jnp.int32)
    lower = pair_index * BLK + column
    upper = (2 * ctx_count - 1 - pair_index) * BLK + column - BLK
    return jnp.where(column < BLK, lower, upper)


PAIR = 2 * HEAD_DIM
CHUNK = 8 * 2 * BLK
NT = (((1,), (1,)), ((), ()))


def chunk_of(total):
    return CHUNK if total % CHUNK == 0 else total


def head_only(block, head):
    lane = lax.broadcasted_iota(jnp.int32, block.shape, 1)
    return jnp.where((lane // HEAD_DIM) == head, block, jnp.zeros_like(block))


def head_pick(first, second):
    lane = lax.broadcasted_iota(jnp.int32, first.shape, 1)
    return jnp.where(lane < HEAD_DIM, first, second)


def dot_nt(left, right):
    return lax.dot_general(left, right, NT, preferred_element_type=jnp.float32)


def dot_nn(left, right):
    return jnp.dot(left, right, preferred_element_type=jnp.float32)


def forward_kernel(qpos_ref, kpos_ref, q_ref, k_ref, v_ref, out_ref, lse_ref, max_ref, sum_ref):
    step = pl.program_id(1)
    last = pl.num_programs(1) - 1

    @pl.when(step == 0)
    def _():
        max_ref[...] = jnp.full_like(max_ref, masked_score)
        sum_ref[...] = jnp.zeros_like(sum_ref)
        out_ref[...] = jnp.zeros_like(out_ref)

    allowed = kpos_ref[...] <= qpos_ref[...]
    query, keys, values = q_ref[...], k_ref[...], v_ref[...]
    mixed, factors = [], []
    for head in range(2):
        scores = jnp.where(allowed, dot_nt(head_only(query, head), keys), masked_score)
        old_max = max_ref[head]
        new_max = jnp.maximum(old_max, jnp.max(scores, axis=-1, keepdims=True))
        expd = jnp.exp(scores - new_max)
        factor = jnp.exp(old_max - new_max)
        sum_ref[head] = sum_ref[head] * factor + jnp.sum(expd, axis=-1, keepdims=True)
        max_ref[head] = new_max
        mixed.append(dot_nn(expd.astype(jnp.bfloat16), values))
        factors.append(factor)
    rows = query.shape[0]
    scale = head_pick(*(jnp.broadcast_to(f, (rows, PAIR)) for f in factors))
    out_ref[...] = out_ref[...] * scale + head_pick(mixed[0], mixed[1])

    @pl.when(step == last)
    def _():
        total = head_pick(*(jnp.broadcast_to(sum_ref[h], (rows, PAIR)) for h in range(2)))
        out_ref[...] = out_ref[...] / total
        lse_ref[0] = jnp.concatenate(
            [max_ref[h] + jnp.log(sum_ref[h]) for h in range(2)], axis=-1
        )


def forward_attention(query_pos, key_pos, query, keys_values):
    rows, width = query.shape
    total = keys_values.shape[0]
    chunk = chunk_of(total)
    pairs = width // PAIR
    return pl.pallas_call(
        forward_kernel,
        grid=(pairs, total // chunk),
        in_specs=[
            pl.BlockSpec((rows, 1), lambda h, c: (0, 0)),
            pl.BlockSpec((1, chunk), lambda h, c: (0, c)),
            pl.BlockSpec((rows, PAIR), lambda h, c: (0, h)),
            pl.BlockSpec((chunk, PAIR), lambda h, c: (c, h)),
            pl.BlockSpec((chunk, PAIR), lambda h, c: (c, h + pairs)),
        ],
        out_specs=[
            pl.BlockSpec((rows, PAIR), lambda h, c: (0, h)),
            pl.BlockSpec((1, rows, 2), lambda h, c: (h, 0, 0)),
        ],
        out_shape=[
            jax.ShapeDtypeStruct((rows, width), jnp.float32),
            jax.ShapeDtypeStruct((pairs, rows, 2), jnp.float32),
        ],
        scratch_shapes=[
            pltpu.VMEM((2, rows, 1), jnp.float32),
            pltpu.VMEM((2, rows, 1), jnp.float32),
        ],
        compiler_params=pltpu.CompilerParams(vmem_limit_bytes=40 * 2**20),
        cost_estimate=pl.CostEstimate(
            flops=8 * rows * total * width,
            bytes_accessed=4 * total * width,
            transcendentals=rows * total * H,
        ),
        name="attention_forward",
    )(query_pos[:, None], key_pos[None, :], query, keys_values, keys_values)


def query_kernel(qpos_ref, kpos_ref, q_ref, do_ref, stat_ref, k_ref, v_ref, dq_ref):
    @pl.when(pl.program_id(1) == 0)
    def _():
        dq_ref[...] = jnp.zeros_like(dq_ref)

    allowed = kpos_ref[...] <= qpos_ref[...]
    query, d_out, keys, values = q_ref[...], do_ref[...], k_ref[...], v_ref[...]
    parts = []
    for head in range(2):
        lse = stat_ref[0, :, head : head + 1]
        delta = stat_ref[0, :, head + 2 : head + 3]
        scores = jnp.where(allowed, dot_nt(head_only(query, head), keys), masked_score)
        prob = jnp.exp(scores - lse)
        d_prob = dot_nt(head_only(d_out, head), values)
        d_score = (prob * (d_prob - delta)).astype(jnp.bfloat16)
        parts.append(dot_nn(d_score, keys))
    dq_ref[...] += head_pick(parts[0], parts[1]) * HEAD_DIM ** (-0.5)


def query_gradient(query_pos, key_pos, query, d_out, stats, keys_values):
    rows, width = query.shape
    total = keys_values.shape[0]
    chunk = chunk_of(total)
    pairs = width // PAIR
    return pl.pallas_call(
        query_kernel,
        grid=(pairs, total // chunk),
        in_specs=[
            pl.BlockSpec((rows, 1), lambda h, c: (0, 0)),
            pl.BlockSpec((1, chunk), lambda h, c: (0, c)),
            pl.BlockSpec((rows, PAIR), lambda h, c: (0, h)),
            pl.BlockSpec((rows, PAIR), lambda h, c: (0, h)),
            pl.BlockSpec((1, rows, 4), lambda h, c: (h, 0, 0)),
            pl.BlockSpec((chunk, PAIR), lambda h, c: (c, h)),
            pl.BlockSpec((chunk, PAIR), lambda h, c: (c, h + pairs)),
        ],
        out_specs=pl.BlockSpec((rows, PAIR), lambda h, c: (0, h)),
        out_shape=jax.ShapeDtypeStruct((rows, width), jnp.float32),
        compiler_params=pltpu.CompilerParams(vmem_limit_bytes=40 * 2**20),
        cost_estimate=pl.CostEstimate(
            flops=12 * rows * total * width,
            bytes_accessed=4 * total * width,
            transcendentals=rows * total * H,
        ),
        name="attention_query_gradient",
    )(query_pos[:, None], key_pos[None, :], query, d_out, stats, keys_values, keys_values)


def key_kernel(kpos_ref, qpos_ref, k_ref, v_ref, q_ref, do_ref, stat_ref, dk_ref, dv_ref):
    @pl.when(pl.program_id(1) == 0)
    def _():
        dk_ref[...] = jnp.zeros_like(dk_ref)
        dv_ref[...] = jnp.zeros_like(dv_ref)

    allowed = kpos_ref[...] <= qpos_ref[...]
    keys, values, query, d_out = k_ref[...], v_ref[...], q_ref[...], do_ref[...]
    key_parts, value_parts = [], []
    for head in range(2):
        lse = stat_ref[0, head : head + 1, :]
        delta = stat_ref[0, head + 2 : head + 3, :]
        scores = jnp.where(allowed, dot_nt(head_only(keys, head), query), masked_score)
        prob = jnp.exp(scores - lse)
        value_parts.append(dot_nn(prob.astype(jnp.bfloat16), d_out))
        d_prob = dot_nt(head_only(values, head), d_out)
        d_score = (prob * (d_prob - delta)).astype(jnp.bfloat16)
        key_parts.append(dot_nn(d_score, query))
    dk_ref[...] += head_pick(key_parts[0], key_parts[1])
    dv_ref[...] += head_pick(value_parts[0], value_parts[1])


def key_gradients(key_pos, query_pos, qkv, query_all, d_out_all, stats_all):
    rows = qkv.shape[0]
    total, width = query_all.shape
    chunk = chunk_of(total)
    pairs = width // PAIR
    grad_spec = pl.BlockSpec((rows, PAIR), lambda h, c: (0, h))
    return pl.pallas_call(
        key_kernel,
        grid=(pairs, total // chunk),
        in_specs=[
            pl.BlockSpec((rows, 1), lambda h, c: (0, 0)),
            pl.BlockSpec((1, chunk), lambda h, c: (0, c)),
            pl.BlockSpec((rows, PAIR), lambda h, c: (0, h)),
            pl.BlockSpec((rows, PAIR), lambda h, c: (0, h + pairs)),
            pl.BlockSpec((chunk, PAIR), lambda h, c: (c, h)),
            pl.BlockSpec((chunk, PAIR), lambda h, c: (c, h)),
            pl.BlockSpec((1, 4, chunk), lambda h, c: (h, 0, c)),
        ],
        out_specs=[grad_spec, grad_spec],
        out_shape=[jax.ShapeDtypeStruct((rows, width), jnp.float32)] * 2,
        compiler_params=pltpu.CompilerParams(vmem_limit_bytes=40 * 2**20),
        cost_estimate=pl.CostEstimate(
            flops=16 * rows * total * width,
            bytes_accessed=4 * total * width,
            transcendentals=rows * total * H,
        ),
        name="attention_key_gradients",
    )(key_pos[:, None], query_pos[None, :], qkv, qkv, query_all, d_out_all, stats_all)


def whole_weight(weight):
    share = weight.shape[0] // lax.axis_size("ctx")
    mine = lax.dynamic_slice_in_dim(weight, lax.axis_index("ctx") * share, share, 0)
    return lax.all_gather(mine, ("fsdp", "ctx"), axis=0, tiled=True)


def gather_kernel(chips, shards, count, *refs):
    shares, wholes = refs[:count], refs[count : 2 * count]
    own_sem, z_send, z_recv, c_send, c_recv, k_send, k_recv = refs[2 * count :]
    me, row = lax.axis_index("ctx"), lax.axis_index("fsdp")
    chip, core = me // 2, me % 2
    sibling = (chip * 2 + 1 - core, row)

    def above(step):
        return (me, lax.rem(row + step, shards))

    def across(step):
        return (lax.rem(chip + step, chips) * 2 + core, row)

    barrier = pltpu.get_barrier_semaphore()
    greeted = [above(d) for d in range(1, shards)] + [across(d) for d in range(1, chips)]
    greeted.append(sibling)
    for other in greeted:
        pl.semaphore_signal(barrier, inc=1, device_id=other, device_id_type=pl.DeviceIdType.MESH)
    pl.semaphore_wait(barrier, len(greeted))

    def send(src, dst, send_sem, recv_sem, target):
        copy = pltpu.make_async_remote_copy(
            src_ref=src,
            dst_ref=dst,
            send_sem=send_sem,
            recv_sem=recv_sem,
            device_id=target,
            device_id_type=pl.DeviceIdType.MESH,
        )
        copy.start()
        return copy

    def column(item, index):
        return wholes[item].at[:, index]

    own, along, between, inside = {}, {}, {}, {}
    for i in range(count):
        own[i] = pltpu.make_async_copy(shares[i], wholes[i].at[row, me], own_sem.at[i])
        own[i].start()
        for d in range(1, shards):
            along[i, d] = send(
                shares[i],
                wholes[i].at[row, me],
                z_send.at[i, d - 1],
                z_recv.at[i, d - 1],
                above(d),
            )
    for i in range(count):
        own[i].wait()
        for d in range(1, shards):
            along[i, d].wait_recv()
        for d in range(1, chips):
            mine = column(i, me)
            between[i, d] = send(mine, mine, c_send.at[i, d - 1], c_recv.at[i, d - 1], across(d))
        inside[i, 0] = send(
            column(i, me), column(i, me), k_send.at[i, 0], k_recv.at[i, 0], sibling
        )
    for i in range(count):
        for d in range(1, chips):
            between[i, d].wait_recv()
            came = column(i, lax.rem(chip - d + chips, chips) * 2 + core)
            inside[i, d] = send(came, came, k_send.at[i, d], k_recv.at[i, d], sibling)
    for copy in inside.values():
        copy.wait_recv()
    for copies in (along, between, inside):
        for copy in copies.values():
            copy.wait_send()


def whole_weights(weights):
    ctx_count, shards = lax.axis_size("ctx"), lax.axis_size("fsdp")
    chips = ctx_count // 2
    if ctx_count != 8:
        return [whole_weight(item) for item in weights]
    count = len(weights)
    mine = []
    for item in weights:
        share = item.shape[0] // ctx_count
        mine.append(
            lax.dynamic_slice_in_dim(item, lax.axis_index("ctx") * share, share, 0)
        )
    anywhere = pl.BlockSpec(memory_space=pl.ANY)
    dma = pltpu.SemaphoreType.DMA
    wholes = pl.pallas_call(
        partial(gather_kernel, chips, shards, count),
        in_specs=[anywhere] * count,
        out_specs=[anywhere] * count,
        out_shape=[
            jax.ShapeDtypeStruct((shards, ctx_count) + item.shape, item.dtype) for item in mine
        ],
        scratch_shapes=[
            dma((count,)),
            dma((count, shards - 1)),
            dma((count, shards - 1)),
            dma((count, chips - 1)),
            dma((count, chips - 1)),
            dma((count, chips)),
            dma((count, chips)),
        ],
        compiler_params=pltpu.CompilerParams(collective_id=0, has_side_effects=True),
        name="gather_weights",
    )(*mine)
    return [
        whole.reshape(item.shape[0] * shards, item.shape[1])
        for whole, item in zip(wholes, weights)
    ]


def scatter_kernel(chips, shards, spans, packed, out, own, k_land, c_land, z_land, *sems):
    local, k_send, k_recv, c_send, c_recv, z_send, z_recv = sems
    me, row = lax.axis_index("ctx"), lax.axis_index("fsdp")
    chip, core = me // 2, me % 2
    sibling = (chip * 2 + 1 - core, row)

    def above(step):
        return (me, lax.rem(row + step, shards))

    def across(step):
        return (lax.rem(chip + step, chips) * 2 + core, row)

    barrier = pltpu.get_barrier_semaphore()
    greeted = [above(d) for d in range(1, shards)] + [across(d) for d in range(1, chips)]
    greeted.append(sibling)
    for other in greeted:
        pl.semaphore_signal(barrier, inc=1, device_id=other, device_id_type=pl.DeviceIdType.MESH)
    pl.semaphore_wait(barrier, len(greeted))

    def send(src, dst, send_sem, recv_sem, target):
        copy = pltpu.make_async_remote_copy(
            src_ref=src,
            dst_ref=dst,
            send_sem=send_sem,
            recv_sem=recv_sem,
            device_id=target,
            device_id_type=pl.DeviceIdType.MESH,
        )
        copy.start()
        return copy

    order = list(range(1, chips)) + [0]
    kept, inside, between, along = {}, {}, {}, {}
    for i, span in enumerate(spans):
        rows = pl.ds(*span)
        for d in order:
            part = lax.rem(chip + d, chips)
            inside[i, d] = send(
                packed.at[part, 1 - core, :, rows],
                k_land.at[part, :, rows],
                k_send.at[i, d],
                k_recv.at[i, d],
                sibling,
            )
            kept[i, d] = pltpu.make_async_copy(
                packed.at[part, core, :, rows], own.at[part, :, rows], local.at[i, d]
            )
            kept[i, d].start()
    for i, span in enumerate(spans):
        rows = pl.ds(*span)
        for d in order:
            part = lax.rem(chip + d, chips)
            kept[i, d].wait()
            inside[i, d].wait_recv()

            @pl.loop(0, shards)
            def _(f):
                total = own[part, f, rows].astype(jnp.float32)
                total += k_land[part, f, rows].astype(jnp.float32)
                own[part, f, rows] = total.astype(jnp.bfloat16)

            if d:
                between[i, d] = send(
                    own.at[part, :, rows],
                    c_land.at[d - 1, :, rows],
                    c_send.at[i, d - 1],
                    c_recv.at[i, d - 1],
                    across(d),
                )
    for i, span in enumerate(spans):
        rows = pl.ds(*span)
        for d in range(1, chips):
            between[i, d].wait_recv()

        @pl.loop(0, shards)
        def _(f):
            total = own[chip, f, rows].astype(jnp.float32)
            for d in range(1, chips):
                total += c_land[d - 1, f, rows].astype(jnp.float32)
            own[chip, f, rows] = total.astype(jnp.bfloat16)

        for d in range(1, shards):
            along[i, d] = send(
                own.at[chip, lax.rem(row + d, shards), rows],
                z_land.at[d - 1, rows],
                z_send.at[i, d - 1],
                z_recv.at[i, d - 1],
                above(d),
            )
    for i, span in enumerate(spans):
        rows = pl.ds(*span)
        for d in range(1, shards):
            along[i, d].wait_recv()
        total = own[chip, row, rows].astype(jnp.float32)
        for d in range(1, shards):
            total += z_land[d - 1, rows].astype(jnp.float32)
        out[rows] = total
    for copies in (inside, between, along):
        for copy in copies.values():
            copy.wait_send()


def scatter_packed(packed):
    ctx_count, shards = lax.axis_size("ctx"), lax.axis_size("fsdp")
    _, rows, width = packed.shape
    if ctx_count != 8:
        return scatter(packed.reshape(-1, width)).astype(jnp.float32)
    chips = ctx_count // 2
    first = 16 * (-(-rows // 32))
    spans = ((0, first), (first, rows - first))
    dma = pltpu.SemaphoreType.DMA
    low = jnp.bfloat16
    return pl.pallas_call(
        partial(scatter_kernel, chips, shards, spans),
        in_specs=[pl.BlockSpec(memory_space=pl.ANY)],
        out_specs=pl.BlockSpec(memory_space=pltpu.VMEM),
        out_shape=jax.ShapeDtypeStruct((rows, width), jnp.float32),
        scratch_shapes=[
            pltpu.VMEM((chips, shards, rows, width), low),
            pltpu.VMEM((chips, shards, rows, width), low),
            pltpu.VMEM((chips - 1, shards, rows, width), low),
            pltpu.VMEM((shards - 1, rows, width), low),
            dma((2, chips)),
            dma((2, chips)),
            dma((2, chips)),
            dma((2, chips - 1)),
            dma((2, chips - 1)),
            dma((2, shards - 1)),
            dma((2, shards - 1)),
        ],
        compiler_params=pltpu.CompilerParams(
            collective_id=1, has_side_effects=True, vmem_limit_bytes=44 * 2**20
        ),
        name="sum_gradients",
    )(packed.reshape(chips, 2, shards, rows, width))


def all_positions(pair_table, ctx_count):
    column = jnp.arange(2 * BLK, dtype=jnp.int32)[None, :]
    pair = pair_table[:, None]
    lower = pair * BLK + column
    upper = (2 * ctx_count - 1 - pair) * BLK + column - BLK
    return jnp.where(column < BLK, lower, upper).reshape(-1)


def scatter(term):
    return lax.psum_scatter(term, ("ctx", "fsdp"), scatter_dimension=0, tiled=True)


class Spot:
    def __init__(self, shards):
        self.shards = shards
        self.me, self.row = lax.axis_index("ctx"), lax.axis_index("fsdp")
        chip, core = self.me // 2, self.me % 2
        y, x = chip // 2, chip % 2
        self.core = core
        self.a = (1 - core) * x + core * y
        self.b = (1 - core) * y + core * x
        self.first = self.index(1 - self.a, self.b)
        self.second = self.index(self.a, 1 - self.b)
        self.corner = self.index(1 - self.a, 1 - self.b)
        self.sibling = chip * 2 + 1 - core

    def chip_of(self, a, b):
        return (1 - self.core) * (2 * b + a) + self.core * (2 * a + b)

    def index(self, a, b):
        return self.chip_of(a, b) * 2 + self.core

    def near(self, ctx):
        return (ctx, self.row)

    def above(self, step):
        return (self.me, lax.rem(self.row + step, self.shards))

    def came(self, step):
        return lax.rem(self.row - step + self.shards, self.shards)

    def greet(self):
        barrier = pltpu.get_barrier_semaphore()
        others = [self.above(d) for d in range(1, self.shards)]
        others += [self.near(i) for i in (self.first, self.second, self.sibling)]
        for other in others:
            pl.semaphore_signal(
                barrier, inc=1, device_id=other, device_id_type=pl.DeviceIdType.MESH
            )
        pl.semaphore_wait(barrier, len(others))


def send(src, dst, send_sem, recv_sem, target):
    copy = pltpu.make_async_remote_copy(
        src_ref=src,
        dst_ref=dst,
        send_sem=send_sem,
        recv_sem=recv_sem,
        device_id=target,
        device_id_type=pl.DeviceIdType.MESH,
    )
    copy.start()
    return copy


class Gather:
    def __init__(self, spot, shard, whole, begin, columns, sems):
        self.spot, self.shard, self.whole, self.sems = spot, shard, whole, sems
        self.rows, self.begin, self.half = shard.shape[0], begin, columns // 2
        self.copies = {}

    def cols(self):
        return pl.ds(pl.multiple_of(self.begin + self.spot.core * self.half, 128), self.half)

    def part(self, row, start, size):
        begin = pl.multiple_of(row * self.rows + start, 16)
        return self.whole.at[pl.ds(begin, size), self.cols()]

    def post(self, stage, d, src, dst, target):
        at = stage * (self.spot.shards - 1) + d - 1
        self.copies[stage, d] = send(
            src, dst, self.sems[0].at[at], self.sems[1].at[at], target
        )

    def along(self):
        spot, quarter = self.spot, self.rows // 4
        start = (2 * spot.b + spot.a) * quarter
        src = self.shard.at[pl.ds(pl.multiple_of(start, 16), quarter), self.cols()]
        for d in range(1, spot.shards):
            self.post(0, d, src, self.part(spot.row, start, quarter), spot.above(d))

    def steps(self, d):
        return (d,) if d else range(1, self.spot.shards)

    def step_one(self, only=None):
        spot, quarter = self.spot, self.rows // 4
        start = (2 * spot.b + spot.a) * quarter
        for d in self.steps(only):
            self.copies[0, d].wait_recv()
            ref = self.part(spot.came(d), start, quarter)
            self.post(1, d, ref, ref, spot.near(spot.first))

    def step_two(self, only=None):
        spot, half = self.spot, self.rows // 2
        for d in self.steps(only):
            self.copies[1, d].wait_recv()
            ref = self.part(spot.came(d), spot.b * half, half)
            self.post(2, d, ref, ref, spot.near(spot.second))
            self.post(3, d, ref, ref, spot.near(spot.sibling))

    def step_three(self, d):
        spot, half = self.spot, self.rows // 2
        self.copies[2, d].wait_recv()
        ref = self.part(spot.came(d), (1 - spot.b) * half, half)
        self.post(4, d, ref, ref, spot.near(spot.sibling))

    def finish(self, d):
        self.copies[3, d].wait_recv()
        self.copies[4, d].wait_recv()

    def complete(self):
        for d in range(1, self.spot.shards):
            self.step_three(d)
        for d in range(1, self.spot.shards):
            self.finish(d)

    def drain(self):
        for copy in self.copies.values():
            copy.wait_send()


class Exchange:
    def __init__(self, spot, view, sems):
        self.spot, self.sems, self.view = spot, sems, view
        self.copies = {}

    def post(self, at, device, target):
        ref = self.view(device)
        self.copies[at] = send(
            ref, ref, self.sems[0].at[at], self.sems[1].at[at], self.spot.near(target)
        )

    def start(self):
        spot = self.spot
        self.post(0, spot.me, spot.first)
        self.post(1, spot.me, spot.second)
        self.post(2, spot.me, spot.sibling)

    def pass_on(self):
        spot = self.spot
        self.copies[0].wait_recv()
        self.post(3, spot.first, spot.second)
        self.post(4, spot.first, spot.sibling)

    def share(self):
        spot = self.spot
        self.copies[1].wait_recv()
        self.post(5, spot.second, spot.sibling)
        self.copies[3].wait_recv()
        self.post(6, spot.corner, spot.sibling)

    def finish(self):
        for at in (2, 4, 5, 6):
            self.copies[at].wait_recv()

    def drain(self):
        for copy in self.copies.values():
            copy.wait_send()


class Unit:
    def __init__(self, spot, packed, lands, sems, store):
        self.spot, self.packed, self.sems, self.store = spot, packed, sems, store
        self.core_land, self.first_land, self.second_land, self.z_land = lands
        self.copies = {}

    def post(self, at, src, dst, target):
        self.copies[at] = send(src, dst, self.sems[0].at[at], self.sems[1].at[at], target)

    def cores(self):
        spot = self.spot
        self.post(
            0, self.packed.at[:, 1 - spot.core], self.core_land, spot.near(spot.sibling)
        )

    def step_one(self):
        spot, land, packed = self.spot, self.core_land, self.packed
        self.copies[0].wait_recv()
        for k, b in enumerate((1 - spot.b, spot.b)):
            chip = spot.chip_of(1 - spot.a, b)
            land[chip] = land[chip] + packed[chip, spot.core]
            self.post(1 + k, land.at[chip], self.first_land.at[k], spot.near(spot.first))
        for b in (1 - spot.b, spot.b):
            chip = spot.chip_of(spot.a, b)
            land[chip] = land[chip] + packed[chip, spot.core]

    def step_two(self):
        spot, land = self.spot, self.first_land
        self.copies[1].wait_recv()
        land[0] = land[0] + self.core_land[spot.chip_of(spot.a, 1 - spot.b)]
        self.post(3, land.at[0], self.second_land, spot.near(spot.second))
        self.copies[2].wait_recv()
        land[1] = land[1] + self.core_land[spot.chip_of(spot.a, spot.b)]

    def along(self):
        spot, land = self.spot, self.second_land
        self.copies[3].wait_recv()
        land[...] = land[...] + self.first_land[1]
        for d in range(1, spot.shards):
            other = lax.rem(spot.row + d, spot.shards)
            self.post(3 + d, land.at[other], self.z_land.at[d - 1], spot.above(d))

    def finish(self):
        spot = self.spot
        total = self.second_land[spot.row].astype(jnp.float32)
        for d in range(1, spot.shards):
            self.copies[3 + d].wait_recv()
            total += self.z_land[d - 1].astype(jnp.float32)
        self.store(total)

    def drain(self):
        for at, copy in self.copies.items():
            if at:
                copy.wait_send()


class UnitAlongFirst(Unit):
    def step_one(self):
        spot, land, packed = self.spot, self.core_land, self.packed
        self.copies[0].wait_recv()
        for chip in range(land.shape[0]):
            land[chip] = land[chip] + packed[chip, spot.core]
        for d in range(1, spot.shards):
            other = lax.rem(spot.row + d, spot.shards)
            self.post(d, land.at[:, other], self.z_land.at[d - 1], spot.above(d))

    def step_two(self):
        spot, land, low = self.spot, self.z_land, self.z_land.dtype
        for d in range(1, spot.shards):
            self.copies[d].wait_recv()

        def add(chip):
            total = self.core_land[chip, spot.row].astype(jnp.float32)
            for d in range(1, spot.shards):
                total += land[d - 1, chip].astype(jnp.float32)
            land[0, chip] = total.astype(low)

        for k, b in enumerate((1 - spot.b, spot.b)):
            chip = spot.chip_of(1 - spot.a, b)
            add(chip)
            at = spot.shards + k
            self.post(at, land.at[0, chip], self.first_land.at[k], spot.near(spot.first))
        for b in (1 - spot.b, spot.b):
            add(spot.chip_of(spot.a, b))

    def along(self):
        spot, land, at = self.spot, self.first_land, self.spot.shards
        self.copies[at].wait_recv()
        land[0] = land[0] + self.z_land[0, spot.chip_of(spot.a, 1 - spot.b)]
        self.post(at + 2, land.at[0], self.second_land, spot.near(spot.second))

    def finish(self):
        spot, at = self.spot, self.spot.shards
        total = self.z_land[0, spot.chip_of(spot.a, spot.b)].astype(jnp.float32)
        self.copies[at + 1].wait_recv()
        total += self.first_land[1].astype(jnp.float32)
        self.copies[at + 2].wait_recv()
        self.store(total + self.second_land[...].astype(jnp.float32))


def dot_tn(left, right):
    return lax.dot_general(
        left, right, (((0,), (0,)), ((), ())), preferred_element_type=jnp.float32
    )


def gelu_pair(u):
    inner = 0.7978845608028654
    cubic = 0.044715
    square = u * u
    bend = jnp.tanh(inner * (u + cubic * (u * square)))
    half = 0.5 * (1.0 + bend)
    slope = half + 0.5 * u * (1.0 - bend * bend) * (inner * (1.0 + 3.0 * cubic * square))
    return u * half, slope


PROJ_COLS, TILE = 256, 256
DELAYS = (0, 1, 3, 5, 7)
DELAYS_ALONG = (0, 1, 7, 9, 10)
ALONG_FIRST = (0, 1)


def layer_kernel(shards, names, *refs):
    r = SimpleNamespace(**dict(zip(names, refs)))
    landings = refs[len(names) :]
    spot = Spot(shards)
    rows, width = r.x.shape
    low = jnp.bfloat16
    pairs = width // PAIR
    kv, qd, stat = r.kv, r.qd, r.stat
    count = kv.shape[0]
    total = count * rows
    own = []
    shards_here = (r.qkv_shard, r.out_shard, r.fc_shard, r.proj_shard)
    for i, (shard, whole) in enumerate(zip(shards_here, (r.qkv, r.out, r.fc, r.proj))):
        size = shard.shape[0]
        begin = pl.multiple_of(spot.row * size, 16)
        own.append(
            pltpu.make_async_copy(shard, whole.at[pl.ds(begin, size)], r.own_sem.at[i])
        )
        own[-1].start()
    every_in = r.every_in
    every_in[spot.me] = r.x[...]
    spot.greet()

    def gather(shard, whole, number, begin, columns):
        sems = r.gather_send.at[number], r.gather_recv.at[number]
        return Gather(spot, shard, whole, begin, columns, sems)

    hidden = r.fc.shape[1]
    w_k = gather(r.qkv_shard, r.qkv, 0, width, width)
    w_v = gather(r.qkv_shard, r.qkv, 1, 2 * width, width)
    w_q = gather(r.qkv_shard, r.qkv, 2, 0, width)
    w_out = gather(r.out_shard, r.out, 3, 0, width)
    w_fc = gather(r.fc_shard, r.fc, 4, 0, hidden)
    w_proj = gather(r.proj_shard, r.proj, 5, 0, width)
    gathers = (w_k, w_v, w_q, w_out, w_fc, w_proj)

    def exchange(number, view):
        return Exchange(spot, view, (r.ex_send.at[number], r.ex_recv.at[number]))

    def columns_of(ref, start):
        return lambda device: ref.at[device, :, pl.ds(start, width)]

    x_in = exchange(0, lambda device: r.every_in.at[device])
    x_d_out = exchange(1, columns_of(qd, width))
    x_stat = exchange(2, lambda device: stat.at[device])

    def vector(ref):
        return ref[...].reshape(1, -1)

    x_in.start()
    for item in gathers:
        item.along()
    table = r.table

    def spread(position, pair):
        lower = pair * BLK + position
        upper = (2 * count - 1 - pair) * BLK + position - BLK
        return jnp.where(position < BLK, lower, upper)

    r.qpos[...] = spread(
        lax.broadcasted_iota(jnp.int32, (rows, 1), 0), table[spot.me]
    )
    lane = lax.broadcasted_iota(jnp.int32, (1, total), 1)
    key_pos = jnp.zeros((1, total), jnp.int32)
    for device in range(count):
        local = lane - device * rows
        key_pos = jnp.where(
            (local >= 0) & (local < rows), spread(local, table[device]), key_pos
        )
    r.kpos[...] = key_pos
    x_in.pass_on()
    w_k.step_one()
    w_v.step_one()
    x_in.share()
    w_k.step_two()
    w_q.step_one()
    w_v.step_two()
    x_in.finish()
    x_in.drain()

    @pl.loop(0, count)
    def _(device):
        normed, _ = normalize(every_in[device].astype(jnp.float32))
        every_in[device] = (normed * vector(r.attn_gain) + vector(r.attn_shift)).astype(low)

    def project(start, finish):
        @pl.loop(0, count // 2)
        def _(i):
            two = pl.ds(2 * i, 2)
            block = dot_nn(
                every_in[two].reshape(2 * rows, width), r.qkv[:, pl.ds(start, width)]
            )
            finish(two, block)

    def put_keys(two, block):
        kv[two, :, pl.ds(0, width)] = block.astype(low).reshape(2, rows, width)

    def put_values(two, block):
        block = block + vector(r.value_bias)
        kv[two, :, pl.ds(width, width)] = block.astype(low).reshape(2, rows, width)

    def put_query(two, block):
        block = (block + vector(r.query_bias)).astype(low) * jnp.bfloat16(HEAD_DIM ** (-0.5))
        qd[two, :, pl.ds(0, width)] = block.reshape(2, rows, width)

    w_out.step_one()
    w_q.step_two()
    own[0].wait()
    w_k.complete()
    project(width, put_keys)
    w_fc.step_one()
    w_v.complete()
    w_out.step_two()
    project(2 * width, put_values)
    w_q.complete()
    w_fc.step_two()
    project(0, put_query)
    w_proj.step_one()

    stat_lane = lax.broadcasted_iota(jnp.int32, r.stat_mine.shape, 1)

    def put_stat(index, column):
        r.stat_mine[...] = jnp.where(stat_lane == index, column, r.stat_mine[...])

    def take_stat(index):
        return jnp.sum(
            jnp.where(stat_lane == index, r.stat_mine[...], 0.0), axis=-1, keepdims=True
        )

    r.stat_mine[...] = jnp.zeros_like(r.stat_mine)

    def lanes_of(h, start=0):
        return pl.ds(pl.multiple_of(start + h * PAIR, PAIR), PAIR)

    def attend(h):
        allowed = r.kpos[...] <= r.qpos[...]
        query = qd[spot.me, :, lanes_of(h)]
        keys = kv[:, :, lanes_of(h)].reshape(total, PAIR)
        values = kv[:, :, lanes_of(h, width)].reshape(total, PAIR)
        mixed = []
        for head in range(2):
            scores = jnp.where(allowed, dot_nt(head_only(query, head), keys), masked_score)
            most = jnp.max(scores, axis=-1, keepdims=True)
            expd = jnp.exp(scores - most)
            norm = jnp.sum(expd, axis=-1, keepdims=True)
            mixed.append(dot_nn(expd.astype(low), values) / norm)
            put_stat(4 * h + head, most + jnp.log(norm))
        r.attn[:, lanes_of(h)] = head_pick(mixed[0], mixed[1])

    pl.loop(0, 2)(attend)
    w_out.complete()
    w_proj.step_two()
    pl.loop(2, 4)(attend)
    for d in range(1, shards):
        w_fc.step_three(d)
    pl.loop(4, pairs)(attend)
    own[1].wait()
    attended = r.attn[...].astype(low)
    middle = r.x[...].astype(jnp.float32) + dot_nn(attended, r.out[...]) + vector(r.out_bias)
    r.middle[...] = middle
    normed, _ = normalize(middle)
    r.second[...] = (normed * vector(r.mlp_gain) + vector(r.mlp_shift)).astype(low)
    r.fc_line[...] = vector(r.fc_bias)
    own[2].wait()
    for d in range(1, shards):
        w_fc.finish(d)
    own[3].wait()
    piece = hidden // shards
    for d in range(shards):
        if d:
            w_proj.finish(d)
        n = spot.came(d)
        lanes = pl.ds(pl.multiple_of(n * piece, 128), piece)
        share = pl.ds(pl.multiple_of(n * piece, 16), piece)
        pre = dot_nn(r.second[...], r.fc[:, lanes]) + r.fc_line[:, lanes]
        activated, slope = gelu_pair(pre)
        activated = activated.astype(low)
        r.act[:, lanes] = activated
        result = dot_nn(activated, r.proj[share])
        d_act = dot_nt(r.cot[...], r.proj[share])
        d_pre = (d_act * slope).astype(low)
        r.d_pre[:, lanes] = d_pre
        d_second = dot_nt(d_pre, r.fc[:, lanes])
        if d:
            r.result[...] += result
            r.d_second[...] += d_second
        else:
            r.result[...] = result
            r.d_second[...] = d_second
            for k in range(1, shards):
                w_proj.step_three(k)

    units, makers = [], []
    used = ([], [])

    def make_proj(packed, n):
        right = r.cot[:, n * PROJ_COLS : (n + 1) * PROJ_COLS]

        @pl.loop(0, 4)
        def _(chip):
            share = hidden // 4
            left = r.act[:, pl.ds(pl.multiple_of(chip * share, 128), share)]
            packed[chip] = dot_tn(left, right).reshape(packed.shape[1:]).astype(low)

    def make_rows(packed, left_ref, right_ref, start):
        left = left_ref[...]

        @pl.loop(0, width // TILE)
        def _(n):
            right = right_ref[:, pl.ds(pl.multiple_of(start + n * TILE, 128), TILE)]
            block = dot_tn(left, right).reshape(packed.shape[:-1] + (TILE,))
            packed[..., pl.ds(pl.multiple_of(n * TILE, 128), TILE)] = block.astype(low)

    def add(kind, out_ref, start, columns, make):
        packs = (r.mid_pack, r.proj_pack)[kind]
        slots = packs.shape[0]
        packed = packs.at[len(used[kind]) % slots]
        number = len(units)

        def store(total):
            out_ref[:, start : start + columns] = total

        lands = landings[4 * number : 4 * number + 4]
        sems = r.unit_send.at[number], r.unit_recv.at[number]
        kind_of = UnitAlongFirst if number in ALONG_FIRST else Unit
        unit = kind_of(spot, packed, lands, sems, store)
        earlier = used[kind][-slots] if len(used[kind]) >= slots else None
        used[kind].append(unit)
        units.append(unit)

        def begin():
            if earlier is not None:
                earlier.copies[0].wait_send()
            make(packed)
            unit.cores()

        makers.append(begin)

    for n in range(hidden // width):
        add(0, r.g_fc, n * width, width, lambda p, n=n: make_rows(p, r.second, r.d_pre, n * width))
    for n in range(width // PROJ_COLS):
        add(1, r.g_proj, n * PROJ_COLS, PROJ_COLS, lambda p, n=n: make_proj(p, n))
    add(0, r.g_out, 0, width, lambda p: make_rows(p, r.attended, r.d_branch, 0))
    for n in range(3):
        add(0, r.g_qkv, n * width, width, lambda p, n=n: make_rows(p, every_in.at[spot.me], r.d_qkv, n * width))

    starts = [*range(9), 10, 11]

    def slot(number):
        if number in starts:
            makers[starts.index(number)]()
        for stage in range(1, 5):
            for i, unit in enumerate(units):
                delays = DELAYS_ALONG if i in ALONG_FIRST else DELAYS
                if number - starts[i] == delays[stage]:
                    (unit.step_one, unit.step_two, unit.along, unit.finish)[stage - 1]()

    slot(0)
    middle = r.middle[...]
    r.layer_out[...] = (middle + r.result[...] + vector(r.proj_bias)).astype(low)
    normed, inverse = normalize(middle)
    d_norm, grad_mlp_gain, grad_mlp_shift = norm_back(
        r.d_second[...], normed, inverse, vector(r.mlp_gain)
    )
    d_middle = r.cot[...].astype(jnp.float32) + d_norm
    r.d_middle[...] = d_middle
    d_branch = d_middle.astype(low)
    r.d_branch[...] = d_branch
    d_attended = dot_nt(d_branch, r.out[...]).astype(low)
    qd[spot.me, :, pl.ds(width, width)] = d_attended
    x_d_out.start()
    r.attended[...] = r.attn[...].astype(low)

    def deltas(h):
        d_out = qd[spot.me, :, lanes_of(h, width)].astype(jnp.float32)
        both = d_out * r.attn[:, lanes_of(h)]
        for head in range(2):
            put_stat(4 * h + 2 + head, jnp.sum(head_only(both, head), axis=-1, keepdims=True))

    pl.loop(0, pairs)(deltas)
    stat[spot.me] = jnp.transpose(r.stat_mine[...])[: stat.shape[1]]
    x_stat.start()
    slot(1)
    x_d_out.pass_on()
    x_stat.pass_on()

    def query_pair(h):
        allowed = r.kpos[...] <= r.qpos[...]
        query, d_out = qd[spot.me, :, lanes_of(h)], qd[spot.me, :, lanes_of(h, width)]
        keys = kv[:, :, lanes_of(h)].reshape(total, PAIR)
        values = kv[:, :, lanes_of(h, width)].reshape(total, PAIR)
        parts = []
        for head in range(2):
            lse, delta = take_stat(4 * h + head), take_stat(4 * h + 2 + head)
            scores = jnp.where(allowed, dot_nt(head_only(query, head), keys), masked_score)
            prob = jnp.exp(scores - lse)
            d_prob = dot_nt(head_only(d_out, head), values)
            parts.append(dot_nn((prob * (d_prob - delta)).astype(low), keys))
        d_query = head_pick(parts[0], parts[1]) * HEAD_DIM ** (-0.5)
        r.d_qkv[:, lanes_of(h)] = d_query.astype(low)

    def key_pair(h):
        keys, values = kv[spot.me, :, lanes_of(h)], kv[spot.me, :, lanes_of(h, width)]
        my_keys = [head_only(keys, head) for head in range(2)]
        my_values = [head_only(values, head) for head in range(2)]
        key_parts = [jnp.zeros((rows, PAIR), jnp.float32)] * 2
        value_parts = [jnp.zeros((rows, PAIR), jnp.float32)] * 2
        half = count // 2
        span = half * rows
        for chunk in range(2):
            part = pl.ds(chunk * half, half)
            allowed = r.qpos[...] <= r.kpos[:, chunk * span : (chunk + 1) * span]
            query = qd[part, :, lanes_of(h)].reshape(span, PAIR)
            d_out = qd[part, :, lanes_of(h, width)].reshape(span, PAIR)

            def line(index):
                parts = [stat[chunk * half + i, pl.ds(index, 1), :] for i in range(half)]
                return jnp.concatenate(parts, axis=-1)

            for head in range(2):
                lse, delta = line(4 * h + head), line(4 * h + 2 + head)
                scores = jnp.where(allowed, dot_nt(my_keys[head], query), masked_score)
                prob = jnp.exp(scores - lse)
                value_parts[head] = value_parts[head] + dot_nn(prob.astype(low), d_out)
                d_prob = dot_nt(my_values[head], d_out)
                d_score = (prob * (d_prob - delta)).astype(low)
                key_parts[head] = key_parts[head] + dot_nn(d_score, query)
        r.d_qkv[:, lanes_of(h, width)] = head_pick(*key_parts).astype(low)
        r.d_qkv[:, lanes_of(h, 2 * width)] = head_pick(*value_parts).astype(low)

    slot(2)
    slot(3)
    slot(4)
    x_d_out.share()
    x_stat.share()
    pl.loop(0, 2)(query_pair)
    slot(5)
    pl.loop(2, 4)(query_pair)
    slot(6)
    pl.loop(4, pairs)(query_pair)
    x_d_out.finish()
    x_stat.finish()
    slot(7)
    pl.loop(0, 2)(key_pair)
    slot(8)
    pl.loop(2, 4)(key_pair)
    slot(9)
    pl.loop(4, pairs)(key_pair)
    slot(10)
    slot(11)
    slot(12)
    d_qkv = r.d_qkv[...]
    d_first = dot_nt(d_qkv, r.qkv[...])
    normed, inverse = normalize(r.x[...].astype(jnp.float32))
    d_norm, grad_gain, grad_shift = norm_back(d_first, normed, inverse, vector(r.attn_gain))
    d_middle = r.d_middle[...]
    r.grad_in[...] = d_middle + d_norm

    def over_tokens(block):
        return jnp.sum(block.astype(jnp.float32), axis=0, keepdims=True)

    bias_fc = over_tokens(r.d_pre[...])
    lines = [
        over_tokens(d_qkv[:, :width]),
        over_tokens(d_qkv[:, 2 * width :]),
        over_tokens(d_middle),
        over_tokens(r.cot[...]),
        grad_gain.reshape(1, -1),
        grad_shift.reshape(1, -1),
        grad_mlp_gain.reshape(1, -1),
        grad_mlp_shift.reshape(1, -1),
    ]
    lines += [bias_fc[:, i * width : (i + 1) * width] for i in range(hidden // width)]
    vec_land, vec_part = r.vec_land, r.vec_part
    vec_part[0] = jnp.zeros(vec_part.shape[1:], jnp.float32)
    for i, item in enumerate(lines):
        vec_part[0, i : i + 1] = item
    vec_copies = []

    def vec_post(k, src, target):
        copy = send(src, vec_land.at[k], r.vec_send.at[k], r.vec_recv.at[k], target)
        vec_copies.append(copy)
        return copy

    for k, other in enumerate((spot.sibling, spot.first, spot.second)):
        copy = vec_post(k, vec_part.at[k], spot.near(other))
        slot(13 + k)
        copy.wait_recv()
        vec_part[k + 1] = vec_part[k] + vec_land[k]
    for d in range(1, shards):
        vec_post(2 + d, vec_part.at[3], spot.above(d))
    for number in range(16, 12 + DELAYS[-1]):
        slot(number)
    summed = vec_part[3]
    for d in range(1, shards):
        vec_copies[2 + d].wait_recv()
        summed = summed + vec_land[2 + d]
    r.sums[...] = summed
    for copy in vec_copies:
        copy.wait_send()
    for kind, packs in zip(used, (r.mid_pack, r.proj_pack)):
        for unit in kind[-packs.shape[0] :]:
            unit.copies[0].wait_send()
    for item in (*units, *gathers):
        item.drain()
    for item in (x_d_out, x_stat):
        item.drain()


def whole_layer(**inputs):
    shards, ctx_count = lax.axis_size("fsdp"), lax.axis_size("ctx")
    rows, width = inputs.get("x").shape
    hidden = inputs.get("fc_shard").shape[1]
    low, wide = jnp.bfloat16, jnp.float32
    dma = pltpu.SemaphoreType.DMA
    chips, devices = ctx_count // 2, ctx_count * shards
    mid = (width // devices, width)
    tall = (hidden // devices, PROJ_COLS)
    shapes = [mid] * (hidden // width) + [tall] * (width // PROJ_COLS) + [mid] * 4
    vmem = pltpu.VMEM
    scratch = dict(
        qkv=vmem((width, 3 * width), low),
        out=vmem((width, width), low),
        fc=vmem((width, hidden), low),
        proj=vmem((hidden, width), low),
        kv=vmem((ctx_count, rows, 2 * width), low),
        qd=vmem((ctx_count, rows, 2 * width), low),
        stat=vmem((ctx_count, 4 * width // PAIR, rows), wide),
        stat_mine=vmem((rows, 128), wide),
        qpos=vmem((rows, 1), jnp.int32),
        kpos=vmem((1, ctx_count * rows), jnp.int32),
        every_in=vmem((ctx_count, rows, width), low),
        attn=vmem((rows, width), wide),
        attended=vmem((rows, width), low),
        middle=vmem((rows, width), wide),
        second=vmem((rows, width), low),
        fc_line=vmem((1, hidden), wide),
        act=vmem((rows, hidden), low),
        d_pre=vmem((rows, hidden), low),
        result=vmem((rows, width), wide),
        d_second=vmem((rows, width), wide),
        d_middle=vmem((rows, width), wide),
        d_branch=vmem((rows, width), low),
        d_qkv=vmem((rows, 3 * width), low),
        vec_land=vmem((2 + shards, 16, width), wide),
        vec_part=vmem((4, 16, width), wide),
        mid_pack=vmem((3, chips, 2, shards) + mid, low),
        proj_pack=vmem((2, chips, 2, shards) + tall, low),
        own_sem=dma((4,)),
        gather_send=dma((6, 5 * (shards - 1))),
        gather_recv=dma((6, 5 * (shards - 1))),
        ex_send=dma((3, 7)),
        ex_recv=dma((3, 7)),
        unit_send=dma((len(shapes), 3 + shards)),
        unit_recv=dma((len(shapes), 3 + shards)),
        vec_send=dma((2 + shards,)),
        vec_recv=dma((2 + shards,)),
    )
    landings = []
    for i, shape in enumerate(shapes):
        if i in ALONG_FIRST:
            landings += [
                vmem((chips, shards) + shape, low),
                vmem((2,) + shape, low),
                vmem(shape, low),
                vmem((shards - 1, chips) + shape, low),
            ]
            continue
        landings += [
            vmem((chips, shards) + shape, low),
            vmem((2, shards) + shape, low),
            vmem((shards,) + shape, low),
            vmem((shards - 1,) + shape, low),
        ]
    outputs = dict(
        layer_out=jax.ShapeDtypeStruct((rows, width), low),
        grad_in=jax.ShapeDtypeStruct((rows, width), wide),
        g_qkv=jax.ShapeDtypeStruct((width // devices, 3 * width), wide),
        g_out=jax.ShapeDtypeStruct((width // devices, width), wide),
        g_fc=jax.ShapeDtypeStruct((width // devices, hidden), wide),
        g_proj=jax.ShapeDtypeStruct((hidden // devices, width), wide),
        sums=jax.ShapeDtypeStruct((16, width), wide),
    )
    inside = pl.BlockSpec(memory_space=pltpu.VMEM)
    anywhere = pl.BlockSpec(memory_space=pl.ANY)
    return pl.pallas_call(
        partial(layer_kernel, shards, (*inputs, *outputs, *scratch)),
        in_specs=[pl.BlockSpec(memory_space=pltpu.SMEM)]
        + [inside] * (len(inputs) - 5)
        + [anywhere] * 4,
        out_specs=[inside] * len(outputs),
        out_shape=list(outputs.values()),
        scratch_shapes=list(scratch.values()) + landings,
        compiler_params=pltpu.CompilerParams(
            collective_id=0, has_side_effects=True, vmem_limit_bytes=VMEM_LIMIT
        ),
        name="whole",
    )(*inputs.values())


VMEM_LIMIT = 62 * 2**20


def finish_kernel(*refs):
    ins, outs = refs[:7], refs[7:]
    for src, dst in zip(ins[:6], outs[:6]):
        dst[...] = src[...]
    sums, small = ins[6], outs[6:]
    shards = lax.axis_size("fsdp")
    devices = lax.axis_size("ctx") * shards
    device = lax.axis_index("ctx") * shards + lax.axis_index("fsdp")
    width = sums.shape[1]

    def piece(rows, start, size):
        return pltpu.roll(rows, lax.rem(width - start, width), 1)[:, :size]

    share = width // devices
    lines = piece(sums[0:8], device * share, share)
    for i in range(8):
        small[i][...] = lines[i : i + 1]
    share = small[8].shape[1]
    fit = width // share
    line = sums[pl.ds(8 + device // fit, 1), :]
    eight = jnp.broadcast_to(line, (8, width))
    small[8][...] = piece(eight, lax.rem(device, fit) * share, share)[0:1]


def device_slices(*parts, shape):
    devices = lax.axis_size("ctx") * lax.axis_size("fsdp")
    width = parts[6].shape[1]
    inside = pl.BlockSpec(memory_space=pltpu.VMEM)
    shares = [width // devices] * 8 + [parts[4].shape[1] // devices]
    outs = pl.pallas_call(
        finish_kernel,
        in_specs=[inside] * 7,
        out_specs=[inside] * 15,
        out_shape=[jax.ShapeDtypeStruct(p.shape, p.dtype) for p in parts[:6]]
        + [jax.ShapeDtypeStruct((1, share), jnp.float32) for share in shares],
        name="finish",
    )(*parts)
    layer_out, grad_in, g_qkv, g_out, g_fc, g_proj = outs[:6]
    small = [item.reshape(-1) for item in outs[6:]]
    return (
        layer_out.reshape(shape),
        grad_in.reshape(shape),
        g_qkv,
        small[0],
        small[1],
        g_out,
        small[2],
        g_fc,
        small[8],
        g_proj,
        *small[3:8],
    )


def per_device(
    layer_in,
    qkv_weight,
    query_bias,
    value_bias,
    out_weight,
    out_bias,
    fc_weight,
    fc_bias,
    proj_weight,
    proj_bias,
    attn_norm_gain,
    attn_norm_shift,
    mlp_norm_gain,
    mlp_norm_shift,
    cotangent,
    pair_table,
):
    ctx_count = lax.axis_size("ctx")
    shards = ctx_count * lax.axis_size("fsdp")
    _, _, rows, width = layer_in.shape
    if ctx_count == 8:
        outs = whole_layer(
            table=pair_table,
            x=layer_in.reshape(rows, width),
            cot=cotangent.reshape(rows, width),
            attn_gain=attn_norm_gain,
            attn_shift=attn_norm_shift,
            mlp_gain=mlp_norm_gain,
            mlp_shift=mlp_norm_shift,
            query_bias=query_bias,
            value_bias=value_bias,
            out_bias=out_bias,
            proj_bias=proj_bias,
            fc_bias=fc_bias,
            qkv_shard=qkv_weight,
            out_shard=out_weight,
            fc_shard=fc_weight,
            proj_shard=proj_weight,
        )
        return device_slices(*outs, shape=layer_in.shape)
    my_pos = block_positions(pair_table, lax.axis_index("ctx"), ctx_count)
    every_pos = all_positions(pair_table, ctx_count)
    flat_in = layer_in.reshape(rows, width).astype(jnp.float32)
    full_qkv, full_out, full_fc, full_proj = whole_weights(
        (qkv_weight, out_weight, fc_weight, proj_weight)
    )
    normed_one, inverse_one = normalize(flat_in)
    first_in = (normed_one * attn_norm_gain + attn_norm_shift).astype(jnp.bfloat16)
    keys_values = (
        jnp.dot(first_in, full_qkv[:, width:], preferred_element_type=jnp.float32)
        + jnp.concatenate([jnp.zeros_like(value_bias), value_bias])
    ).astype(jnp.bfloat16)
    every_kv = lax.all_gather(keys_values, "ctx", axis=0, tiled=True)
    query = (
        jnp.dot(first_in, full_qkv[:, :width], preferred_element_type=jnp.float32) + query_bias
    ).astype(jnp.bfloat16) * jnp.bfloat16(HEAD_DIM ** (-0.5))
    every_query = lax.all_gather(query, "ctx", axis=0, tiled=True)
    attn_exact, lse = forward_attention(my_pos, every_pos, query, every_kv)
    attended = attn_exact.astype(jnp.bfloat16)
    middle = flat_in + jnp.dot(attended, full_out, preferred_element_type=jnp.float32) + out_bias
    normed_two, inverse_two = normalize(middle)
    second_in = (normed_two * mlp_norm_gain + mlp_norm_shift).astype(jnp.bfloat16)
    pre_act = jnp.dot(second_in, full_fc, preferred_element_type=jnp.float32) + fc_bias
    activated, gelu_back = jax.vjp(partial(jax.nn.gelu, approximate=True), pre_act)
    act_low = activated.astype(jnp.bfloat16)
    result = middle + jnp.dot(act_low, full_proj, preferred_element_type=jnp.float32) + proj_bias
    layer_out = result.astype(jnp.bfloat16).reshape(layer_in.shape)
    d_result = cotangent.reshape(rows, width)
    d_act = jnp.einsum("td,fd->tf", d_result, full_proj, preferred_element_type=jnp.float32)
    (d_pre,) = gelu_back(d_act)
    d_pre_low = d_pre.astype(jnp.bfloat16)
    d_second = jnp.einsum("tf,df->td", d_pre_low, full_fc, preferred_element_type=jnp.float32)
    d_mid_norm, grad_mlp_gain, grad_mlp_shift = norm_back(
        d_second, normed_two, inverse_two, mlp_norm_gain
    )
    d_middle = d_result.astype(jnp.float32) + d_mid_norm
    d_branch = d_middle.astype(jnp.bfloat16)
    d_attended = jnp.einsum(
        "te,de->td", d_branch, full_out, preferred_element_type=jnp.float32
    ).astype(jnp.bfloat16)
    delta = jnp.sum(
        (d_attended.astype(jnp.float32) * attn_exact).reshape(rows, width // PAIR, 2, HEAD_DIM),
        axis=-1,
    )
    stats = jnp.concatenate([lse, jnp.transpose(delta, (1, 0, 2))], axis=-1)
    every_d_out = lax.all_gather(d_attended, "ctx", axis=0, tiled=True)
    every_stat = lax.all_gather(
        jnp.transpose(stats, (0, 2, 1)).reshape(-1, rows), "ctx", axis=1, tiled=True
    ).reshape(width // PAIR, 4, ctx_count * rows)
    grad_proj = jnp.einsum("tf,td->fd", act_low, d_result, preferred_element_type=jnp.float32)
    grad_fc = jnp.einsum("td,tf->df", second_in, d_pre_low, preferred_element_type=jnp.float32)
    grad_out = jnp.einsum("td,te->de", attended, d_branch, preferred_element_type=jnp.float32)
    d_query = query_gradient(my_pos, every_pos, query, d_attended, stats, every_kv)
    d_key, d_value = key_gradients(
        my_pos, every_pos, keys_values, every_query, every_d_out, every_stat
    )
    d_qkv = jnp.concatenate([d_query, d_key, d_value], axis=1).astype(jnp.bfloat16)
    grad_qkv = jnp.einsum("td,te->de", first_in, d_qkv, preferred_element_type=jnp.float32)
    d_first = jnp.einsum("te,de->td", d_qkv, full_qkv, preferred_element_type=jnp.float32)
    d_in_norm, grad_attn_gain, grad_attn_shift = norm_back(
        d_first, normed_one, inverse_one, attn_norm_gain
    )
    grad_in = (d_middle + d_in_norm).reshape(layer_in.shape)
    bias_sum = jnp.sum(d_qkv.astype(jnp.float32), axis=0)
    vectors = (
        bias_sum[:width],
        bias_sum[2 * width :],
        jnp.sum(d_middle, axis=0),
        jnp.sum(d_pre_low.astype(jnp.float32), axis=0),
        jnp.sum(d_result.astype(jnp.float32), axis=0),
        grad_attn_gain,
        grad_attn_shift,
        grad_mlp_gain,
        grad_mlp_shift,
    )
    small = jnp.concatenate([item.reshape(shards, -1) for item in vectors], axis=1)
    lines = 16 * -(-small.shape[1] // (16 * width))
    small = jnp.pad(small, ((0, 0), (0, lines * width - small.shape[1])))
    matrices = (
        [grad_qkv[:, i * width : (i + 1) * width] for i in range(3)]
        + [grad_out]
        + [grad_fc[:, i * width : (i + 1) * width] for i in range(grad_fc.shape[1] // width)]
        + [grad_proj, small.reshape(shards * lines, width)]
    )
    packed = jnp.concatenate(
        [item.astype(jnp.bfloat16).reshape(shards, -1, width) for item in matrices], axis=1
    )
    summed = scatter_packed(packed)
    pieces, start = [], 0
    for item in matrices:
        size = item.shape[0] // shards
        pieces.append(summed[start : start + size])
        start += size
    sum_qkv = jnp.concatenate(pieces[:3], axis=1)
    sum_out = pieces[3]
    sum_fc = jnp.concatenate(pieces[4:-2], axis=1)
    sum_proj = pieces[-2]
    sum_small = pieces[-1].reshape(-1)
    small, start = [], 0
    for item in vectors:
        size = item.shape[0] // shards
        small.append(sum_small[start : start + size])
        start += size
    return (
        layer_out,
        grad_in,
        sum_qkv,
        small[0],
        small[1],
        sum_out,
        small[2],
        sum_fc,
        small[3],
        sum_proj,
        small[4],
        small[5],
        small[6],
        small[7],
        small[8],
    )


def solution(mesh):
    return jax.shard_map(
        per_device,
        mesh=mesh,
        in_specs=(
            P("fsdp", "ctx", None, None),
            P("fsdp", None),
            P(),
            P(),
            P("fsdp", None),
            P(),
            P("fsdp", None),
            P(),
            P("fsdp", None),
            P(),
            P(),
            P(),
            P(),
            P(),
            P("fsdp", "ctx", None, None),
            P(),
        ),
        out_specs=(
            P("fsdp", "ctx", None, None),
            P("fsdp", "ctx", None, None),
            P(("ctx", "fsdp"), None),
            P(("ctx", "fsdp")),
            P(("ctx", "fsdp")),
            P(("ctx", "fsdp"), None),
            P(("ctx", "fsdp")),
            P(("ctx", "fsdp"), None),
            P(("ctx", "fsdp")),
            P(("ctx", "fsdp"), None),
            P(("ctx", "fsdp")),
            P(("ctx", "fsdp")),
            P(("ctx", "fsdp")),
            P(("ctx", "fsdp")),
            P(("ctx", "fsdp")),
        ),
        check_vma=False,
    )
```
